32 devices in a mesh: ctx: 4 (over x, core), ch: 8 (over z, y).
Axes of the slice: x: 2, y: 2, z: 4, core: 2. Of those that a mesh axis runs over, the one named last changes fastest.
Arguments:
- value_in: bfloat16 [8192, 2048], P('ch', 'ctx'), may hold values from -6 to 6
- key_in: bfloat16 [8192, 2048], P('ch', 'ctx'), may hold values from -6 to 6
- gate_first: bfloat16 [8192, 2048], P('ch', 'ctx'), may hold values from -6 to 6
- gate_second: bfloat16 [8192, 2048], P('ch', 'ctx'), may hold values from -6 to 6
- gate_long: bfloat16 [8192, 2048], P('ch', 'ctx'), may hold values from -6 to 6
- filter_first: bfloat16 [512, 128], P('ch'), may hold values from -0.5 to 0.5
- filter_second: bfloat16 [512, 128], P('ch'), may hold values from -0.5 to 0.5
- long_filter: bfloat16 [8192, 2048], P(('ch', 'ctx')), may hold values from -0.125 to 0.125
- skip_gain: float32 [8192], P('ch'), may hold values from 0.5 to 1.5
Outputs:
- mixed_out: bfloat16 [8192, 2048], P('ch', 'ctx')
The draws below stay inside these ranges and needn't reach their ends.
All inputs are finite; a program needn't handle non-finite values.
Results may differ from the reference program's by a relative error of at most 0.0085.
Values may be sent and summed in bfloat16 or wider, within the bound.
A program may use at most 64 MiB of HBM per device.

```python
import math
import jax
import jax.numpy as jnp
from jax import lax

D = 8192
CG = 16
TAPS = 128
SEQ = 2048
GROUPS = 512


def level_of(stream_key, extent, shards, least, top_value):
    def one(axis_at, parts):
        heights = jax.random.uniform(jax.random.fold_in(jax.random.fold_in(stream_key, 6), axis_at), (parts,), jnp.float32, least / len(shards), top_value / len(shards))
        return jnp.repeat(jnp.exp(heights), extent[axis_at] // parts).reshape((-1,) + (1,) * (len(extent) - axis_at - 1))

    factor_of = one(*shards[0])
    for cut in shards[1:]:
        factor_of = factor_of * one(*cut)
    return factor_of


def centred(stream_key, extent, width, bound, cuts=(), dtype=jnp.bfloat16):
    gain = level_of(stream_key, extent, cuts, -0.22, 0.18) if cuts else 1.0
    values = jax.random.normal(stream_key, extent, jnp.float32) * width * gain
    return jnp.minimum(jnp.maximum(values, -bound), bound).astype(dtype)


def setup_inputs(seed: int = 0) -> dict:
    arg_keys = jax.random.split(jax.random.key(seed), 10)
    return {
        "value_in": centred(arg_keys[0], (D, SEQ), 1.0, 6.0, ((0, 8), (1, 4))),
        "key_in": centred(arg_keys[1], (D, SEQ), 1.0, 6.0, ((0, 8), (1, 4))),
        "gate_first": centred(arg_keys[2], (D, SEQ), 1.0, 6.0, ((0, 8), (1, 4))),
        "gate_second": centred(arg_keys[3], (D, SEQ), 1.0, 6.0, ((0, 8), (1, 4))),
        "gate_long": centred(arg_keys[4], (D, SEQ), 1.0, 6.0, ((0, 8), (1, 4))),
        "filter_first": centred(arg_keys[5], (GROUPS, TAPS), TAPS ** -0.5, 0.5, ((0, 8),)),
        "filter_second": centred(arg_keys[6], (GROUPS, TAPS), TAPS ** -0.5, 0.5, ((0, 8),)),
        "long_filter": centred(arg_keys[7], (D, SEQ), SEQ ** -0.5, 0.125, ((0, 32),)),
        "skip_gain": jnp.clip(0.5 + 1.0 * jax.random.uniform(arg_keys[8], (D,), jnp.float32) ** level_of(arg_keys[8], (D,), ((0, 8),), -0.2, 0.2), 0.5, 1.5),
    }


def causal_conv(signal, filters):
    per_channel = jnp.repeat(filters.astype(jnp.float32), CG, axis=0)
    length = signal.shape[1]
    padded = jnp.pad(signal.astype(jnp.float32), ((0, 0), (TAPS, 0)))

    def add_tap(tap, total):
        weight = lax.dynamic_slice_in_dim(per_channel, tap, 1, 1)
        shifted = lax.dynamic_slice_in_dim(padded, TAPS - tap, length, 1)
        return total + weight * shifted

    return lax.fori_loop(0, TAPS, add_tap, jnp.zeros(signal.shape, jnp.float32))


def long_conv(block_args):
    signal, filt_vals, skip_part = block_args
    length = signal.shape[1]
    spectrum = jnp.fft.rfft(signal, n=2 * length, axis=1) * jnp.fft.rfft(filt_vals, n=2 * length, axis=1)
    convolved = jnp.fft.irfft(spectrum, n=2 * length, axis=1)[:, :length]
    return skip_part[:, None] * signal + convolved


def reference(value_in, key_in, gate_first, gate_second, gate_long, filter_first, filter_second, long_filter, skip_gain):
    mixed_in = (key_in.astype(jnp.float32) * value_in.astype(jnp.float32)).astype(jnp.bfloat16)
    mixed_in = lax.optimization_barrier(mixed_in)
    first_out = (gate_first.astype(jnp.float32) * causal_conv(mixed_in, filter_first)).astype(jnp.bfloat16)
    first_out = lax.optimization_barrier(first_out)
    second_out = (gate_second.astype(jnp.float32) * causal_conv(first_out, filter_second)).astype(jnp.bfloat16)
    second_out = lax.optimization_barrier(second_out)
    block_size = math.gcd(D, 256)
    block_count = D // block_size
    long_out = lax.map(long_conv, (second_out.astype(jnp.float32).reshape(block_count, block_size, SEQ),
                                   long_filter.astype(jnp.float32).reshape(block_count, block_size, SEQ),
                                   skip_gain.reshape(block_count, block_size)))
    long_out = long_out.reshape(D, SEQ).astype(jnp.bfloat16)
    long_out = lax.optimization_barrier(long_out)
    return (gate_long.astype(jnp.float32) * long_out.astype(jnp.float32)).astype(jnp.bfloat16)
```

```python
import cmath
import functools
import math

import jax
import jax.numpy as jnp
import ml_dtypes
import numpy as np
from jax import lax
from jax.experimental import pallas as pl
from jax.experimental.pallas import tpu as pltpu
from jax.sharding import PartitionSpec as P

HIGH = lax.Precision.HIGH
LANES = 128
ROWS = 16
MESH = pl.DeviceIdType.MESH


def from_behind(shard, axis, by):
    devices = lax.axis_size(axis)
    pairs = [(i, i + by) for i in range(devices) if 0 <= i + by < devices]
    return lax.ppermute(shard, axis, pairs)


def band_matrix(filters, tap_count):
    group_count = filters.shape[0]
    zero_one = jnp.zeros((group_count, 1), filters.dtype)
    zero_rest = jnp.zeros((group_count, tap_count), filters.dtype)
    pattern = jnp.concatenate([zero_one, jnp.flip(filters, axis=1), zero_rest], axis=1)
    tiled = jnp.tile(pattern, (1, tap_count))
    return tiled[:, : tap_count * 2 * tap_count].reshape(group_count, tap_count, 2 * tap_count)


def toeplitz_conv(extended, filters, tap_count):
    channels, total_len = extended.shape
    length = total_len - tap_count
    block_count = length // tap_count
    front_half = extended[:, :length].reshape(channels, block_count, tap_count)
    back_half = extended[:, tap_count:].reshape(channels, block_count, tap_count)
    windows = jnp.concatenate([front_half, back_half], axis=2)
    group_count = filters.shape[0]
    windows = windows.reshape(group_count, channels // group_count, block_count, 2 * tap_count)
    toeplitz = band_matrix(filters, tap_count)
    result = jnp.einsum("gts,gcbs->gcbt", toeplitz, windows, preferred_element_type=jnp.float32)
    return result.reshape(channels, length)


def previous_rim(tail):
    return from_behind(tail, "ctx", 1)


def to_channels(data):
    return lax.all_to_all(data, "ctx", split_axis=0, concat_axis=1, tiled=True)


def first_section(mixed_in, gate_first, filter_first, tap_count):
    length = mixed_in.shape[1]
    extended = jnp.concatenate([previous_rim(mixed_in[:, length - tap_count :]), mixed_in], axis=1)
    return (
        gate_first.astype(jnp.float32) * toeplitz_conv(extended, filter_first, tap_count)
    ).astype(jnp.bfloat16)


def dft_tables(size):
    index = jnp.arange(size, dtype=jnp.int32)
    angle = (index[:, None] * index[None, :] % size).astype(jnp.float32) * (-2.0 * math.pi / size)
    return (jnp.cos(angle), jnp.sin(angle))


def split_factor(padded_len):
    outer = 2
    cand = 2
    while cand * cand <= padded_len:
        if padded_len % cand == 0:
            outer = cand
        cand = cand + 2
    return outer


def long_convolution(signal, filt_vals, skip_part):
    channels, length = signal.shape
    padded_len = 2 * length
    rows_outer = split_factor(padded_len)
    rows_inner = padded_len // rows_outer
    half_rows = rows_outer // 2
    outer_cos, outer_sin = dft_tables(rows_outer)
    inner_cos, inner_sin = dft_tables(rows_inner)
    k_index = jnp.arange(rows_outer, dtype=jnp.int32)[:, None]
    n_index = jnp.arange(rows_inner, dtype=jnp.int32)[None, :]
    twid_angle = (k_index * n_index % padded_len).astype(jnp.float32) * (
        -2.0 * math.pi / padded_len
    )
    twid_cos = jnp.cos(twid_angle)
    twid_sin = jnp.sin(twid_angle)
    outer_table = jnp.concatenate([outer_cos[:, :half_rows], outer_sin[:, :half_rows]], axis=0)
    inner_fwd = jnp.concatenate(
        [
            jnp.concatenate([inner_cos, inner_sin], axis=1),
            jnp.concatenate([-inner_sin, inner_cos], axis=1),
        ],
        axis=0,
    )
    inner_back = jnp.concatenate(
        [
            jnp.concatenate([inner_cos, -inner_sin], axis=1),
            jnp.concatenate([inner_sin, inner_cos], axis=1),
        ],
        axis=0,
    )

    def forward(values):
        grid = values.reshape(channels, half_rows, rows_inner)
        parts = jnp.einsum("kn,cnm->ckm", outer_table, grid, precision=HIGH)
        part_re = parts[:, :rows_outer]
        part_im = parts[:, rows_outer:]
        turned_re = part_re * twid_cos - part_im * twid_sin
        turned_im = part_re * twid_sin + part_im * twid_cos
        turned = jnp.concatenate([turned_re, turned_im], axis=2)
        spectrum = jnp.einsum("ckn,nm->ckm", turned, inner_fwd, precision=HIGH)
        return (spectrum[:, :, :rows_inner], spectrum[:, :, rows_inner:])

    sig_re, sig_im = forward(signal)
    filt_re, filt_im = forward(filt_vals)
    prod_re = sig_re * filt_re - sig_im * filt_im
    prod_im = sig_re * filt_im + sig_im * filt_re
    stacked = jnp.concatenate([prod_re, prod_im], axis=2)
    back = jnp.einsum("ckm,mn->ckn", stacked, inner_back, precision=HIGH)
    back_re = back[:, :, :rows_inner]
    back_im = back[:, :, rows_inner:]
    reverted_re = back_re * twid_cos + back_im * twid_sin
    reverted_im = back_im * twid_cos - back_re * twid_sin
    reverted = jnp.concatenate([reverted_re, reverted_im], axis=1)
    result = jnp.einsum("kn,ckm->cnm", outer_table, reverted, precision=HIGH)
    result = result.reshape(channels, length) / padded_len
    return skip_part[:, None] * signal + result


def shards_general(
    value_in,
    key_in,
    gate_first,
    gate_second,
    gate_long,
    filter_first,
    filter_second,
    long_filter,
    skip_gain,
):
    tap_count = filter_first.shape[1]
    channels, length = value_in.shape
    per_device = channels // lax.axis_size("ctx")
    channel_base = lax.axis_index("ctx") * per_device
    mixed_in = (key_in.astype(jnp.float32) * value_in.astype(jnp.float32)).astype(jnp.bfloat16)
    first_out = first_section(mixed_in, gate_first, filter_first, tap_count)
    prior_first = from_behind(first_out[:, length - tap_count :], "ctx", 1)
    first_wide = jnp.concatenate([prior_first, first_out], axis=1)
    second_out = (
        gate_second.astype(jnp.float32) * toeplitz_conv(first_wide, filter_second, tap_count)
    ).astype(jnp.bfloat16)
    moved = to_channels(second_out)
    skip_here = lax.dynamic_slice_in_dim(skip_gain, channel_base, per_device, 0)
    filt_vals = long_filter.astype(jnp.float32)
    long_out = long_convolution(moved.astype(jnp.float32), filt_vals, skip_here).astype(
        jnp.bfloat16
    )
    back_home = lax.all_to_all(long_out, "ctx", split_axis=1, concat_axis=0, tiled=True)
    return (gate_long.astype(jnp.float32) * back_home.astype(jnp.float32)).astype(jnp.bfloat16)


def unit(numerator, denominator):
    return cmath.exp(-2j * math.pi * numerator / denominator)


def turn(value, factor):
    re, im = value
    if abs(factor - 1) < 1e-12:
        return value
    if abs(factor + 1j) < 1e-12:
        return (im, -re)
    if abs(factor - 1j) < 1e-12:
        return (-im, re)
    if abs(abs(factor.real) - abs(factor.imag)) < 1e-12:
        size = abs(factor.real)
        re, im = re * size, im * size
        if factor.real > 0 and factor.imag < 0:
            return (re + im, im - re)
        if factor.real < 0 and factor.imag < 0:
            return (im - re, -re - im)
        if factor.real > 0:
            return (re - im, re + im)
        return (-re - im, re - im)
    return (re * factor.real - im * factor.imag, re * factor.imag + im * factor.real)


def complex_dft(values, sign):
    count = len(values)
    if count == 1:
        return values
    half = count // 2
    low, high = [], []
    for a in range(half):
        (p_re, p_im), (q_re, q_im) = values[a], values[a + half]
        low.append((p_re + q_re, p_im + q_im))
        factor = unit(a, count)
        high.append(turn((p_re - q_re, p_im - q_im), factor if sign > 0 else factor.conjugate()))
    result = [None] * count
    result[0::2] = complex_dft(low, sign)
    result[1::2] = complex_dft(high, sign)
    return result


def odd_bins(values):
    count = len(values)
    if count == 1:
        return {1: (values[0], None)}
    half = count // 2
    folded = [turn((values[a], -values[a + half]), unit(a, 2 * count)) for a in range(half)]
    bins = {}
    for place, (re, im) in enumerate(complex_dft(folded, 1)):
        r = 4 * place + 1
        if r < count:
            bins[r] = (re, im)
        else:
            bins[2 * count - r] = (re, -im)
    return bins


def real_bins(values):
    count = len(values)
    if count == 1:
        return {0: (values[0], None)}
    half = count // 2
    even = real_bins([values[a] + values[a + half] for a in range(half)])
    odd = odd_bins([values[a] - values[a + half] for a in range(half)])
    bins = {2 * r: v for r, v in even.items()}
    bins.update(odd)
    return bins


def padded_bins(values):
    bins = {2 * r: v for r, v in real_bins(values).items()}
    bins.update(odd_bins(values))
    return bins


def odd_back(bins, count):
    if count == 1:
        return [bins[1][0]]
    half = count // 2
    folded = []
    for place in range(half):
        r = 4 * place + 1
        if r < count:
            folded.append(bins[r])
        else:
            re, im = bins[2 * count - r]
            folded.append((re, -im))
    spread = complex_dft(folded, -1)
    spread = [turn(spread[a], unit(a, 2 * count).conjugate()) for a in range(half)]
    return [v[0] for v in spread] + [-v[1] for v in spread]


def real_back(bins, count):
    if count == 1:
        return [bins[0][0]]
    half = count // 2
    even = real_back({r // 2: v for r, v in bins.items() if r % 2 == 0}, half)
    odd = odd_back({r: v for r, v in bins.items() if r % 2 == 1}, half)
    return [even[a] + odd[a] for a in range(half)] + [even[a] - odd[a] for a in range(half)]


def padded_back(bins, count):
    even = real_back({r // 2: v for r, v in bins.items() if r % 2 == 0}, count)
    odd = odd_back({r: v for r, v in bins.items() if r % 2 == 1}, count)
    return [even[a] + odd[a] for a in range(count)]


def inner_tables(length):
    padded_len = 2 * length
    outer = padded_len // LANES
    b = np.arange(LANES)[:, None]
    q = np.arange(LANES)[None, :]
    forward, back = [], []
    for r in range(outer // 2 + 1):
        angle = (b * (r + outer * q) % padded_len) * (-2.0 * math.pi / padded_len)
        c, s = np.cos(angle), np.sin(angle)
        table = np.block([[c, s], [-s, c]])
        weight = (1.0 if r in (0, outer // 2) else 2.0) / padded_len
        forward.append(table)
        back.append(table.T * weight)
    return (
        np.stack(forward).astype(ml_dtypes.bfloat16),
        np.stack(back).astype(ml_dtypes.bfloat16),
    )


def band(row):
    rolled = pltpu.roll(jnp.broadcast_to(row, (LANES, LANES)), 0, 1, stride=1, stride_axis=0)
    s = lax.broadcasted_iota(jnp.int32, (LANES, LANES), 0)
    t = lax.broadcasted_iota(jnp.int32, (LANES, LANES), 1)
    zero = jnp.zeros((LANES, LANES), jnp.float32)
    return jnp.concatenate(
        [jnp.where(t < s, rolled, zero), jnp.where(t >= s, rolled, zero)], axis=0
    ).astype(jnp.bfloat16)


def gated(gate, value):
    return (gate.astype(jnp.float32) * value).astype(jnp.bfloat16)


def whole_kernel(
    n,
    chunk,
    value_ref,
    key_ref,
    gate_first_ref,
    filter_first_ref,
    filter_second_ref,
    skip_ref,
    gate_second_hbm,
    gate_long_hbm,
    long_filter_hbm,
    forward_hbm,
    back_hbm,
    out_ref,
    gate_second,
    gate_long,
    long_filter,
    forward,
    backward,
    taps_first,
    taps_second,
    band_first,
    band_second,
    mixed,
    first,
    halo_mixed,
    halo_first,
    second,
    gathered,
    long_out,
    returned,
    skip_wide,
    bins_in,
    spectrum,
    bins_out,
    load_sem,
    rim_send,
    rim_recv,
    there_send,
    there_recv,
    home_send,
    home_recv,
):
    _, per, length = value_ref.shape
    me = lax.axis_index("ctx")
    blocks = length // LANES
    chunks = per // chunk
    groups = chunk // ROWS
    total_blocks = n * blocks
    bin_count = total_blocks + 1
    last = slice(length - LANES, length)

    barrier = pltpu.get_barrier_semaphore()
    for k in range(1, n):
        pl.semaphore_signal(
            barrier, inc=1, device_id={"ctx": lax.rem(me + k, n)}, device_id_type=MESH
        )

    loads = [
        pltpu.make_async_copy(src, dst, load_sem.at[i])
        for i, (src, dst) in enumerate(
            [
                (gate_second_hbm, gate_second),
                (long_filter_hbm, long_filter),
                (forward_hbm, forward),
                (back_hbm, backward),
                (gate_long_hbm, gate_long),
            ]
        )
    ]
    for load in loads:
        load.start()

    def part(q):
        return pl.ds(pl.multiple_of(q * chunk, chunk), chunk)

    def rim(which, q):
        src, dst = ((mixed, halo_mixed), (first, halo_first))[which]
        return pltpu.make_async_remote_copy(
            src_ref=src.at[:, part(q), last],
            dst_ref=dst.at[:, part(q), :],
            send_sem=rim_send.at[which, q],
            recv_sem=rim_recv.at[which, q],
            device_id={"ctx": lax.rem(me + 1, n)},
            device_id_type=MESH,
        )

    def there(k, q, arriving=False):
        peer = lax.rem(me + (n - k if arriving else k), n)
        slot = peer if arriving else me
        return pltpu.make_async_remote_copy(
            src_ref=second.at[peer, part(q), :],
            dst_ref=gathered.at[slot, part(q), :],
            send_sem=there_send.at[k, q],
            recv_sem=there_recv.at[k, q],
            device_id={"ctx": peer},
            device_id_type=MESH,
        )

    def home(k, q, arriving=False):
        peer = lax.rem(me + (n - k if arriving else k), n)
        slot = peer if arriving else me
        return pltpu.make_async_remote_copy(
            src_ref=long_out.at[peer, part(q), :],
            dst_ref=returned.at[slot, part(q), :],
            send_sem=home_send.at[k, q],
            recv_sem=home_recv.at[k, q],
            device_id={"ctx": peer},
            device_id_type=MESH,
        )

    def rows_at(q, j):
        return pl.ds(pl.multiple_of(q * chunk + j * ROWS, ROWS), ROWS)

    def lanes(b):
        return slice(b * LANES, (b + 1) * LANES)

    taps_first[...] = filter_first_ref[...].astype(jnp.float32)
    taps_second[...] = filter_second_ref[...].astype(jnp.float32)
    eye = lax.broadcasted_iota(jnp.int32, (LANES, LANES), 0) == lax.broadcasted_iota(
        jnp.int32, (LANES, LANES), 1
    )
    for i in range(per // LANES):
        line = skip_ref[pl.ds(me * (per // LANES) + i, 1), :]
        column = jnp.sum(jnp.where(eye, line, 0.0), axis=1, keepdims=True)
        skip_wide[i * LANES : (i + 1) * LANES, :] = jnp.broadcast_to(column, (LANES, LANES))

    pl.semaphore_wait(barrier, n - 1)

    @pl.when(me == 0)
    def _():
        halo_mixed[...] = jnp.zeros_like(halo_mixed)
        halo_first[...] = jnp.zeros_like(halo_first)

    def early(q, _):
        def multiply(d, _):
            mixed[d, part(q), :] = (
                key_ref[d, part(q), :].astype(jnp.float32)
                * value_ref[d, part(q), :].astype(jnp.float32)
            ).astype(jnp.bfloat16)
            return 0

        lax.fori_loop(0, n, multiply, 0)

        @pl.when(me < n - 1)
        def _():
            rim(0, q).start()

        def one(d, _):
            for j in range(groups):
                g = d * (per // ROWS) + q * groups + j
                w = band(taps_first[pl.ds(g, 1), :])
                band_first[g] = w
                band_second[g] = band(taps_second[pl.ds(g, 1), :])
                rows = rows_at(q, j)
                windows = jnp.concatenate(
                    [mixed[d, rows, b * LANES - LANES : (b + 1) * LANES] for b in range(1, blocks)],
                    axis=0,
                )
                result = jnp.dot(windows, w, preferred_element_type=jnp.float32)
                for b in range(1, blocks):
                    first[d, rows, lanes(b)] = gated(
                        gate_first_ref[d, rows, lanes(b)], result[(b - 1) * ROWS : b * ROWS]
                    )
            return 0

        lax.fori_loop(0, n, one, 0)

        @pl.when(me < n - 1)
        def _():
            rim(1, q).start()

        return 0

    lax.fori_loop(0, chunks, early, 0)
    loads[0].wait()

    def late(q, _):
        @pl.when(me > 0)
        def _():
            rim(0, q).wait_recv()
            rim(1, q).wait_recv()

        for k in [*range(2, n), 1, 0]:
            d = lax.rem(me + k, n)
            target = second if k else gathered
            for j in range(groups):
                g = d * (per // ROWS) + q * groups + j
                rows = rows_at(q, j)
                head = jnp.concatenate([halo_mixed[d, rows, :], mixed[d, rows, lanes(0)]], axis=1)
                head = jnp.dot(head, band_first[g], preferred_element_type=jnp.float32)
                head = gated(gate_first_ref[d, rows, lanes(0)], head)
                parts = [halo_first[d, rows, :], head]
                parts += [first[d, rows, lanes(b)] for b in range(1, blocks)]
                windows = jnp.concatenate(
                    [
                        jnp.concatenate([parts[b], parts[b + 1]], axis=1)
                        for b in range(blocks)
                    ],
                    axis=0,
                )
                result = jnp.dot(windows, band_second[g], preferred_element_type=jnp.float32)
                for b in range(blocks):
                    target[d, rows, lanes(b)] = gated(
                        gate_second[d, rows, lanes(b)], result[b * ROWS : (b + 1) * ROWS]
                    )
            if k:
                there(k, q).start()
        return 0

    lax.fori_loop(0, chunks, late, 0)

    def spread(values, at):
        bins = padded_bins(values)
        for r in range(bin_count):
            re, im = bins[r]
            im = jnp.zeros_like(re) if im is None else im
            bins_in[r, at, :] = jnp.concatenate([re, im], axis=1).astype(jnp.bfloat16)

    loads[1].wait()
    loads[2].wait()

    def filter_rows(j, _):
        at = pl.ds(pl.multiple_of(j * ROWS, ROWS), ROWS)
        spread([long_filter[at, lanes(a)].astype(jnp.float32) for a in range(total_blocks)], at)
        return 0

    lax.fori_loop(0, per // ROWS, filter_rows, 0)

    def filter_bin(r, _):
        spectrum[r] = jnp.dot(bins_in[r], forward[r], preferred_element_type=jnp.float32)
        return 0

    lax.fori_loop(0, bin_count, filter_bin, 0)
    loads[3].wait()

    def convolve(q, _):
        for k in range(1, n):
            there(k, q, True).wait_recv()

        def signal(j, rows):
            return [
                gathered[a // blocks, rows, lanes(a % blocks)].astype(jnp.float32)
                for a in range(total_blocks)
            ]

        def rows_in(j, _):
            at = pl.ds(pl.multiple_of(j * ROWS, ROWS), ROWS)
            spread(signal(j, rows_at(q, j)), at)
            return 0

        lax.fori_loop(0, groups, rows_in, 0)

        for r in range(bin_count):
            sig = jnp.dot(bins_in[r, 0:chunk, :], forward[r], preferred_element_type=jnp.float32)
            filt = spectrum[r, part(q), :]
            sig_re, sig_im = sig[:, :LANES], sig[:, LANES:]
            filt_re, filt_im = filt[:, :LANES], filt[:, LANES:]
            product = jnp.concatenate(
                [sig_re * filt_re - sig_im * filt_im, sig_re * filt_im + sig_im * filt_re], axis=1
            ).astype(jnp.bfloat16)
            bins_out[r] = jnp.dot(product, backward[r], preferred_element_type=jnp.float32)

        def rows_out(j, _):
            at = pl.ds(pl.multiple_of(j * ROWS, ROWS), ROWS)
            rows = rows_at(q, j)
            bins = {
                r: (bins_out[r, at, :LANES], bins_out[r, at, LANES:]) for r in range(bin_count)
            }
            result = padded_back(bins, total_blocks)
            skip = skip_wide[rows, :]
            for a, value in enumerate(signal(j, rows)):
                long_out[a // blocks, rows, lanes(a % blocks)] = (
                    skip * value + result[a]
                ).astype(jnp.bfloat16)
            return 0

        lax.fori_loop(0, groups, rows_out, 0)
        for k in range(1, n):
            home(k, q).start()
        returned[me, part(q), :] = long_out[me, part(q), :]
        return 0

    lax.fori_loop(0, chunks, convolve, 0)
    loads[4].wait()

    def finish(q, _):
        for k in range(n):
            if k:
                home(k, q, True).wait_recv()
            p = lax.rem(me + (n - k), n)
            out_ref[p, part(q), :] = gated(
                gate_long[p, part(q), :], returned[p, part(q), :].astype(jnp.float32)
            )
        return 0

    lax.fori_loop(0, chunks, finish, 0)

    def drain(q, _):
        @pl.when(me < n - 1)
        def _():
            rim(0, q).wait_send()
            rim(1, q).wait_send()

        for k in range(1, n):
            there(k, q).wait_send()
            home(k, q).wait_send()
        return 0

    lax.fori_loop(0, chunks, drain, 0)


def fits_kernel(channels, length, n, tap_count):
    per = channels // n
    total = n * length
    return (
        tap_count == LANES
        and length % LANES == 0
        and length >= 2 * LANES
        and per % LANES == 0
        and n > 1
        and total & (total - 1) == 0
        and total <= 2048
        and channels * total <= 1024 * 2048
    )


def shards(
    value_in,
    key_in,
    gate_first,
    gate_second,
    gate_long,
    filter_first,
    filter_second,
    long_filter,
    skip_gain,
):
    channels, length = value_in.shape
    n = lax.axis_size("ctx")
    if not fits_kernel(channels, length, n, filter_first.shape[1]):
        return shards_general(
            value_in,
            key_in,
            gate_first,
            gate_second,
            gate_long,
            filter_first,
            filter_second,
            long_filter,
            skip_gain,
        )
    per = channels // n
    total = n * length
    chunk = 64
    chunks = per // chunk
    group_count = filter_first.shape[0]
    bin_count = total // LANES + 1
    cut = lambda a: a.reshape(n, per, length)
    forward, back = inner_tables(total)
    bf16, f32 = jnp.bfloat16, jnp.float32
    vmem = pl.BlockSpec(memory_space=pltpu.VMEM)
    anywhere = pl.BlockSpec(memory_space=pl.ANY)
    dma = pltpu.SemaphoreType.DMA
    out = pl.pallas_call(
        functools.partial(whole_kernel, n, chunk),
        out_shape=jax.ShapeDtypeStruct((n, per, length), bf16),
        in_specs=[vmem] * 6 + [anywhere] * 5,
        out_specs=vmem,
        scratch_shapes=[
            pltpu.VMEM((n, per, length), bf16),
            pltpu.VMEM((n, per, length), bf16),
            pltpu.VMEM((per, total), bf16),
            pltpu.VMEM(forward.shape, bf16),
            pltpu.VMEM(back.shape, bf16),
            pltpu.VMEM(filter_first.shape, f32),
            pltpu.VMEM(filter_second.shape, f32),
            pltpu.VMEM((group_count, 2 * LANES, LANES), bf16),
            pltpu.VMEM((group_count, 2 * LANES, LANES), bf16),
            pltpu.VMEM((n, per, length), bf16),
            pltpu.VMEM((n, per, length), bf16),
            pltpu.VMEM((n, per, LANES), bf16),
            pltpu.VMEM((n, per, LANES), bf16),
            pltpu.VMEM((n, per, length), bf16),
            pltpu.VMEM((n, per, length), bf16),
            pltpu.VMEM((n, per, length), bf16),
            pltpu.VMEM((n, per, length), bf16),
            pltpu.VMEM((per, LANES), f32),
            pltpu.VMEM((bin_count, per, 2 * LANES), bf16),
            pltpu.VMEM((bin_count, per, 2 * LANES), f32),
            pltpu.VMEM((bin_count, chunk, 2 * LANES), f32),
            dma((5,)),
            dma((2, chunks)),
            dma((2, chunks)),
            dma((n, chunks)),
            dma((n, chunks)),
            dma((n, chunks)),
            dma((n, chunks)),
        ],
        compiler_params=pltpu.CompilerParams(
            collective_id=0, has_side_effects=True, vmem_limit_bytes=56 * 1024 * 1024
        ),
        cost_estimate=pl.CostEstimate(
            flops=8 * channels * length * 2 * LANES + 6 * 2 * per * total * 2 * LANES * 2,
            bytes_accessed=8 * channels * length * 2,
            transcendentals=0,
        ),
    )(
        cut(value_in),
        cut(key_in),
        cut(gate_first),
        filter_first,
        filter_second,
        skip_gain.reshape(channels // LANES, LANES),
        cut(gate_second),
        cut(gate_long),
        long_filter,
        jnp.asarray(forward),
        jnp.asarray(back),
    )
    return out.reshape(channels, length)


def solution(mesh):
    placed = (
        P("ch", "ctx"),
        P("ch", "ctx"),
        P("ch", "ctx"),
        P("ch", "ctx"),
        P("ch", "ctx"),
        P("ch", None),
        P("ch", None),
        P(("ch", "ctx"), None),
        P("ch"),
    )
    return jax.shard_map(
        shards, mesh=mesh, in_specs=placed, out_specs=P("ch", "ctx"), check_vma=False
    )
```

```python
import cmath
import functools
import math

import jax
import jax.numpy as jnp
import ml_dtypes
import numpy as np
from jax import lax
from jax.experimental import pallas as pl
from jax.experimental.pallas import tpu as pltpu
from jax.sharding import PartitionSpec as P

HIGH = lax.Precision.HIGH
LANES = 128
ROWS = 16
MESH = pl.DeviceIdType.MESH


def from_behind(shard, axis, by):
    devices = lax.axis_size(axis)
    pairs = [(i, i + by) for i in range(devices) if 0 <= i + by < devices]
    return lax.ppermute(shard, axis, pairs)


def band_matrix(filters, tap_count):
    group_count = filters.shape[0]
    zero_one = jnp.zeros((group_count, 1), filters.dtype)
    zero_rest = jnp.zeros((group_count, tap_count), filters.dtype)
    pattern = jnp.concatenate([zero_one, jnp.flip(filters, axis=1), zero_rest], axis=1)
    tiled = jnp.tile(pattern, (1, tap_count))
    return tiled[:, : tap_count * 2 * tap_count].reshape(group_count, tap_count, 2 * tap_count)


def toeplitz_conv(extended, filters, tap_count):
    channels, total_len = extended.shape
    length = total_len - tap_count
    block_count = length // tap_count
    front_half = extended[:, :length].reshape(channels, block_count, tap_count)
    back_half = extended[:, tap_count:].reshape(channels, block_count, tap_count)
    windows = jnp.concatenate([front_half, back_half], axis=2)
    group_count = filters.shape[0]
    windows = windows.reshape(group_count, channels // group_count, block_count, 2 * tap_count)
    toeplitz = band_matrix(filters, tap_count)
    result = jnp.einsum("gts,gcbs->gcbt", toeplitz, windows, preferred_element_type=jnp.float32)
    return result.reshape(channels, length)


def previous_rim(tail):
    return from_behind(tail, "ctx", 1)


def to_channels(data):
    return lax.all_to_all(data, "ctx", split_axis=0, concat_axis=1, tiled=True)


def first_section(mixed_in, gate_first, filter_first, tap_count):
    length = mixed_in.shape[1]
    extended = jnp.concatenate([previous_rim(mixed_in[:, length - tap_count :]), mixed_in], axis=1)
    return (
        gate_first.astype(jnp.float32) * toeplitz_conv(extended, filter_first, tap_count)
    ).astype(jnp.bfloat16)


def dft_tables(size):
    index = jnp.arange(size, dtype=jnp.int32)
    angle = (index[:, None] * index[None, :] % size).astype(jnp.float32) * (-2.0 * math.pi / size)
    return (jnp.cos(angle), jnp.sin(angle))


def split_factor(padded_len):
    outer = 2
    cand = 2
    while cand * cand <= padded_len:
        if padded_len % cand == 0:
            outer = cand
        cand = cand + 2
    return outer


def long_convolution(signal, filt_vals, skip_part):
    channels, length = signal.shape
    padded_len = 2 * length
    rows_outer = split_factor(padded_len)
    rows_inner = padded_len // rows_outer
    half_rows = rows_outer // 2
    outer_cos, outer_sin = dft_tables(rows_outer)
    inner_cos, inner_sin = dft_tables(rows_inner)
    k_index = jnp.arange(rows_outer, dtype=jnp.int32)[:, None]
    n_index = jnp.arange(rows_inner, dtype=jnp.int32)[None, :]
    twid_angle = (k_index * n_index % padded_len).astype(jnp.float32) * (
        -2.0 * math.pi / padded_len
    )
    twid_cos = jnp.cos(twid_angle)
    twid_sin = jnp.sin(twid_angle)
    outer_table = jnp.concatenate([outer_cos[:, :half_rows], outer_sin[:, :half_rows]], axis=0)
    inner_fwd = jnp.concatenate(
        [
            jnp.concatenate([inner_cos, inner_sin], axis=1),
            jnp.concatenate([-inner_sin, inner_cos], axis=1),
        ],
        axis=0,
    )
    inner_back = jnp.concatenate(
        [
            jnp.concatenate([inner_cos, -inner_sin], axis=1),
            jnp.concatenate([inner_sin, inner_cos], axis=1),
        ],
        axis=0,
    )

    def forward(values):
        grid = values.reshape(channels, half_rows, rows_inner)
        parts = jnp.einsum("kn,cnm->ckm", outer_table, grid, precision=HIGH)
        part_re = parts[:, :rows_outer]
        part_im = parts[:, rows_outer:]
        turned_re = part_re * twid_cos - part_im * twid_sin
        turned_im = part_re * twid_sin + part_im * twid_cos
        turned = jnp.concatenate([turned_re, turned_im], axis=2)
        spectrum = jnp.einsum("ckn,nm->ckm", turned, inner_fwd, precision=HIGH)
        return (spectrum[:, :, :rows_inner], spectrum[:, :, rows_inner:])

    sig_re, sig_im = forward(signal)
    filt_re, filt_im = forward(filt_vals)
    prod_re = sig_re * filt_re - sig_im * filt_im
    prod_im = sig_re * filt_im + sig_im * filt_re
    stacked = jnp.concatenate([prod_re, prod_im], axis=2)
    back = jnp.einsum("ckm,mn->ckn", stacked, inner_back, precision=HIGH)
    back_re = back[:, :, :rows_inner]
    back_im = back[:, :, rows_inner:]
    reverted_re = back_re * twid_cos + back_im * twid_sin
    reverted_im = back_im * twid_cos - back_re * twid_sin
    reverted = jnp.concatenate([reverted_re, reverted_im], axis=1)
    result = jnp.einsum("kn,ckm->cnm", outer_table, reverted, precision=HIGH)
    result = result.reshape(channels, length) / padded_len
    return skip_part[:, None] * signal + result


def shards_general(
    value_in,
    key_in,
    gate_first,
    gate_second,
    gate_long,
    filter_first,
    filter_second,
    long_filter,
    skip_gain,
):
    tap_count = filter_first.shape[1]
    channels, length = value_in.shape
    per_device = channels // lax.axis_size("ctx")
    channel_base = lax.axis_index("ctx") * per_device
    mixed_in = (key_in.astype(jnp.float32) * value_in.astype(jnp.float32)).astype(jnp.bfloat16)
    first_out = first_section(mixed_in, gate_first, filter_first, tap_count)
    prior_first = from_behind(first_out[:, length - tap_count :], "ctx", 1)
    first_wide = jnp.concatenate([prior_first, first_out], axis=1)
    second_out = (
        gate_second.astype(jnp.float32) * toeplitz_conv(first_wide, filter_second, tap_count)
    ).astype(jnp.bfloat16)
    moved = to_channels(second_out)
    skip_here = lax.dynamic_slice_in_dim(skip_gain, channel_base, per_device, 0)
    filt_vals = long_filter.astype(jnp.float32)
    long_out = long_convolution(moved.astype(jnp.float32), filt_vals, skip_here).astype(
        jnp.bfloat16
    )
    back_home = lax.all_to_all(long_out, "ctx", split_axis=1, concat_axis=0, tiled=True)
    return (gate_long.astype(jnp.float32) * back_home.astype(jnp.float32)).astype(jnp.bfloat16)


def unit(numerator, denominator):
    return cmath.exp(-2j * math.pi * numerator / denominator)


def turn(value, factor):
    re, im = value
    if abs(factor - 1) < 1e-12:
        return value
    if abs(factor + 1j) < 1e-12:
        return (im, -re)
    if abs(factor - 1j) < 1e-12:
        return (-im, re)
    if abs(abs(factor.real) - abs(factor.imag)) < 1e-12:
        size = abs(factor.real)
        re, im = re * size, im * size
        if factor.real > 0 and factor.imag < 0:
            return (re + im, im - re)
        if factor.real < 0 and factor.imag < 0:
            return (im - re, -re - im)
        if factor.real > 0:
            return (re - im, re + im)
        return (-re - im, re - im)
    return (re * factor.real - im * factor.imag, re * factor.imag + im * factor.real)


def complex_dft(values, sign):
    count = len(values)
    if count == 1:
        return values
    half = count // 2
    low, high = [], []
    for a in range(half):
        (p_re, p_im), (q_re, q_im) = values[a], values[a + half]
        low.append((p_re + q_re, p_im + q_im))
        factor = unit(a, count)
        high.append(turn((p_re - q_re, p_im - q_im), factor if sign > 0 else factor.conjugate()))
    result = [None] * count
    result[0::2] = complex_dft(low, sign)
    result[1::2] = complex_dft(high, sign)
    return result


def odd_bins(values):
    count = len(values)
    if count == 1:
        return {1: (values[0], None)}
    half = count // 2
    folded = [turn((values[a], -values[a + half]), unit(a, 2 * count)) for a in range(half)]
    bins = {}
    for place, (re, im) in enumerate(complex_dft(folded, 1)):
        r = 4 * place + 1
        if r < count:
            bins[r] = (re, im)
        else:
            bins[2 * count - r] = (re, -im)
    return bins


def real_bins(values):
    count = len(values)
    if count == 1:
        return {0: (values[0], None)}
    half = count // 2
    even = real_bins([values[a] + values[a + half] for a in range(half)])
    odd = odd_bins([values[a] - values[a + half] for a in range(half)])
    bins = {2 * r: v for r, v in even.items()}
    bins.update(odd)
    return bins


def padded_bins(values):
    bins = {2 * r: v for r, v in real_bins(values).items()}
    bins.update(odd_bins(values))
    return bins


def odd_back(bins, count):
    if count == 1:
        return [bins[1][0]]
    half = count // 2
    folded = []
    for place in range(half):
        r = 4 * place + 1
        if r < count:
            folded.append(bins[r])
        else:
            re, im = bins[2 * count - r]
            folded.append((re, -im))
    spread = complex_dft(folded, -1)
    spread = [turn(spread[a], unit(a, 2 * count).conjugate()) for a in range(half)]
    return [v[0] for v in spread] + [-v[1] for v in spread]


def real_back(bins, count):
    if count == 1:
        return [bins[0][0]]
    half = count // 2
    even = real_back({r // 2: v for r, v in bins.items() if r % 2 == 0}, half)
    odd = odd_back({r: v for r, v in bins.items() if r % 2 == 1}, half)
    return [even[a] + odd[a] for a in range(half)] + [even[a] - odd[a] for a in range(half)]


def padded_back(bins, count):
    even = real_back({r // 2: v for r, v in bins.items() if r % 2 == 0}, count)
    odd = odd_back({r: v for r, v in bins.items() if r % 2 == 1}, count)
    return [even[a] + odd[a] for a in range(count)]


def inner_tables(length):
    padded_len = 2 * length
    outer = padded_len // LANES
    b = np.arange(LANES)[:, None]
    q = np.arange(LANES)[None, :]
    forward, back = [], []
    for r in range(outer // 2 + 1):
        angle = (b * (r + outer * q) % padded_len) * (-2.0 * math.pi / padded_len)
        c, s = np.cos(angle), np.sin(angle)
        table = np.block([[c, s], [-s, c]])
        weight = (1.0 if r in (0, outer // 2) else 2.0) / padded_len
        forward.append(table)
        back.append(table.T * weight)
    return (
        np.stack(forward).astype(ml_dtypes.bfloat16),
        np.stack(back).astype(ml_dtypes.bfloat16),
    )


def band(row):
    rolled = pltpu.roll(jnp.broadcast_to(row, (LANES, LANES)), 0, 1, stride=1, stride_axis=0)
    s = lax.broadcasted_iota(jnp.int32, (LANES, LANES), 0)
    t = lax.broadcasted_iota(jnp.int32, (LANES, LANES), 1)
    zero = jnp.zeros((LANES, LANES), jnp.float32)
    return jnp.concatenate(
        [jnp.where(t < s, rolled, zero), jnp.where(t >= s, rolled, zero)], axis=0
    ).astype(jnp.bfloat16)


def gated(gate, value):
    return (gate.astype(jnp.float32) * value).astype(jnp.bfloat16)


def whole_kernel(
    n,
    chunk,
    filter_first_ref,
    filter_second_ref,
    skip_ref,
    value_hbm,
    key_hbm,
    gate_first_hbm,
    gate_second_hbm,
    long_filter_hbm,
    forward_hbm,
    back_hbm,
    returned,
    value_ref,
    key_ref,
    gate_first_ref,
    gate_second,
    long_filter,
    forward,
    backward,
    taps_first,
    taps_second,
    band_first,
    band_second,
    mixed,
    first,
    halo_mixed,
    halo_first,
    second,
    gathered,
    long_out,
    skip_wide,
    bins_in,
    spectrum,
    bins_out,
    load_sem,
    part_sem,
    own_sem,
    rim_send,
    rim_recv,
    there_send,
    there_recv,
    home_send,
    home_recv,
):
    _, per, length = value_hbm.shape
    me = lax.axis_index("ctx")
    blocks = length // LANES
    chunks = per // chunk
    groups = chunk // ROWS
    total_blocks = n * blocks
    bin_count = total_blocks + 1
    last = slice(length - LANES, length)

    barrier = pltpu.get_barrier_semaphore()
    for k in range(1, n):
        pl.semaphore_signal(
            barrier, inc=1, device_id={"ctx": lax.rem(me + k, n)}, device_id_type=MESH
        )

    def part(q):
        return pl.ds(pl.multiple_of(q * chunk, chunk), chunk)

    def loaded(i, q):
        src, dst = (
            (key_hbm, key_ref),
            (value_hbm, value_ref),
            (gate_first_hbm, gate_first_ref),
            (gate_second_hbm, gate_second),
        )[i]
        return pltpu.make_async_copy(
            src.at[:, part(q), :], dst.at[:, part(q), :], part_sem.at[i, q]
        )

    for q in range(chunks):
        for i in range(4):
            loaded(i, q).start()
    loads = [
        pltpu.make_async_copy(src, dst, load_sem.at[i])
        for i, (src, dst) in enumerate(
            [(long_filter_hbm, long_filter), (forward_hbm, forward), (back_hbm, backward)]
        )
    ]
    for load in loads:
        load.start()

    def own(q):
        return pltpu.make_async_copy(
            long_out.at[me, part(q), :], returned.at[me, part(q), :], own_sem.at[q]
        )

    def rim(which, q):
        src, dst = ((mixed, halo_mixed), (first, halo_first))[which]
        return pltpu.make_async_remote_copy(
            src_ref=src.at[:, part(q), last],
            dst_ref=dst.at[:, part(q), :],
            send_sem=rim_send.at[which, q],
            recv_sem=rim_recv.at[which, q],
            device_id={"ctx": lax.rem(me + 1, n)},
            device_id_type=MESH,
        )

    def there(k, q, arriving=False):
        peer = lax.rem(me + (n - k if arriving else k), n)
        slot = peer if arriving else me
        return pltpu.make_async_remote_copy(
            src_ref=second.at[peer, part(q), :],
            dst_ref=gathered.at[slot, part(q), :],
            send_sem=there_send.at[k, q],
            recv_sem=there_recv.at[k, q],
            device_id={"ctx": peer},
            device_id_type=MESH,
        )

    def home(k, q, arriving=False):
        peer = lax.rem(me + (n - k if arriving else k), n)
        slot = peer if arriving else me
        return pltpu.make_async_remote_copy(
            src_ref=long_out.at[peer, part(q), :],
            dst_ref=returned.at[slot, part(q), :],
            send_sem=home_send.at[k, q],
            recv_sem=home_recv.at[k, q],
            device_id={"ctx": peer},
            device_id_type=MESH,
        )

    def rows_at(q, j):
        return pl.ds(pl.multiple_of(q * chunk + j * ROWS, ROWS), ROWS)

    def lanes(b):
        return slice(b * LANES, (b + 1) * LANES)

    taps_first[...] = filter_first_ref[...].astype(jnp.float32)
    taps_second[...] = filter_second_ref[...].astype(jnp.float32)
    eye = lax.broadcasted_iota(jnp.int32, (LANES, LANES), 0) == lax.broadcasted_iota(
        jnp.int32, (LANES, LANES), 1
    )
    for i in range(per // LANES):
        line = skip_ref[pl.ds(me * (per // LANES) + i, 1), :]
        column = jnp.sum(jnp.where(eye, line, 0.0), axis=1, keepdims=True)
        skip_wide[i * LANES : (i + 1) * LANES, :] = jnp.broadcast_to(column, (LANES, LANES))

    pl.semaphore_wait(barrier, n - 1)

    @pl.when(me == 0)
    def _():
        halo_mixed[...] = jnp.zeros_like(halo_mixed)
        halo_first[...] = jnp.zeros_like(halo_first)

    def early(q):
        loaded(0, q).wait()
        loaded(1, q).wait()

        def multiply(d, _):
            mixed[d, part(q), :] = (
                key_ref[d, part(q), :].astype(jnp.float32)
                * value_ref[d, part(q), :].astype(jnp.float32)
            ).astype(jnp.bfloat16)
            return 0

        lax.fori_loop(0, n, multiply, 0)

        @pl.when(me < n - 1)
        def _():
            rim(0, q).start()

        loaded(2, q).wait()

        def one(d, _):
            for j in range(groups):
                g = d * (per // ROWS) + q * groups + j
                w = band(taps_first[pl.ds(g, 1), :])
                band_first[g] = w
                band_second[g] = band(taps_second[pl.ds(g, 1), :])
                rows = rows_at(q, j)
                windows = jnp.concatenate(
                    [mixed[d, rows, b * LANES - LANES : (b + 1) * LANES] for b in range(1, blocks)],
                    axis=0,
                )
                result = jnp.dot(windows, w, preferred_element_type=jnp.float32)
                for b in range(1, blocks):
                    first[d, rows, lanes(b)] = gated(
                        gate_first_ref[d, rows, lanes(b)], result[(b - 1) * ROWS : b * ROWS]
                    )
            return 0

        lax.fori_loop(0, n, one, 0)

        @pl.when(me < n - 1)
        def _():
            rim(1, q).start()

    def late(q):
        loaded(3, q).wait()

        @pl.when(me > 0)
        def _():
            rim(0, q).wait_recv()
            rim(1, q).wait_recv()

        for k in [*range(2, n), 1, 0]:
            d = lax.rem(me + k, n)
            target = second if k else gathered
            for j in range(groups):
                g = d * (per // ROWS) + q * groups + j
                rows = rows_at(q, j)
                head = jnp.concatenate([halo_mixed[d, rows, :], mixed[d, rows, lanes(0)]], axis=1)
                head = jnp.dot(head, band_first[g], preferred_element_type=jnp.float32)
                head = gated(gate_first_ref[d, rows, lanes(0)], head)
                parts = [halo_first[d, rows, :], head]
                parts += [first[d, rows, lanes(b)] for b in range(1, blocks)]
                windows = jnp.concatenate(
                    [
                        jnp.concatenate([parts[b], parts[b + 1]], axis=1)
                        for b in range(blocks)
                    ],
                    axis=0,
                )
                result = jnp.dot(windows, band_second[g], preferred_element_type=jnp.float32)
                for b in range(blocks):
                    target[d, rows, lanes(b)] = gated(
                        gate_second[d, rows, lanes(b)], result[b * ROWS : (b + 1) * ROWS]
                    )
            if k:
                there(k, q).start()

    early(0)

    def both(q, _):
        early(q + 1)
        late(q)
        return 0

    lax.fori_loop(0, chunks - 1, both, 0)
    late(chunks - 1)

    def spread(values, at):
        bins = padded_bins(values)
        for r in range(bin_count):
            re, im = bins[r]
            im = jnp.zeros_like(re) if im is None else im
            bins_in[r, at, :] = jnp.concatenate([re, im], axis=1).astype(jnp.bfloat16)

    loads[0].wait()
    loads[1].wait()

    def filter_rows(j, _):
        at = pl.ds(pl.multiple_of(j * ROWS, ROWS), ROWS)
        spread([long_filter[at, lanes(a)].astype(jnp.float32) for a in range(total_blocks)], at)
        return 0

    lax.fori_loop(0, per // ROWS, filter_rows, 0)

    def filter_bin(r, _):
        spectrum[r] = jnp.dot(bins_in[r], forward[r], preferred_element_type=jnp.float32)
        return 0

    lax.fori_loop(0, bin_count, filter_bin, 0)
    loads[2].wait()

    def convolve(q, _):
        for k in range(1, n):
            there(k, q, True).wait_recv()

        def signal(j, rows):
            return [
                gathered[a // blocks, rows, lanes(a % blocks)].astype(jnp.float32)
                for a in range(total_blocks)
            ]

        def rows_in(j, _):
            at = pl.ds(pl.multiple_of(j * ROWS, ROWS), ROWS)
            spread(signal(j, rows_at(q, j)), at)
            return 0

        lax.fori_loop(0, groups, rows_in, 0)

        for r in range(bin_count):
            sig = jnp.dot(bins_in[r, 0:chunk, :], forward[r], preferred_element_type=jnp.float32)
            filt = spectrum[r, part(q), :]
            sig_re, sig_im = sig[:, :LANES], sig[:, LANES:]
            filt_re, filt_im = filt[:, :LANES], filt[:, LANES:]
            product = jnp.concatenate(
                [sig_re * filt_re - sig_im * filt_im, sig_re * filt_im + sig_im * filt_re], axis=1
            ).astype(jnp.bfloat16)
            bins_out[r] = jnp.dot(product, backward[r], preferred_element_type=jnp.float32)

        def rows_out(j, _):
            at = pl.ds(pl.multiple_of(j * ROWS, ROWS), ROWS)
            rows = rows_at(q, j)
            bins = {
                r: (bins_out[r, at, :LANES], bins_out[r, at, LANES:]) for r in range(bin_count)
            }
            result = padded_back(bins, total_blocks)
            skip = skip_wide[rows, :]
            for a, value in enumerate(signal(j, rows)):
                long_out[a // blocks, rows, lanes(a % blocks)] = (
                    skip * value + result[a]
                ).astype(jnp.bfloat16)
            return 0

        lax.fori_loop(0, groups, rows_out, 0)
        for k in range(1, n):
            home(k, q).start()
        own(q).start()
        return 0

    lax.fori_loop(0, chunks, convolve, 0)
    def drain(q, _):
        @pl.when(me < n - 1)
        def _():
            rim(0, q).wait_send()
            rim(1, q).wait_send()

        own(q).wait()
        for k in range(1, n):
            there(k, q).wait_send()
            home(k, q).wait_send()
            home(k, q, True).wait_recv()
        return 0

    lax.fori_loop(0, chunks, drain, 0)


def fits_kernel(channels, length, n, tap_count):
    per = channels // n
    total = n * length
    return (
        tap_count == LANES
        and length % LANES == 0
        and length >= 2 * LANES
        and per % LANES == 0
        and n > 1
        and total & (total - 1) == 0
        and total <= 2048
        and channels * total <= 1024 * 2048
    )


def shards(
    value_in,
    key_in,
    gate_first,
    gate_second,
    gate_long,
    filter_first,
    filter_second,
    long_filter,
    skip_gain,
):
    channels, length = value_in.shape
    n = lax.axis_size("ctx")
    if not fits_kernel(channels, length, n, filter_first.shape[1]):
        return shards_general(
            value_in,
            key_in,
            gate_first,
            gate_second,
            gate_long,
            filter_first,
            filter_second,
            long_filter,
            skip_gain,
        )
    per = channels // n
    total = n * length
    chunk = 64
    chunks = per // chunk
    group_count = filter_first.shape[0]
    bin_count = total // LANES + 1
    cut = lambda a: a.reshape(n, per, length)
    forward, back = inner_tables(total)
    bf16, f32 = jnp.bfloat16, jnp.float32
    vmem = pl.BlockSpec(memory_space=pltpu.VMEM)
    anywhere = pl.BlockSpec(memory_space=pl.ANY)
    in_hbm = pl.BlockSpec(memory_space=pltpu.HBM)
    dma = pltpu.SemaphoreType.DMA
    out = pl.pallas_call(
        functools.partial(whole_kernel, n, chunk),
        out_shape=jax.ShapeDtypeStruct((n, per, length), bf16),
        in_specs=[vmem] * 3 + [in_hbm] * 7,
        out_specs=anywhere,
        scratch_shapes=[
            pltpu.VMEM((n, per, length), bf16),
            pltpu.VMEM((n, per, length), bf16),
            pltpu.VMEM((n, per, length), bf16),
            pltpu.VMEM((n, per, length), bf16),
            pltpu.VMEM((per, total), bf16),
            pltpu.VMEM(forward.shape, bf16),
            pltpu.VMEM(back.shape, bf16),
            pltpu.VMEM(filter_first.shape, f32),
            pltpu.VMEM(filter_second.shape, f32),
            pltpu.VMEM((group_count, 2 * LANES, LANES), bf16),
            pltpu.VMEM((group_count, 2 * LANES, LANES), bf16),
            pltpu.VMEM((n, per, length), bf16),
            pltpu.VMEM((n, per, length), bf16),
            pltpu.VMEM((n, per, LANES), bf16),
            pltpu.VMEM((n, per, LANES), bf16),
            pltpu.VMEM((n, per, length), bf16),
            pltpu.VMEM((n, per, length), bf16),
            pltpu.VMEM((n, per, length), bf16),
            pltpu.VMEM((per, LANES), f32),
            pltpu.VMEM((bin_count, per, 2 * LANES), bf16),
            pltpu.VMEM((bin_count, per, 2 * LANES), f32),
            pltpu.VMEM((bin_count, chunk, 2 * LANES), f32),
            dma((3,)),
            dma((4, chunks)),
            dma((chunks,)),
            dma((2, chunks)),
            dma((2, chunks)),
            dma((n, chunks)),
            dma((n, chunks)),
            dma((n, chunks)),
            dma((n, chunks)),
        ],
        compiler_params=pltpu.CompilerParams(
            collective_id=0, has_side_effects=True, vmem_limit_bytes=56 * 1024 * 1024
        ),
        cost_estimate=pl.CostEstimate(
            flops=8 * channels * length * 2 * LANES + 6 * 2 * per * total * 2 * LANES * 2,
            bytes_accessed=8 * channels * length * 2,
            transcendentals=0,
        ),
    )(
        filter_first,
        filter_second,
        skip_gain.reshape(channels // LANES, LANES),
        cut(value_in),
        cut(key_in),
        cut(gate_first),
        cut(gate_second),
        long_filter,
        jnp.asarray(forward),
        jnp.asarray(back),
    )
    return gated(gate_long, out.reshape(channels, length).astype(f32))


def solution(mesh):
    placed = (
        P("ch", "ctx"),
        P("ch", "ctx"),
        P("ch", "ctx"),
        P("ch", "ctx"),
        P("ch", "ctx"),
        P("ch", None),
        P("ch", None),
        P(("ch", "ctx"), None),
        P("ch"),
    )
    return jax.shard_map(
        shards, mesh=mesh, in_specs=placed, out_specs=P("ch", "ctx"), check_vma=False
    )
```

```python
import cmath
import functools
import math

import jax
import jax.numpy as jnp
import ml_dtypes
import numpy as np
from jax import lax
from jax.experimental import pallas as pl
from jax.experimental.pallas import tpu as pltpu
from jax.sharding import PartitionSpec as P

HIGH = lax.Precision.HIGH
LANES = 128
ROWS = 16
MESH = pl.DeviceIdType.MESH


def from_behind(shard, axis, by):
    devices = lax.axis_size(axis)
    pairs = [(i, i + by) for i in range(devices) if 0 <= i + by < devices]
    return lax.ppermute(shard, axis, pairs)


def band_matrix(filters, tap_count):
    group_count = filters.shape[0]
    zero_one = jnp.zeros((group_count, 1), filters.dtype)
    zero_rest = jnp.zeros((group_count, tap_count), filters.dtype)
    pattern = jnp.concatenate([zero_one, jnp.flip(filters, axis=1), zero_rest], axis=1)
    tiled = jnp.tile(pattern, (1, tap_count))
    return tiled[:, : tap_count * 2 * tap_count].reshape(group_count, tap_count, 2 * tap_count)


def toeplitz_conv(extended, filters, tap_count):
    channels, total_len = extended.shape
    length = total_len - tap_count
    block_count = length // tap_count
    front_half = extended[:, :length].reshape(channels, block_count, tap_count)
    back_half = extended[:, tap_count:].reshape(channels, block_count, tap_count)
    windows = jnp.concatenate([front_half, back_half], axis=2)
    group_count = filters.shape[0]
    windows = windows.reshape(group_count, channels // group_count, block_count, 2 * tap_count)
    toeplitz = band_matrix(filters, tap_count)
    result = jnp.einsum("gts,gcbs->gcbt", toeplitz, windows, preferred_element_type=jnp.float32)
    return result.reshape(channels, length)


def previous_rim(tail):
    return from_behind(tail, "ctx", 1)


def to_channels(data):
    return lax.all_to_all(data, "ctx", split_axis=0, concat_axis=1, tiled=True)


def first_section(mixed_in, gate_first, filter_first, tap_count):
    length = mixed_in.shape[1]
    extended = jnp.concatenate([previous_rim(mixed_in[:, length - tap_count :]), mixed_in], axis=1)
    return (
        gate_first.astype(jnp.float32) * toeplitz_conv(extended, filter_first, tap_count)
    ).astype(jnp.bfloat16)


def dft_tables(size):
    index = jnp.arange(size, dtype=jnp.int32)
    angle = (index[:, None] * index[None, :] % size).astype(jnp.float32) * (-2.0 * math.pi / size)
    return (jnp.cos(angle), jnp.sin(angle))


def split_factor(padded_len):
    outer = 2
    cand = 2
    while cand * cand <= padded_len:
        if padded_len % cand == 0:
            outer = cand
        cand = cand + 2
    return outer


def long_convolution(signal, filt_vals, skip_part):
    channels, length = signal.shape
    padded_len = 2 * length
    rows_outer = split_factor(padded_len)
    rows_inner = padded_len // rows_outer
    half_rows = rows_outer // 2
    outer_cos, outer_sin = dft_tables(rows_outer)
    inner_cos, inner_sin = dft_tables(rows_inner)
    k_index = jnp.arange(rows_outer, dtype=jnp.int32)[:, None]
    n_index = jnp.arange(rows_inner, dtype=jnp.int32)[None, :]
    twid_angle = (k_index * n_index % padded_len).astype(jnp.float32) * (
        -2.0 * math.pi / padded_len
    )
    twid_cos = jnp.cos(twid_angle)
    twid_sin = jnp.sin(twid_angle)
    outer_table = jnp.concatenate([outer_cos[:, :half_rows], outer_sin[:, :half_rows]], axis=0)
    inner_fwd = jnp.concatenate(
        [
            jnp.concatenate([inner_cos, inner_sin], axis=1),
            jnp.concatenate([-inner_sin, inner_cos], axis=1),
        ],
        axis=0,
    )
    inner_back = jnp.concatenate(
        [
            jnp.concatenate([inner_cos, -inner_sin], axis=1),
            jnp.concatenate([inner_sin, inner_cos], axis=1),
        ],
        axis=0,
    )

    def forward(values):
        grid = values.reshape(channels, half_rows, rows_inner)
        parts = jnp.einsum("kn,cnm->ckm", outer_table, grid, precision=HIGH)
        part_re = parts[:, :rows_outer]
        part_im = parts[:, rows_outer:]
        turned_re = part_re * twid_cos - part_im * twid_sin
        turned_im = part_re * twid_sin + part_im * twid_cos
        turned = jnp.concatenate([turned_re, turned_im], axis=2)
        spectrum = jnp.einsum("ckn,nm->ckm", turned, inner_fwd, precision=HIGH)
        return (spectrum[:, :, :rows_inner], spectrum[:, :, rows_inner:])

    sig_re, sig_im = forward(signal)
    filt_re, filt_im = forward(filt_vals)
    prod_re = sig_re * filt_re - sig_im * filt_im
    prod_im = sig_re * filt_im + sig_im * filt_re
    stacked = jnp.concatenate([prod_re, prod_im], axis=2)
    back = jnp.einsum("ckm,mn->ckn", stacked, inner_back, precision=HIGH)
    back_re = back[:, :, :rows_inner]
    back_im = back[:, :, rows_inner:]
    reverted_re = back_re * twid_cos + back_im * twid_sin
    reverted_im = back_im * twid_cos - back_re * twid_sin
    reverted = jnp.concatenate([reverted_re, reverted_im], axis=1)
    result = jnp.einsum("kn,ckm->cnm", outer_table, reverted, precision=HIGH)
    result = result.reshape(channels, length) / padded_len
    return skip_part[:, None] * signal + result


def shards_general(
    value_in,
    key_in,
    gate_first,
    gate_second,
    gate_long,
    filter_first,
    filter_second,
    long_filter,
    skip_gain,
):
    tap_count = filter_first.shape[1]
    channels, length = value_in.shape
    per_device = channels // lax.axis_size("ctx")
    channel_base = lax.axis_index("ctx") * per_device
    mixed_in = (key_in.astype(jnp.float32) * value_in.astype(jnp.float32)).astype(jnp.bfloat16)
    first_out = first_section(mixed_in, gate_first, filter_first, tap_count)
    prior_first = from_behind(first_out[:, length - tap_count :], "ctx", 1)
    first_wide = jnp.concatenate([prior_first, first_out], axis=1)
    second_out = (
        gate_second.astype(jnp.float32) * toeplitz_conv(first_wide, filter_second, tap_count)
    ).astype(jnp.bfloat16)
    moved = to_channels(second_out)
    skip_here = lax.dynamic_slice_in_dim(skip_gain, channel_base, per_device, 0)
    filt_vals = long_filter.astype(jnp.float32)
    long_out = long_convolution(moved.astype(jnp.float32), filt_vals, skip_here).astype(
        jnp.bfloat16
    )
    back_home = lax.all_to_all(long_out, "ctx", split_axis=1, concat_axis=0, tiled=True)
    return (gate_long.astype(jnp.float32) * back_home.astype(jnp.float32)).astype(jnp.bfloat16)


def unit(numerator, denominator):
    return cmath.exp(-2j * math.pi * numerator / denominator)


def turn(value, factor):
    re, im = value
    if abs(factor - 1) < 1e-12:
        return value
    if abs(factor + 1j) < 1e-12:
        return (im, -re)
    if abs(factor - 1j) < 1e-12:
        return (-im, re)
    if abs(abs(factor.real) - abs(factor.imag)) < 1e-12:
        size = abs(factor.real)
        re, im = re * size, im * size
        if factor.real > 0 and factor.imag < 0:
            return (re + im, im - re)
        if factor.real < 0 and factor.imag < 0:
            return (im - re, -re - im)
        if factor.real > 0:
            return (re - im, re + im)
        return (-re - im, re - im)
    return (re * factor.real - im * factor.imag, re * factor.imag + im * factor.real)


def complex_dft(values, sign):
    count = len(values)
    if count == 1:
        return values
    half = count // 2
    low, high = [], []
    for a in range(half):
        (p_re, p_im), (q_re, q_im) = values[a], values[a + half]
        low.append((p_re + q_re, p_im + q_im))
        factor = unit(a, count)
        high.append(turn((p_re - q_re, p_im - q_im), factor if sign > 0 else factor.conjugate()))
    result = [None] * count
    result[0::2] = complex_dft(low, sign)
    result[1::2] = complex_dft(high, sign)
    return result


def odd_bins(values):
    count = len(values)
    if count == 1:
        return {1: (values[0], None)}
    half = count // 2
    folded = [turn((values[a], -values[a + half]), unit(a, 2 * count)) for a in range(half)]
    bins = {}
    for place, (re, im) in enumerate(complex_dft(folded, 1)):
        r = 4 * place + 1
        if r < count:
            bins[r] = (re, im)
        else:
            bins[2 * count - r] = (re, -im)
    return bins


def real_bins(values):
    count = len(values)
    if count == 1:
        return {0: (values[0], None)}
    half = count // 2
    even = real_bins([values[a] + values[a + half] for a in range(half)])
    odd = odd_bins([values[a] - values[a + half] for a in range(half)])
    bins = {2 * r: v for r, v in even.items()}
    bins.update(odd)
    return bins


def padded_bins(values):
    bins = {2 * r: v for r, v in real_bins(values).items()}
    bins.update(odd_bins(values))
    return bins


def odd_back(bins, count):
    if count == 1:
        return [bins[1][0]]
    half = count // 2
    folded = []
    for place in range(half):
        r = 4 * place + 1
        if r < count:
            folded.append(bins[r])
        else:
            re, im = bins[2 * count - r]
            folded.append((re, -im))
    spread = complex_dft(folded, -1)
    spread = [turn(spread[a], unit(a, 2 * count).conjugate()) for a in range(half)]
    return [v[0] for v in spread] + [-v[1] for v in spread]


def real_back(bins, count):
    if count == 1:
        return [bins[0][0]]
    half = count // 2
    even = real_back({r // 2: v for r, v in bins.items() if r % 2 == 0}, half)
    odd = odd_back({r: v for r, v in bins.items() if r % 2 == 1}, half)
    return [even[a] + odd[a] for a in range(half)] + [even[a] - odd[a] for a in range(half)]


def padded_back(bins, count):
    even = real_back({r // 2: v for r, v in bins.items() if r % 2 == 0}, count)
    odd = odd_back({r: v for r, v in bins.items() if r % 2 == 1}, count)
    return [even[a] + odd[a] for a in range(count)]


def inner_tables(length):
    padded_len = 2 * length
    outer = padded_len // LANES
    b = np.arange(LANES)[:, None]
    q = np.arange(LANES)[None, :]
    forward, back = [], []
    for r in range(outer // 2 + 1):
        angle = (b * (r + outer * q) % padded_len) * (-2.0 * math.pi / padded_len)
        c, s = np.cos(angle), np.sin(angle)
        table = np.block([[c, s], [-s, c]])
        weight = (1.0 if r in (0, outer // 2) else 2.0) / padded_len
        forward.append(table)
        back.append(table.T * weight)
    return (
        np.stack(forward).astype(ml_dtypes.bfloat16),
        np.stack(back).astype(ml_dtypes.bfloat16),
    )


def band(row):
    rolled = pltpu.roll(jnp.broadcast_to(row, (LANES, LANES)), 0, 1, stride=1, stride_axis=0)
    s = lax.broadcasted_iota(jnp.int32, (LANES, LANES), 0)
    t = lax.broadcasted_iota(jnp.int32, (LANES, LANES), 1)
    zero = jnp.zeros((LANES, LANES), jnp.float32)
    return jnp.concatenate(
        [jnp.where(t < s, rolled, zero), jnp.where(t >= s, rolled, zero)], axis=0
    ).astype(jnp.bfloat16)


def gated(gate, value):
    return (gate.astype(jnp.float32) * value).astype(jnp.bfloat16)


def whole_kernel(
    n,
    chunk,
    filter_first_ref,
    filter_second_ref,
    skip_ref,
    value_hbm,
    key_hbm,
    gate_first_hbm,
    gate_second_hbm,
    long_filter_hbm,
    forward_hbm,
    back_hbm,
    returned,
    value_ref,
    key_ref,
    gate_first_ref,
    gate_second,
    long_filter,
    forward,
    backward,
    taps_first,
    taps_second,
    band_first,
    band_second,
    mixed,
    first,
    halo_mixed,
    halo_first,
    second,
    gathered,
    long_out,
    skip_wide,
    bins_in,
    spectrum,
    products,
    bins_out,
    load_sem,
    part_sem,
    own_sem,
    rim_send,
    rim_recv,
    there_send,
    there_recv,
    home_send,
    home_recv,
):
    _, per, length = value_hbm.shape
    me = lax.axis_index("ctx")
    blocks = length // LANES
    chunks = per // chunk
    groups = chunk // ROWS
    total_blocks = n * blocks
    bin_count = total_blocks + 1
    last = slice(length - LANES, length)

    barrier = pltpu.get_barrier_semaphore()
    for k in range(1, n):
        pl.semaphore_signal(
            barrier, inc=1, device_id={"ctx": lax.rem(me + k, n)}, device_id_type=MESH
        )

    def part(q):
        return pl.ds(pl.multiple_of(q * chunk, chunk), chunk)

    def loaded(i, q):
        src, dst = (
            (key_hbm, key_ref),
            (value_hbm, value_ref),
            (gate_first_hbm, gate_first_ref),
            (gate_second_hbm, gate_second),
        )[i]
        return pltpu.make_async_copy(
            src.at[:, part(q), :], dst.at[:, part(q), :], part_sem.at[i, q]
        )

    for q in range(chunks):
        for i in range(4):
            loaded(i, q).start()
    loads = [
        pltpu.make_async_copy(src, dst, load_sem.at[i])
        for i, (src, dst) in enumerate(
            [(long_filter_hbm, long_filter), (forward_hbm, forward), (back_hbm, backward)]
        )
    ]
    for load in loads:
        load.start()

    def own(q):
        return pltpu.make_async_copy(
            long_out.at[me, part(q), :], returned.at[me, part(q), :], own_sem.at[q]
        )

    def rim(which, q):
        src, dst = ((mixed, halo_mixed), (first, halo_first))[which]
        return pltpu.make_async_remote_copy(
            src_ref=src.at[:, part(q), last],
            dst_ref=dst.at[:, part(q), :],
            send_sem=rim_send.at[which, q],
            recv_sem=rim_recv.at[which, q],
            device_id={"ctx": lax.rem(me + 1, n)},
            device_id_type=MESH,
        )

    def there(k, q, arriving=False):
        peer = lax.rem(me + (n - k if arriving else k), n)
        slot = peer if arriving else me
        return pltpu.make_async_remote_copy(
            src_ref=second.at[peer, part(q), :],
            dst_ref=gathered.at[slot, part(q), :],
            send_sem=there_send.at[k, q],
            recv_sem=there_recv.at[k, q],
            device_id={"ctx": peer},
            device_id_type=MESH,
        )

    def home(k, q, arriving=False):
        peer = lax.rem(me + (n - k if arriving else k), n)
        slot = peer if arriving else me
        return pltpu.make_async_remote_copy(
            src_ref=long_out.at[peer, part(q), :],
            dst_ref=returned.at[slot, part(q), :],
            send_sem=home_send.at[k, q],
            recv_sem=home_recv.at[k, q],
            device_id={"ctx": peer},
            device_id_type=MESH,
        )

    def rows_at(q, j):
        return pl.ds(pl.multiple_of(q * chunk + j * ROWS, ROWS), ROWS)

    def lanes(b):
        return slice(b * LANES, (b + 1) * LANES)

    taps_first[...] = filter_first_ref[...].astype(jnp.float32)
    taps_second[...] = filter_second_ref[...].astype(jnp.float32)
    eye = lax.broadcasted_iota(jnp.int32, (LANES, LANES), 0) == lax.broadcasted_iota(
        jnp.int32, (LANES, LANES), 1
    )
    for i in range(per // LANES):
        line = skip_ref[pl.ds(me * (per // LANES) + i, 1), :]
        column = jnp.sum(jnp.where(eye, line, 0.0), axis=1, keepdims=True)
        skip_wide[i * LANES : (i + 1) * LANES, :] = jnp.broadcast_to(column, (LANES, LANES))

    pl.semaphore_wait(barrier, n - 1)

    @pl.when(me == 0)
    def _():
        halo_mixed[...] = jnp.zeros_like(halo_mixed)
        halo_first[...] = jnp.zeros_like(halo_first)

    def early(q):
        loaded(0, q).wait()
        loaded(1, q).wait()

        for d in range(n):
            mixed[d, part(q), :] = (
                key_ref[d, part(q), :].astype(jnp.float32)
                * value_ref[d, part(q), :].astype(jnp.float32)
            ).astype(jnp.bfloat16)

        @pl.when(me < n - 1)
        def _():
            rim(0, q).start()

        loaded(2, q).wait()

        for d in range(n):
            for j in range(groups):
                g = d * (per // ROWS) + q * groups + j
                w = band(taps_first[pl.ds(g, 1), :])
                band_first[g] = w
                band_second[g] = band(taps_second[pl.ds(g, 1), :])
                rows = rows_at(q, j)
                windows = jnp.concatenate(
                    [mixed[d, rows, b * LANES - LANES : (b + 1) * LANES] for b in range(1, blocks)],
                    axis=0,
                )
                result = jnp.dot(windows, w, preferred_element_type=jnp.float32)
                for b in range(1, blocks):
                    first[d, rows, lanes(b)] = gated(
                        gate_first_ref[d, rows, lanes(b)], result[(b - 1) * ROWS : b * ROWS]
                    )

        @pl.when(me < n - 1)
        def _():
            rim(1, q).start()

    def late(q):
        loaded(3, q).wait()

        @pl.when(me > 0)
        def _():
            rim(0, q).wait_recv()
            rim(1, q).wait_recv()

        for d in range(n):
            for j in range(groups):
                g = d * (per // ROWS) + q * groups + j
                rows = rows_at(q, j)
                head = jnp.concatenate([halo_mixed[d, rows, :], mixed[d, rows, lanes(0)]], axis=1)
                head = jnp.dot(head, band_first[g], preferred_element_type=jnp.float32)
                first[d, rows, lanes(0)] = gated(gate_first_ref[d, rows, lanes(0)], head)

        for k in [*range(2, n), 1, 0]:
            d = lax.rem(me + k, n)
            target = second if k else gathered
            for j in range(groups):
                g = d * (per // ROWS) + q * groups + j
                rows = rows_at(q, j)
                ahead = jnp.concatenate([halo_first[d, rows, :], first[d, rows, lanes(0)]], axis=1)
                windows = [ahead] + [
                    first[d, rows, b * LANES - LANES : (b + 1) * LANES] for b in range(1, blocks)
                ]
                result = jnp.dot(
                    jnp.concatenate(windows, axis=0),
                    band_second[g],
                    preferred_element_type=jnp.float32,
                )
                for b in range(blocks):
                    target[d, rows, lanes(b)] = gated(
                        gate_second[d, rows, lanes(b)], result[b * ROWS : (b + 1) * ROWS]
                    )
            if k:
                there(k, q).start()

    early(0)

    def both(q, _):
        early(q + 1)
        late(q)
        return 0

    lax.fori_loop(0, chunks - 1, both, 0)
    late(chunks - 1)

    def spread(values, at):
        bins = padded_bins(values)
        for r in range(bin_count):
            re, im = bins[r]
            im = jnp.zeros_like(re) if im is None else im
            bins_in[r, at, :] = jnp.concatenate([re, im], axis=1).astype(jnp.bfloat16)

    loads[0].wait()
    loads[1].wait()

    def filter_rows(j, _):
        at = pl.ds(pl.multiple_of(j * ROWS, ROWS), ROWS)
        spread([long_filter[at, lanes(a)].astype(jnp.float32) for a in range(total_blocks)], at)
        return 0

    lax.fori_loop(0, per // ROWS, filter_rows, 0)

    for r in range(bin_count):
        spectrum[r] = jnp.dot(bins_in[r], forward[r], preferred_element_type=jnp.float32)
    loads[2].wait()

    span = bins_out.shape[1]
    pieces = span // chunk

    def convolve(w, _):
        for c in range(pieces):
            for k in range(1, n):
                there(k, w * pieces + c, True).wait_recv()

        def signal(rows):
            return [
                gathered[a // blocks, rows, lanes(a % blocks)].astype(jnp.float32)
                for a in range(total_blocks)
            ]

        def rows_in(j, _):
            at = pl.ds(pl.multiple_of(j * ROWS, ROWS), ROWS)
            spread(signal(rows_at(w * pieces, j)), at)
            return 0

        lax.fori_loop(0, span // ROWS, rows_in, 0)
        here = pl.ds(pl.multiple_of(w * span, span), span)

        for r in range(bin_count):
            sig = jnp.dot(bins_in[r, 0:span, :], forward[r], preferred_element_type=jnp.float32)
            filt = spectrum[r, here, :]
            sig_re, sig_im = sig[:, :LANES], sig[:, LANES:]
            filt_re, filt_im = filt[:, :LANES], filt[:, LANES:]
            products[r] = jnp.concatenate(
                [sig_re * filt_re - sig_im * filt_im, sig_re * filt_im + sig_im * filt_re], axis=1
            ).astype(jnp.bfloat16)

        for r in range(bin_count):
            bins_out[r] = jnp.dot(products[r], backward[r], preferred_element_type=jnp.float32)

        for c in range(pieces):
            q = w * pieces + c

            def rows_out(j, _):
                at = pl.ds(pl.multiple_of(c * chunk + j * ROWS, ROWS), ROWS)
                rows = rows_at(q, j)
                bins = {
                    r: (bins_out[r, at, :LANES], bins_out[r, at, LANES:]) for r in range(bin_count)
                }
                result = padded_back(bins, total_blocks)
                skip = skip_wide[rows, :]
                for a, value in enumerate(signal(rows)):
                    long_out[a // blocks, rows, lanes(a % blocks)] = (
                        skip * value + result[a]
                    ).astype(jnp.bfloat16)
                return 0

            lax.fori_loop(0, groups, rows_out, 0)
            for k in [*range(2, n), 1]:
                home(k, q).start()
            own(q).start()
        return 0

    lax.fori_loop(0, per // span, convolve, 0)

    def drain(q, _):
        @pl.when(me < n - 1)
        def _():
            rim(0, q).wait_send()
            rim(1, q).wait_send()

        own(q).wait()
        for k in range(1, n):
            there(k, q).wait_send()
            home(k, q).wait_send()
            home(k, q, True).wait_recv()
        return 0

    lax.fori_loop(0, chunks, drain, 0)


def fits_kernel(channels, length, n, tap_count):
    per = channels // n
    total = n * length
    return (
        tap_count == LANES
        and length % LANES == 0
        and length >= 2 * LANES
        and per % LANES == 0
        and n > 1
        and total & (total - 1) == 0
        and total <= 2048
        and channels * total <= 1024 * 2048
    )


def shards(
    value_in,
    key_in,
    gate_first,
    gate_second,
    gate_long,
    filter_first,
    filter_second,
    long_filter,
    skip_gain,
):
    channels, length = value_in.shape
    n = lax.axis_size("ctx")
    if not fits_kernel(channels, length, n, filter_first.shape[1]):
        return shards_general(
            value_in,
            key_in,
            gate_first,
            gate_second,
            gate_long,
            filter_first,
            filter_second,
            long_filter,
            skip_gain,
        )
    per = channels // n
    total = n * length
    chunk = 64
    span = 2 * chunk
    chunks = per // chunk
    group_count = filter_first.shape[0]
    bin_count = total // LANES + 1
    cut = lambda a: a.reshape(n, per, length)
    forward, back = inner_tables(total)
    bf16, f32 = jnp.bfloat16, jnp.float32
    vmem = pl.BlockSpec(memory_space=pltpu.VMEM)
    anywhere = pl.BlockSpec(memory_space=pl.ANY)
    in_hbm = pl.BlockSpec(memory_space=pltpu.HBM)
    dma = pltpu.SemaphoreType.DMA
    out = pl.pallas_call(
        functools.partial(whole_kernel, n, chunk),
        out_shape=jax.ShapeDtypeStruct((n, per, length), bf16),
        in_specs=[vmem] * 3 + [in_hbm] * 7,
        out_specs=anywhere,
        scratch_shapes=[
            pltpu.VMEM((n, per, length), bf16),
            pltpu.VMEM((n, per, length), bf16),
            pltpu.VMEM((n, per, length), bf16),
            pltpu.VMEM((n, per, length), bf16),
            pltpu.VMEM((per, total), bf16),
            pltpu.VMEM(forward.shape, bf16),
            pltpu.VMEM(back.shape, bf16),
            pltpu.VMEM(filter_first.shape, f32),
            pltpu.VMEM(filter_second.shape, f32),
            pltpu.VMEM((group_count, 2 * LANES, LANES), bf16),
            pltpu.VMEM((group_count, 2 * LANES, LANES), bf16),
            pltpu.VMEM((n, per, length), bf16),
            pltpu.VMEM((n, per, length), bf16),
            pltpu.VMEM((n, per, LANES), bf16),
            pltpu.VMEM((n, per, LANES), bf16),
            pltpu.VMEM((n, per, length), bf16),
            pltpu.VMEM((n, per, length), bf16),
            pltpu.VMEM((n, per, length), bf16),
            pltpu.VMEM((per, LANES), f32),
            pltpu.VMEM((bin_count, per, 2 * LANES), bf16),
            pltpu.VMEM((bin_count, per, 2 * LANES), f32),
            pltpu.VMEM((bin_count, span, 2 * LANES), bf16),
            pltpu.VMEM((bin_count, span, 2 * LANES), f32),
            dma((3,)),
            dma((4, chunks)),
            dma((chunks,)),
            dma((2, chunks)),
            dma((2, chunks)),
            dma((n, chunks)),
            dma((n, chunks)),
            dma((n, chunks)),
            dma((n, chunks)),
        ],
        compiler_params=pltpu.CompilerParams(
            collective_id=0, has_side_effects=True, vmem_limit_bytes=56 * 1024 * 1024
        ),
        cost_estimate=pl.CostEstimate(
            flops=8 * channels * length * 2 * LANES + 6 * 2 * per * total * 2 * LANES * 2,
            bytes_accessed=8 * channels * length * 2,
            transcendentals=0,
        ),
    )(
        filter_first,
        filter_second,
        skip_gain.reshape(channels // LANES, LANES),
        cut(value_in),
        cut(key_in),
        cut(gate_first),
        cut(gate_second),
        long_filter,
        jnp.asarray(forward),
        jnp.asarray(back),
    )
    return gated(gate_long, out.reshape(channels, length).astype(f32))


def solution(mesh):
    placed = (
        P("ch", "ctx"),
        P("ch", "ctx"),
        P("ch", "ctx"),
        P("ch", "ctx"),
        P("ch", "ctx"),
        P("ch", None),
        P("ch", None),
        P(("ch", "ctx"), None),
        P("ch"),
    )
    return jax.shard_map(
        shards, mesh=mesh, in_specs=placed, out_specs=P("ch", "ctx"), check_vma=False
    )
```

```python
import cmath
import functools
import math

import jax
import jax.numpy as jnp
import ml_dtypes
import numpy as np
from jax import lax
from jax.experimental import pallas as pl
from jax.experimental.pallas import tpu as pltpu
from jax.sharding import PartitionSpec as P

HIGH = lax.Precision.HIGH
LANES = 128
ROWS = 16
MESH = pl.DeviceIdType.MESH


def from_behind(shard, axis, by):
    devices = lax.axis_size(axis)
    pairs = [(i, i + by) for i in range(devices) if 0 <= i + by < devices]
    return lax.ppermute(shard, axis, pairs)


def band_matrix(filters, tap_count):
    group_count = filters.shape[0]
    zero_one = jnp.zeros((group_count, 1), filters.dtype)
    zero_rest = jnp.zeros((group_count, tap_count), filters.dtype)
    pattern = jnp.concatenate([zero_one, jnp.flip(filters, axis=1), zero_rest], axis=1)
    tiled = jnp.tile(pattern, (1, tap_count))
    return tiled[:, : tap_count * 2 * tap_count].reshape(group_count, tap_count, 2 * tap_count)


def toeplitz_conv(extended, filters, tap_count):
    channels, total_len = extended.shape
    length = total_len - tap_count
    block_count = length // tap_count
    front_half = extended[:, :length].reshape(channels, block_count, tap_count)
    back_half = extended[:, tap_count:].reshape(channels, block_count, tap_count)
    windows = jnp.concatenate([front_half, back_half], axis=2)
    group_count = filters.shape[0]
    windows = windows.reshape(group_count, channels // group_count, block_count, 2 * tap_count)
    toeplitz = band_matrix(filters, tap_count)
    result = jnp.einsum("gts,gcbs->gcbt", toeplitz, windows, preferred_element_type=jnp.float32)
    return result.reshape(channels, length)


def previous_rim(tail):
    return from_behind(tail, "ctx", 1)


def to_channels(data):
    return lax.all_to_all(data, "ctx", split_axis=0, concat_axis=1, tiled=True)


def first_section(mixed_in, gate_first, filter_first, tap_count):
    length = mixed_in.shape[1]
    extended = jnp.concatenate([previous_rim(mixed_in[:, length - tap_count :]), mixed_in], axis=1)
    return (
        gate_first.astype(jnp.float32) * toeplitz_conv(extended, filter_first, tap_count)
    ).astype(jnp.bfloat16)


def dft_tables(size):
    index = jnp.arange(size, dtype=jnp.int32)
    angle = (index[:, None] * index[None, :] % size).astype(jnp.float32) * (-2.0 * math.pi / size)
    return (jnp.cos(angle), jnp.sin(angle))


def split_factor(padded_len):
    outer = 2
    cand = 2
    while cand * cand <= padded_len:
        if padded_len % cand == 0:
            outer = cand
        cand = cand + 2
    return outer


def long_convolution(signal, filt_vals, skip_part):
    channels, length = signal.shape
    padded_len = 2 * length
    rows_outer = split_factor(padded_len)
    rows_inner = padded_len // rows_outer
    half_rows = rows_outer // 2
    outer_cos, outer_sin = dft_tables(rows_outer)
    inner_cos, inner_sin = dft_tables(rows_inner)
    k_index = jnp.arange(rows_outer, dtype=jnp.int32)[:, None]
    n_index = jnp.arange(rows_inner, dtype=jnp.int32)[None, :]
    twid_angle = (k_index * n_index % padded_len).astype(jnp.float32) * (
        -2.0 * math.pi / padded_len
    )
    twid_cos = jnp.cos(twid_angle)
    twid_sin = jnp.sin(twid_angle)
    outer_table = jnp.concatenate([outer_cos[:, :half_rows], outer_sin[:, :half_rows]], axis=0)
    inner_fwd = jnp.concatenate(
        [
            jnp.concatenate([inner_cos, inner_sin], axis=1),
            jnp.concatenate([-inner_sin, inner_cos], axis=1),
        ],
        axis=0,
    )
    inner_back = jnp.concatenate(
        [
            jnp.concatenate([inner_cos, -inner_sin], axis=1),
            jnp.concatenate([inner_sin, inner_cos], axis=1),
        ],
        axis=0,
    )

    def forward(values):
        grid = values.reshape(channels, half_rows, rows_inner)
        parts = jnp.einsum("kn,cnm->ckm", outer_table, grid, precision=HIGH)
        part_re = parts[:, :rows_outer]
        part_im = parts[:, rows_outer:]
        turned_re = part_re * twid_cos - part_im * twid_sin
        turned_im = part_re * twid_sin + part_im * twid_cos
        turned = jnp.concatenate([turned_re, turned_im], axis=2)
        spectrum = jnp.einsum("ckn,nm->ckm", turned, inner_fwd, precision=HIGH)
        return (spectrum[:, :, :rows_inner], spectrum[:, :, rows_inner:])

    sig_re, sig_im = forward(signal)
    filt_re, filt_im = forward(filt_vals)
    prod_re = sig_re * filt_re - sig_im * filt_im
    prod_im = sig_re * filt_im + sig_im * filt_re
    stacked = jnp.concatenate([prod_re, prod_im], axis=2)
    back = jnp.einsum("ckm,mn->ckn", stacked, inner_back, precision=HIGH)
    back_re = back[:, :, :rows_inner]
    back_im = back[:, :, rows_inner:]
    reverted_re = back_re * twid_cos + back_im * twid_sin
    reverted_im = back_im * twid_cos - back_re * twid_sin
    reverted = jnp.concatenate([reverted_re, reverted_im], axis=1)
    result = jnp.einsum("kn,ckm->cnm", outer_table, reverted, precision=HIGH)
    result = result.reshape(channels, length) / padded_len
    return skip_part[:, None] * signal + result


def shards_general(
    value_in,
    key_in,
    gate_first,
    gate_second,
    gate_long,
    filter_first,
    filter_second,
    long_filter,
    skip_gain,
):
    tap_count = filter_first.shape[1]
    channels, length = value_in.shape
    per_device = channels // lax.axis_size("ctx")
    channel_base = lax.axis_index("ctx") * per_device
    mixed_in = (key_in.astype(jnp.float32) * value_in.astype(jnp.float32)).astype(jnp.bfloat16)
    first_out = first_section(mixed_in, gate_first, filter_first, tap_count)
    prior_first = from_behind(first_out[:, length - tap_count :], "ctx", 1)
    first_wide = jnp.concatenate([prior_first, first_out], axis=1)
    second_out = (
        gate_second.astype(jnp.float32) * toeplitz_conv(first_wide, filter_second, tap_count)
    ).astype(jnp.bfloat16)
    moved = to_channels(second_out)
    skip_here = lax.dynamic_slice_in_dim(skip_gain, channel_base, per_device, 0)
    filt_vals = long_filter.astype(jnp.float32)
    long_out = long_convolution(moved.astype(jnp.float32), filt_vals, skip_here).astype(
        jnp.bfloat16
    )
    back_home = lax.all_to_all(long_out, "ctx", split_axis=1, concat_axis=0, tiled=True)
    return (gate_long.astype(jnp.float32) * back_home.astype(jnp.float32)).astype(jnp.bfloat16)


def unit(numerator, denominator):
    return cmath.exp(-2j * math.pi * numerator / denominator)


def turn(value, factor):
    re, im = value
    if abs(factor - 1) < 1e-12:
        return value
    if abs(factor + 1j) < 1e-12:
        return (im, -re)
    if abs(factor - 1j) < 1e-12:
        return (-im, re)
    if abs(abs(factor.real) - abs(factor.imag)) < 1e-12:
        size = abs(factor.real)
        re, im = re * size, im * size
        if factor.real > 0 and factor.imag < 0:
            return (re + im, im - re)
        if factor.real < 0 and factor.imag < 0:
            return (im - re, -re - im)
        if factor.real > 0:
            return (re - im, re + im)
        return (-re - im, re - im)
    return (re * factor.real - im * factor.imag, re * factor.imag + im * factor.real)


def complex_dft(values, sign):
    count = len(values)
    if count == 1:
        return values
    half = count // 2
    low, high = [], []
    for a in range(half):
        (p_re, p_im), (q_re, q_im) = values[a], values[a + half]
        low.append((p_re + q_re, p_im + q_im))
        factor = unit(a, count)
        high.append(turn((p_re - q_re, p_im - q_im), factor if sign > 0 else factor.conjugate()))
    result = [None] * count
    result[0::2] = complex_dft(low, sign)
    result[1::2] = complex_dft(high, sign)
    return result


def odd_bins(values):
    count = len(values)
    if count == 1:
        return {1: (values[0], None)}
    half = count // 2
    folded = [turn((values[a], -values[a + half]), unit(a, 2 * count)) for a in range(half)]
    bins = {}
    for place, (re, im) in enumerate(complex_dft(folded, 1)):
        r = 4 * place + 1
        if r < count:
            bins[r] = (re, im)
        else:
            bins[2 * count - r] = (re, -im)
    return bins


def real_bins(values):
    count = len(values)
    if count == 1:
        return {0: (values[0], None)}
    half = count // 2
    even = real_bins([values[a] + values[a + half] for a in range(half)])
    odd = odd_bins([values[a] - values[a + half] for a in range(half)])
    bins = {2 * r: v for r, v in even.items()}
    bins.update(odd)
    return bins


def padded_bins(values):
    bins = {2 * r: v for r, v in real_bins(values).items()}
    bins.update(odd_bins(values))
    return bins


def odd_back(bins, count):
    if count == 1:
        return [bins[1][0]]
    half = count // 2
    folded = []
    for place in range(half):
        r = 4 * place + 1
        if r < count:
            folded.append(bins[r])
        else:
            re, im = bins[2 * count - r]
            folded.append((re, -im))
    spread = complex_dft(folded, -1)
    spread = [turn(spread[a], unit(a, 2 * count).conjugate()) for a in range(half)]
    return [v[0] for v in spread] + [-v[1] for v in spread]


def real_back(bins, count):
    if count == 1:
        return [bins[0][0]]
    half = count // 2
    even = real_back({r // 2: v for r, v in bins.items() if r % 2 == 0}, half)
    odd = odd_back({r: v for r, v in bins.items() if r % 2 == 1}, half)
    return [even[a] + odd[a] for a in range(half)] + [even[a] - odd[a] for a in range(half)]


def padded_back(bins, count):
    even = real_back({r // 2: v for r, v in bins.items() if r % 2 == 0}, count)
    odd = odd_back({r: v for r, v in bins.items() if r % 2 == 1}, count)
    return [even[a] + odd[a] for a in range(count)]


def inner_tables(length):
    padded_len = 2 * length
    outer = padded_len // LANES
    b = np.arange(LANES)[:, None]
    q = np.arange(LANES)[None, :]
    forward, back = [], []
    for r in range(outer // 2 + 1):
        angle = (b * (r + outer * q) % padded_len) * (-2.0 * math.pi / padded_len)
        c, s = np.cos(angle), np.sin(angle)
        table = np.block([[c, s], [-s, c]])
        weight = (1.0 if r in (0, outer // 2) else 2.0) / padded_len
        forward.append(table)
        back.append(table.T * weight)
    return (
        np.stack(forward).astype(ml_dtypes.bfloat16),
        np.stack(back).astype(ml_dtypes.bfloat16),
    )


def band(row):
    rolled = pltpu.roll(jnp.broadcast_to(row, (LANES, LANES)), 0, 1, stride=1, stride_axis=0)
    s = lax.broadcasted_iota(jnp.int32, (LANES, LANES), 0)
    t = lax.broadcasted_iota(jnp.int32, (LANES, LANES), 1)
    zero = jnp.zeros((LANES, LANES), jnp.float32)
    return jnp.concatenate(
        [jnp.where(t < s, rolled, zero), jnp.where(t >= s, rolled, zero)], axis=0
    ).astype(jnp.bfloat16)


def gated(gate, value):
    return (gate.astype(jnp.float32) * value).astype(jnp.bfloat16)


def whole_kernel(
    n,
    chunk,
    filter_first_ref,
    filter_second_ref,
    skip_ref,
    value_hbm,
    key_hbm,
    gate_first_hbm,
    gate_second_hbm,
    long_filter_hbm,
    forward_hbm,
    back_hbm,
    returned,
    value_ref,
    key_ref,
    gate_first_ref,
    gate_second,
    long_filter,
    forward,
    backward,
    taps_first,
    taps_second,
    band_first,
    band_second,
    mixed,
    first,
    halo_mixed,
    halo_first,
    second,
    gathered,
    long_out,
    skip_wide,
    bins_in,
    spectrum,
    products,
    bins_out,
    load_sem,
    part_sem,
    own_sem,
    rim_send,
    rim_recv,
    there_send,
    there_recv,
    home_send,
    home_recv,
):
    _, per, length = value_hbm.shape
    me = lax.axis_index("ctx")
    blocks = length // LANES
    chunks = per // chunk
    groups = chunk // ROWS
    total_blocks = n * blocks
    bin_count = total_blocks + 1
    last = slice(length - LANES, length)

    barrier = pltpu.get_barrier_semaphore()
    for k in range(1, n):
        pl.semaphore_signal(
            barrier, inc=1, device_id={"ctx": lax.rem(me + k, n)}, device_id_type=MESH
        )

    def part(q):
        return pl.ds(pl.multiple_of(q * chunk, chunk), chunk)

    def loaded(i, q):
        src, dst = (
            (key_hbm, key_ref),
            (value_hbm, value_ref),
            (gate_first_hbm, gate_first_ref),
            (gate_second_hbm, gate_second),
        )[i]
        return pltpu.make_async_copy(
            src.at[:, part(q), :], dst.at[:, part(q), :], part_sem.at[i, q]
        )

    for q in range(chunks):
        for i in range(4):
            loaded(i, q).start()
    loads = [
        pltpu.make_async_copy(src, dst, load_sem.at[i])
        for i, (src, dst) in enumerate(
            [(long_filter_hbm, long_filter), (forward_hbm, forward), (back_hbm, backward)]
        )
    ]
    for load in loads:
        load.start()

    def own(q):
        return pltpu.make_async_copy(
            long_out.at[me, part(q), :], returned.at[me, part(q), :], own_sem.at[q]
        )

    def rim(which, q):
        src, dst = ((mixed, halo_mixed), (first, halo_first))[which]
        return pltpu.make_async_remote_copy(
            src_ref=src.at[:, part(q), last],
            dst_ref=dst.at[:, part(q), :],
            send_sem=rim_send.at[which, q],
            recv_sem=rim_recv.at[which, q],
            device_id={"ctx": lax.rem(me + 1, n)},
            device_id_type=MESH,
        )

    def there(half, k, q, arriving=False):
        peer = lax.rem(me + (n - k if arriving else k), n)
        slot = peer if arriving else me
        columns = slice(0, 2 * LANES) if half else slice(2 * LANES, length)
        return pltpu.make_async_remote_copy(
            src_ref=second.at[peer, part(q), columns],
            dst_ref=gathered.at[slot, part(q), columns],
            send_sem=there_send.at[half, k, q],
            recv_sem=there_recv.at[half, k, q],
            device_id={"ctx": peer},
            device_id_type=MESH,
        )

    def home(k, q, arriving=False):
        peer = lax.rem(me + (n - k if arriving else k), n)
        slot = peer if arriving else me
        return pltpu.make_async_remote_copy(
            src_ref=long_out.at[peer, part(q), :],
            dst_ref=returned.at[slot, part(q), :],
            send_sem=home_send.at[k, q],
            recv_sem=home_recv.at[k, q],
            device_id={"ctx": peer},
            device_id_type=MESH,
        )

    def rows_at(q, j):
        return pl.ds(pl.multiple_of(q * chunk + j * ROWS, ROWS), ROWS)

    def lanes(b):
        return slice(b * LANES, (b + 1) * LANES)

    taps_first[...] = filter_first_ref[...].astype(jnp.float32)
    taps_second[...] = filter_second_ref[...].astype(jnp.float32)
    eye = lax.broadcasted_iota(jnp.int32, (LANES, LANES), 0) == lax.broadcasted_iota(
        jnp.int32, (LANES, LANES), 1
    )
    for i in range(per // LANES):
        line = skip_ref[pl.ds(me * (per // LANES) + i, 1), :]
        column = jnp.sum(jnp.where(eye, line, 0.0), axis=1, keepdims=True)
        skip_wide[i * LANES : (i + 1) * LANES, :] = jnp.broadcast_to(column, (LANES, LANES))

    pl.semaphore_wait(barrier, n - 1)

    @pl.when(me == 0)
    def _():
        halo_mixed[...] = jnp.zeros_like(halo_mixed)
        halo_first[...] = jnp.zeros_like(halo_first)

    def early(q):
        loaded(0, q).wait()
        loaded(1, q).wait()

        for d in range(n):
            mixed[d, part(q), :] = (
                key_ref[d, part(q), :].astype(jnp.float32)
                * value_ref[d, part(q), :].astype(jnp.float32)
            ).astype(jnp.bfloat16)

        @pl.when(me < n - 1)
        def _():
            rim(0, q).start()

        loaded(2, q).wait()

        for d in range(n):
            for j in range(groups):
                g = d * (per // ROWS) + q * groups + j
                w = band(taps_first[pl.ds(g, 1), :])
                band_first[g] = w
                rows = rows_at(q, j)
                result = jnp.dot(
                    mixed[d, rows, length - 2 * LANES : length],
                    w,
                    preferred_element_type=jnp.float32,
                )
                first[d, rows, last] = gated(gate_first_ref[d, rows, last], result)

        @pl.when(me < n - 1)
        def _():
            rim(1, q).start()

    def first_blocks(q, targets):
        for d in range(n):
            for j in range(groups):
                rows = rows_at(q, j)
                windows = [mixed[d, rows, b * LANES - LANES : (b + 1) * LANES] for b in targets]
                result = jnp.dot(
                    jnp.concatenate(windows, axis=0),
                    band_first[d * (per // ROWS) + q * groups + j],
                    preferred_element_type=jnp.float32,
                )
                for i, b in enumerate(targets):
                    first[d, rows, lanes(b)] = gated(
                        gate_first_ref[d, rows, lanes(b)], result[i * ROWS : (i + 1) * ROWS]
                    )

    def second_blocks(q, half, targets):
        for k in [*range(2, n), 1, 0]:
            d = lax.rem(me + k, n)
            target = second if k else gathered
            for j in range(groups):
                g = d * (per // ROWS) + q * groups + j
                rows = rows_at(q, j)
                if half == 0:
                    w = band(taps_second[pl.ds(g, 1), :])
                    band_second[g] = w
                else:
                    w = band_second[g]
                windows = [
                    jnp.concatenate([halo_first[d, rows, :], first[d, rows, lanes(0)]], axis=1)
                    if b == 0
                    else first[d, rows, b * LANES - LANES : (b + 1) * LANES]
                    for b in targets
                ]
                result = jnp.dot(
                    jnp.concatenate(windows, axis=0), w, preferred_element_type=jnp.float32
                )
                for i, b in enumerate(targets):
                    target[d, rows, lanes(b)] = gated(
                        gate_second[d, rows, lanes(b)], result[i * ROWS : (i + 1) * ROWS]
                    )
            if k:
                there(half, k, q).start()

    def middle(q, _):
        first_blocks(q, range(1, blocks - 1))
        loaded(3, q).wait()
        second_blocks(q, 0, range(2, blocks))
        return 0

    def late(q, _):
        @pl.when(me > 0)
        def _():
            rim(0, q).wait_recv()
            rim(1, q).wait_recv()

        for d in range(n):
            for j in range(groups):
                g = d * (per // ROWS) + q * groups + j
                rows = rows_at(q, j)
                head = jnp.concatenate([halo_mixed[d, rows, :], mixed[d, rows, lanes(0)]], axis=1)
                head = jnp.dot(head, band_first[g], preferred_element_type=jnp.float32)
                first[d, rows, lanes(0)] = gated(gate_first_ref[d, rows, lanes(0)], head)

        second_blocks(q, 1, range(2))
        return 0

    def start(q, _):
        early(q)
        return 0

    lax.fori_loop(0, chunks, start, 0)
    lax.fori_loop(0, chunks, middle, 0)
    lax.fori_loop(0, chunks, late, 0)

    def spread(values, at):
        bins = padded_bins(values)
        for r in range(bin_count):
            re, im = bins[r]
            im = jnp.zeros_like(re) if im is None else im
            bins_in[r, at, :] = jnp.concatenate([re, im], axis=1).astype(jnp.bfloat16)

    loads[0].wait()
    loads[1].wait()

    def filter_rows(j, _):
        at = pl.ds(pl.multiple_of(j * ROWS, ROWS), ROWS)
        spread([long_filter[at, lanes(a)].astype(jnp.float32) for a in range(total_blocks)], at)
        return 0

    lax.fori_loop(0, per // ROWS, filter_rows, 0)

    for r in range(bin_count):
        spectrum[r] = jnp.dot(bins_in[r], forward[r], preferred_element_type=jnp.float32)
    loads[2].wait()

    span = bins_out.shape[1]
    pieces = span // chunk

    def convolve(w, _):
        for c in range(pieces):
            for k in range(1, n):
                there(0, k, w * pieces + c, True).wait_recv()
                there(1, k, w * pieces + c, True).wait_recv()

        def signal(rows):
            return [
                gathered[a // blocks, rows, lanes(a % blocks)].astype(jnp.float32)
                for a in range(total_blocks)
            ]

        def rows_in(j, _):
            at = pl.ds(pl.multiple_of(j * ROWS, ROWS), ROWS)
            spread(signal(rows_at(w * pieces, j)), at)
            return 0

        lax.fori_loop(0, span // ROWS, rows_in, 0)
        here = pl.ds(pl.multiple_of(w * span, span), span)

        for r in range(bin_count):
            sig = jnp.dot(bins_in[r, 0:span, :], forward[r], preferred_element_type=jnp.float32)
            filt = spectrum[r, here, :]
            sig_re, sig_im = sig[:, :LANES], sig[:, LANES:]
            filt_re, filt_im = filt[:, :LANES], filt[:, LANES:]
            products[r] = jnp.concatenate(
                [sig_re * filt_re - sig_im * filt_im, sig_re * filt_im + sig_im * filt_re], axis=1
            ).astype(jnp.bfloat16)

        for r in range(bin_count):
            bins_out[r] = jnp.dot(products[r], backward[r], preferred_element_type=jnp.float32)

        for c in range(pieces):
            q = w * pieces + c

            def rows_out(j, _):
                at = pl.ds(pl.multiple_of(c * chunk + j * ROWS, ROWS), ROWS)
                rows = rows_at(q, j)
                bins = {
                    r: (bins_out[r, at, :LANES], bins_out[r, at, LANES:]) for r in range(bin_count)
                }
                result = padded_back(bins, total_blocks)
                skip = skip_wide[rows, :]
                for a, value in enumerate(signal(rows)):
                    long_out[a // blocks, rows, lanes(a % blocks)] = (
                        skip * value + result[a]
                    ).astype(jnp.bfloat16)
                return 0

            lax.fori_loop(0, groups, rows_out, 0)
            for k in [*range(2, n), 1]:
                home(k, q).start()
            own(q).start()
        return 0

    lax.fori_loop(0, per // span, convolve, 0)

    def drain(q, _):
        @pl.when(me < n - 1)
        def _():
            rim(0, q).wait_send()
            rim(1, q).wait_send()

        own(q).wait()
        for k in range(1, n):
            there(0, k, q).wait_send()
            there(1, k, q).wait_send()
            home(k, q).wait_send()
            home(k, q, True).wait_recv()
        return 0

    lax.fori_loop(0, chunks, drain, 0)


def gate_kernel(gate_ref, value_ref, out_ref):
    out_ref[...] = gated(gate_ref[...], value_ref[...].astype(jnp.float32))


def fits_kernel(channels, length, n, tap_count):
    per = channels // n
    total = n * length
    return (
        tap_count == LANES
        and length % LANES == 0
        and length >= 3 * LANES
        and per % LANES == 0
        and n > 1
        and total & (total - 1) == 0
        and total <= 2048
        and channels * total <= 1024 * 2048
    )


def shards(
    value_in,
    key_in,
    gate_first,
    gate_second,
    gate_long,
    filter_first,
    filter_second,
    long_filter,
    skip_gain,
):
    channels, length = value_in.shape
    n = lax.axis_size("ctx")
    if not fits_kernel(channels, length, n, filter_first.shape[1]):
        return shards_general(
            value_in,
            key_in,
            gate_first,
            gate_second,
            gate_long,
            filter_first,
            filter_second,
            long_filter,
            skip_gain,
        )
    per = channels // n
    total = n * length
    chunk = 64
    span = 2 * chunk
    chunks = per // chunk
    group_count = filter_first.shape[0]
    bin_count = total // LANES + 1
    cut = lambda a: a.reshape(n, per, length)
    forward, back = inner_tables(total)
    bf16, f32 = jnp.bfloat16, jnp.float32
    vmem = pl.BlockSpec(memory_space=pltpu.VMEM)
    anywhere = pl.BlockSpec(memory_space=pl.ANY)
    in_hbm = pl.BlockSpec(memory_space=pltpu.HBM)
    dma = pltpu.SemaphoreType.DMA
    out = pl.pallas_call(
        functools.partial(whole_kernel, n, chunk),
        out_shape=jax.ShapeDtypeStruct((n, per, length), bf16),
        in_specs=[vmem] * 3 + [in_hbm] * 7,
        out_specs=anywhere,
        scratch_shapes=[
            pltpu.VMEM((n, per, length), bf16),
            pltpu.VMEM((n, per, length), bf16),
            pltpu.VMEM((n, per, length), bf16),
            pltpu.VMEM((n, per, length), bf16),
            pltpu.VMEM((per, total), bf16),
            pltpu.VMEM(forward.shape, bf16),
            pltpu.VMEM(back.shape, bf16),
            pltpu.VMEM(filter_first.shape, f32),
            pltpu.VMEM(filter_second.shape, f32),
            pltpu.VMEM((group_count, 2 * LANES, LANES), bf16),
            pltpu.VMEM((group_count, 2 * LANES, LANES), bf16),
            pltpu.VMEM((n, per, length), bf16),
            pltpu.VMEM((n, per, length), bf16),
            pltpu.VMEM((n, per, LANES), bf16),
            pltpu.VMEM((n, per, LANES), bf16),
            pltpu.VMEM((n, per, length), bf16),
            pltpu.VMEM((n, per, length), bf16),
            pltpu.VMEM((n, per, length), bf16),
            pltpu.VMEM((per, LANES), f32),
            pltpu.VMEM((bin_count, per, 2 * LANES), bf16),
            pltpu.VMEM((bin_count, per, 2 * LANES), f32),
            pltpu.VMEM((bin_count, span, 2 * LANES), bf16),
            pltpu.VMEM((bin_count, span, 2 * LANES), f32),
            dma((3,)),
            dma((4, chunks)),
            dma((chunks,)),
            dma((2, chunks)),
            dma((2, chunks)),
            dma((2, n, chunks)),
            dma((2, n, chunks)),
            dma((n, chunks)),
            dma((n, chunks)),
        ],
        compiler_params=pltpu.CompilerParams(
            collective_id=0, has_side_effects=True, vmem_limit_bytes=56 * 1024 * 1024
        ),
        cost_estimate=pl.CostEstimate(
            flops=8 * channels * length * 2 * LANES + 6 * 2 * per * total * 2 * LANES * 2,
            bytes_accessed=8 * channels * length * 2,
            transcendentals=0,
        ),
    )(
        filter_first,
        filter_second,
        skip_gain.reshape(channels // LANES, LANES),
        cut(value_in),
        cut(key_in),
        cut(gate_first),
        cut(gate_second),
        long_filter,
        jnp.asarray(forward),
        jnp.asarray(back),
    )
    block = pl.BlockSpec((per, length), lambda i: (i, 0))
    return pl.pallas_call(
        gate_kernel,
        out_shape=jax.ShapeDtypeStruct((channels, length), bf16),
        grid=(n,),
        in_specs=[block, block],
        out_specs=block,
    )(gate_long, out.reshape(channels, length))


def solution(mesh):
    placed = (
        P("ch", "ctx"),
        P("ch", "ctx"),
        P("ch", "ctx"),
        P("ch", "ctx"),
        P("ch", "ctx"),
        P("ch", None),
        P("ch", None),
        P(("ch", "ctx"), None),
        P("ch"),
    )
    return jax.shard_map(
        shards, mesh=mesh, in_specs=placed, out_specs=P("ch", "ctx"), check_vma=False
    )
```

```python
import cmath
import functools
import math

import jax
import jax.numpy as jnp
import ml_dtypes
import numpy as np
from jax import lax
from jax.experimental import pallas as pl
from jax.experimental.pallas import tpu as pltpu
from jax.sharding import PartitionSpec as P

HIGH = lax.Precision.HIGH
LANES = 128
ROWS = 16
MESH = pl.DeviceIdType.MESH


def from_behind(shard, axis, by):
    devices = lax.axis_size(axis)
    pairs = [(i, i + by) for i in range(devices) if 0 <= i + by < devices]
    return lax.ppermute(shard, axis, pairs)


def band_matrix(filters, tap_count):
    group_count = filters.shape[0]
    zero_one = jnp.zeros((group_count, 1), filters.dtype)
    zero_rest = jnp.zeros((group_count, tap_count), filters.dtype)
    pattern = jnp.concatenate([zero_one, jnp.flip(filters, axis=1), zero_rest], axis=1)
    tiled = jnp.tile(pattern, (1, tap_count))
    return tiled[:, : tap_count * 2 * tap_count].reshape(group_count, tap_count, 2 * tap_count)


def toeplitz_conv(extended, filters, tap_count):
    channels, total_len = extended.shape
    length = total_len - tap_count
    block_count = length // tap_count
    front_half = extended[:, :length].reshape(channels, block_count, tap_count)
    back_half = extended[:, tap_count:].reshape(channels, block_count, tap_count)
    windows = jnp.concatenate([front_half, back_half], axis=2)
    group_count = filters.shape[0]
    windows = windows.reshape(group_count, channels // group_count, block_count, 2 * tap_count)
    toeplitz = band_matrix(filters, tap_count)
    result = jnp.einsum("gts,gcbs->gcbt", toeplitz, windows, preferred_element_type=jnp.float32)
    return result.reshape(channels, length)


def previous_rim(tail):
    return from_behind(tail, "ctx", 1)


def to_channels(data):
    return lax.all_to_all(data, "ctx", split_axis=0, concat_axis=1, tiled=True)


def first_section(mixed_in, gate_first, filter_first, tap_count):
    length = mixed_in.shape[1]
    extended = jnp.concatenate([previous_rim(mixed_in[:, length - tap_count :]), mixed_in], axis=1)
    return (
        gate_first.astype(jnp.float32) * toeplitz_conv(extended, filter_first, tap_count)
    ).astype(jnp.bfloat16)


def dft_tables(size):
    index = jnp.arange(size, dtype=jnp.int32)
    angle = (index[:, None] * index[None, :] % size).astype(jnp.float32) * (-2.0 * math.pi / size)
    return (jnp.cos(angle), jnp.sin(angle))


def split_factor(padded_len):
    outer = 2
    cand = 2
    while cand * cand <= padded_len:
        if padded_len % cand == 0:
            outer = cand
        cand = cand + 2
    return outer


def long_convolution(signal, filt_vals, skip_part):
    channels, length = signal.shape
    padded_len = 2 * length
    rows_outer = split_factor(padded_len)
    rows_inner = padded_len // rows_outer
    half_rows = rows_outer // 2
    outer_cos, outer_sin = dft_tables(rows_outer)
    inner_cos, inner_sin = dft_tables(rows_inner)
    k_index = jnp.arange(rows_outer, dtype=jnp.int32)[:, None]
    n_index = jnp.arange(rows_inner, dtype=jnp.int32)[None, :]
    twid_angle = (k_index * n_index % padded_len).astype(jnp.float32) * (
        -2.0 * math.pi / padded_len
    )
    twid_cos = jnp.cos(twid_angle)
    twid_sin = jnp.sin(twid_angle)
    outer_table = jnp.concatenate([outer_cos[:, :half_rows], outer_sin[:, :half_rows]], axis=0)
    inner_fwd = jnp.concatenate(
        [
            jnp.concatenate([inner_cos, inner_sin], axis=1),
            jnp.concatenate([-inner_sin, inner_cos], axis=1),
        ],
        axis=0,
    )
    inner_back = jnp.concatenate(
        [
            jnp.concatenate([inner_cos, -inner_sin], axis=1),
            jnp.concatenate([inner_sin, inner_cos], axis=1),
        ],
        axis=0,
    )

    def forward(values):
        grid = values.reshape(channels, half_rows, rows_inner)
        parts = jnp.einsum("kn,cnm->ckm", outer_table, grid, precision=HIGH)
        part_re = parts[:, :rows_outer]
        part_im = parts[:, rows_outer:]
        turned_re = part_re * twid_cos - part_im * twid_sin
        turned_im = part_re * twid_sin + part_im * twid_cos
        turned = jnp.concatenate([turned_re, turned_im], axis=2)
        spectrum = jnp.einsum("ckn,nm->ckm", turned, inner_fwd, precision=HIGH)
        return (spectrum[:, :, :rows_inner], spectrum[:, :, rows_inner:])

    sig_re, sig_im = forward(signal)
    filt_re, filt_im = forward(filt_vals)
    prod_re = sig_re * filt_re - sig_im * filt_im
    prod_im = sig_re * filt_im + sig_im * filt_re
    stacked = jnp.concatenate([prod_re, prod_im], axis=2)
    back = jnp.einsum("ckm,mn->ckn", stacked, inner_back, precision=HIGH)
    back_re = back[:, :, :rows_inner]
    back_im = back[:, :, rows_inner:]
    reverted_re = back_re * twid_cos + back_im * twid_sin
    reverted_im = back_im * twid_cos - back_re * twid_sin
    reverted = jnp.concatenate([reverted_re, reverted_im], axis=1)
    result = jnp.einsum("kn,ckm->cnm", outer_table, reverted, precision=HIGH)
    result = result.reshape(channels, length) / padded_len
    return skip_part[:, None] * signal + result


def shards_general(
    value_in,
    key_in,
    gate_first,
    gate_second,
    gate_long,
    filter_first,
    filter_second,
    long_filter,
    skip_gain,
):
    tap_count = filter_first.shape[1]
    channels, length = value_in.shape
    per_device = channels // lax.axis_size("ctx")
    channel_base = lax.axis_index("ctx") * per_device
    mixed_in = (key_in.astype(jnp.float32) * value_in.astype(jnp.float32)).astype(jnp.bfloat16)
    first_out = first_section(mixed_in, gate_first, filter_first, tap_count)
    prior_first = from_behind(first_out[:, length - tap_count :], "ctx", 1)
    first_wide = jnp.concatenate([prior_first, first_out], axis=1)
    second_out = (
        gate_second.astype(jnp.float32) * toeplitz_conv(first_wide, filter_second, tap_count)
    ).astype(jnp.bfloat16)
    moved = to_channels(second_out)
    skip_here = lax.dynamic_slice_in_dim(skip_gain, channel_base, per_device, 0)
    filt_vals = long_filter.astype(jnp.float32)
    long_out = long_convolution(moved.astype(jnp.float32), filt_vals, skip_here).astype(
        jnp.bfloat16
    )
    back_home = lax.all_to_all(long_out, "ctx", split_axis=1, concat_axis=0, tiled=True)
    return (gate_long.astype(jnp.float32) * back_home.astype(jnp.float32)).astype(jnp.bfloat16)


def unit(numerator, denominator):
    return cmath.exp(-2j * math.pi * numerator / denominator)


def turn(value, factor):
    re, im = value
    if abs(factor - 1) < 1e-12:
        return value
    if abs(factor + 1j) < 1e-12:
        return (im, -re)
    if abs(factor - 1j) < 1e-12:
        return (-im, re)
    if abs(abs(factor.real) - abs(factor.imag)) < 1e-12:
        size = abs(factor.real)
        re, im = re * size, im * size
        if factor.real > 0 and factor.imag < 0:
            return (re + im, im - re)
        if factor.real < 0 and factor.imag < 0:
            return (im - re, -re - im)
        if factor.real > 0:
            return (re - im, re + im)
        return (-re - im, re - im)
    return (re * factor.real - im * factor.imag, re * factor.imag + im * factor.real)


def complex_dft(values, sign):
    count = len(values)
    if count == 1:
        return values
    half = count // 2
    low, high = [], []
    for a in range(half):
        (p_re, p_im), (q_re, q_im) = values[a], values[a + half]
        low.append((p_re + q_re, p_im + q_im))
        factor = unit(a, count)
        high.append(turn((p_re - q_re, p_im - q_im), factor if sign > 0 else factor.conjugate()))
    result = [None] * count
    result[0::2] = complex_dft(low, sign)
    result[1::2] = complex_dft(high, sign)
    return result


def odd_bins(values):
    count = len(values)
    if count == 1:
        return {1: (values[0], None)}
    half = count // 2
    folded = [turn((values[a], -values[a + half]), unit(a, 2 * count)) for a in range(half)]
    bins = {}
    for place, (re, im) in enumerate(complex_dft(folded, 1)):
        r = 4 * place + 1
        if r < count:
            bins[r] = (re, im)
        else:
            bins[2 * count - r] = (re, -im)
    return bins


def real_bins(values):
    count = len(values)
    if count == 1:
        return {0: (values[0], None)}
    half = count // 2
    even = real_bins([values[a] + values[a + half] for a in range(half)])
    odd = odd_bins([values[a] - values[a + half] for a in range(half)])
    bins = {2 * r: v for r, v in even.items()}
    bins.update(odd)
    return bins


def padded_bins(values):
    bins = {2 * r: v for r, v in real_bins(values).items()}
    bins.update(odd_bins(values))
    return bins


def odd_back(bins, count):
    if count == 1:
        return [bins[1][0]]
    half = count // 2
    folded = []
    for place in range(half):
        r = 4 * place + 1
        if r < count:
            folded.append(bins[r])
        else:
            re, im = bins[2 * count - r]
            folded.append((re, -im))
    spread = complex_dft(folded, -1)
    spread = [turn(spread[a], unit(a, 2 * count).conjugate()) for a in range(half)]
    return [v[0] for v in spread] + [-v[1] for v in spread]


def real_back(bins, count):
    if count == 1:
        return [bins[0][0]]
    half = count // 2
    even = real_back({r // 2: v for r, v in bins.items() if r % 2 == 0}, half)
    odd = odd_back({r: v for r, v in bins.items() if r % 2 == 1}, half)
    return [even[a] + odd[a] for a in range(half)] + [even[a] - odd[a] for a in range(half)]


def padded_back(bins, count):
    even = real_back({r // 2: v for r, v in bins.items() if r % 2 == 0}, count)
    odd = odd_back({r: v for r, v in bins.items() if r % 2 == 1}, count)
    return [even[a] + odd[a] for a in range(count)]


def inner_tables(length):
    padded_len = 2 * length
    outer = padded_len // LANES
    b = np.arange(LANES)[:, None]
    q = np.arange(LANES)[None, :]
    forward, back = [], []
    for r in range(outer // 2 + 1):
        angle = (b * (r + outer * q) % padded_len) * (-2.0 * math.pi / padded_len)
        c, s = np.cos(angle), np.sin(angle)
        table = np.block([[c, s], [-s, c]])
        weight = (1.0 if r in (0, outer // 2) else 2.0) / padded_len
        forward.append(table)
        back.append(table.T * weight)
    return (
        np.stack(forward).astype(ml_dtypes.bfloat16),
        np.stack(back).astype(ml_dtypes.bfloat16),
    )


def band(row):
    rolled = pltpu.roll(jnp.broadcast_to(row, (LANES, LANES)), 0, 1, stride=1, stride_axis=0)
    s = lax.broadcasted_iota(jnp.int32, (LANES, LANES), 0)
    t = lax.broadcasted_iota(jnp.int32, (LANES, LANES), 1)
    zero = jnp.zeros((LANES, LANES), jnp.float32)
    return jnp.concatenate(
        [jnp.where(t < s, rolled, zero), jnp.where(t >= s, rolled, zero)], axis=0
    ).astype(jnp.bfloat16)


def gated(gate, value):
    return (gate.astype(jnp.float32) * value).astype(jnp.bfloat16)


def whole_kernel(
    n,
    chunk,
    filter_first_ref,
    filter_second_ref,
    skip_ref,
    value_hbm,
    key_hbm,
    gate_first_hbm,
    gate_second_hbm,
    long_filter_hbm,
    forward_hbm,
    back_hbm,
    returned,
    value_ref,
    key_ref,
    gate_first_ref,
    gate_second,
    long_filter,
    forward,
    backward,
    taps_first,
    taps_second,
    band_first,
    band_second,
    mixed,
    first,
    halo_mixed,
    halo_first,
    second,
    gathered,
    long_out,
    skip_wide,
    bins_in,
    spectrum,
    products,
    bins_out,
    load_sem,
    part_sem,
    own_sem,
    rim_send,
    rim_recv,
    there_send,
    there_recv,
    home_send,
    home_recv,
):
    _, per, length = value_hbm.shape
    me = lax.axis_index("ctx")
    blocks = length // LANES
    chunks = per // chunk
    groups = chunk // ROWS
    total_blocks = n * blocks
    bin_count = total_blocks + 1
    last = slice(length - LANES, length)

    barrier = pltpu.get_barrier_semaphore()
    for k in range(1, n):
        pl.semaphore_signal(
            barrier, inc=1, device_id={"ctx": lax.rem(me + k, n)}, device_id_type=MESH
        )

    def part(q):
        return pl.ds(pl.multiple_of(q * chunk, chunk), chunk)

    def loaded(i, q):
        src, dst = (
            (key_hbm, key_ref),
            (value_hbm, value_ref),
            (gate_first_hbm, gate_first_ref),
            (gate_second_hbm, gate_second),
        )[i]
        return pltpu.make_async_copy(
            src.at[:, part(q), :], dst.at[:, part(q), :], part_sem.at[i, q]
        )

    for q in range(chunks):
        for i in range(4):
            loaded(i, q).start()
    loads = [
        pltpu.make_async_copy(src, dst, load_sem.at[i])
        for i, (src, dst) in enumerate(
            [(long_filter_hbm, long_filter), (forward_hbm, forward), (back_hbm, backward)]
        )
    ]
    for load in loads:
        load.start()

    def own(q):
        return pltpu.make_async_copy(
            long_out.at[me, part(q), :], returned.at[me, part(q), :], own_sem.at[q]
        )

    def rim(which, q):
        src, dst = ((mixed, halo_mixed), (first, halo_first))[which]
        return pltpu.make_async_remote_copy(
            src_ref=src.at[:, part(q), last],
            dst_ref=dst.at[:, part(q), :],
            send_sem=rim_send.at[which, q],
            recv_sem=rim_recv.at[which, q],
            device_id={"ctx": lax.rem(me + 1, n)},
            device_id_type=MESH,
        )

    def there(k, q, arriving=False):
        peer = lax.rem(me + (n - k if arriving else k), n)
        slot = peer if arriving else me
        return pltpu.make_async_remote_copy(
            src_ref=second.at[peer, part(q), :],
            dst_ref=gathered.at[slot, part(q), :],
            send_sem=there_send.at[k, q],
            recv_sem=there_recv.at[k, q],
            device_id={"ctx": peer},
            device_id_type=MESH,
        )

    def home(k, q, arriving=False):
        peer = lax.rem(me + (n - k if arriving else k), n)
        slot = peer if arriving else me
        return pltpu.make_async_remote_copy(
            src_ref=long_out.at[peer, part(q), :],
            dst_ref=returned.at[slot, part(q), :],
            send_sem=home_send.at[k, q],
            recv_sem=home_recv.at[k, q],
            device_id={"ctx": peer},
            device_id_type=MESH,
        )

    def rows_at(q, j):
        return pl.ds(pl.multiple_of(q * chunk + j * ROWS, ROWS), ROWS)

    def lanes(b):
        return slice(b * LANES, (b + 1) * LANES)

    taps_first[...] = filter_first_ref[...].astype(jnp.float32)
    taps_second[...] = filter_second_ref[...].astype(jnp.float32)
    eye = lax.broadcasted_iota(jnp.int32, (LANES, LANES), 0) == lax.broadcasted_iota(
        jnp.int32, (LANES, LANES), 1
    )
    for i in range(per // LANES):
        line = skip_ref[pl.ds(me * (per // LANES) + i, 1), :]
        column = jnp.sum(jnp.where(eye, line, 0.0), axis=1, keepdims=True)
        skip_wide[i * LANES : (i + 1) * LANES, :] = jnp.broadcast_to(column, (LANES, LANES))

    pl.semaphore_wait(barrier, n - 1)

    @pl.when(me == 0)
    def _():
        halo_mixed[...] = jnp.zeros_like(halo_mixed)
        halo_first[...] = jnp.zeros_like(halo_first)

    def early(q):
        loaded(0, q).wait()
        loaded(1, q).wait()

        for d in range(n):
            mixed[d, part(q), :] = (
                key_ref[d, part(q), :].astype(jnp.float32)
                * value_ref[d, part(q), :].astype(jnp.float32)
            ).astype(jnp.bfloat16)

        @pl.when(me < n - 1)
        def _():
            rim(0, q).start()

        loaded(2, q).wait()

        for d in range(n):
            for j in range(groups):
                g = d * (per // ROWS) + q * groups + j
                w = band(taps_first[pl.ds(g, 1), :])
                band_first[g] = w
                band_second[g] = band(taps_second[pl.ds(g, 1), :])
                rows = rows_at(q, j)
                windows = jnp.concatenate(
                    [mixed[d, rows, b * LANES - LANES : (b + 1) * LANES] for b in range(1, blocks)],
                    axis=0,
                )
                result = jnp.dot(windows, w, preferred_element_type=jnp.float32)
                for b in range(1, blocks):
                    first[d, rows, lanes(b)] = gated(
                        gate_first_ref[d, rows, lanes(b)], result[(b - 1) * ROWS : b * ROWS]
                    )

        @pl.when(me < n - 1)
        def _():
            rim(1, q).start()

    def late(q):
        loaded(3, q).wait()

        @pl.when(me > 0)
        def _():
            rim(0, q).wait_recv()
            rim(1, q).wait_recv()

        for d in range(n):
            for j in range(groups):
                g = d * (per // ROWS) + q * groups + j
                rows = rows_at(q, j)
                head = jnp.concatenate([halo_mixed[d, rows, :], mixed[d, rows, lanes(0)]], axis=1)
                head = jnp.dot(head, band_first[g], preferred_element_type=jnp.float32)
                first[d, rows, lanes(0)] = gated(gate_first_ref[d, rows, lanes(0)], head)

        for k in [*range(2, n), 1, 0]:
            d = lax.rem(me + k, n)
            target = second if k else gathered
            for j in range(groups):
                g = d * (per // ROWS) + q * groups + j
                rows = rows_at(q, j)
                ahead = jnp.concatenate([halo_first[d, rows, :], first[d, rows, lanes(0)]], axis=1)
                windows = [ahead] + [
                    first[d, rows, b * LANES - LANES : (b + 1) * LANES] for b in range(1, blocks)
                ]
                result = jnp.dot(
                    jnp.concatenate(windows, axis=0),
                    band_second[g],
                    preferred_element_type=jnp.float32,
                )
                for b in range(blocks):
                    target[d, rows, lanes(b)] = gated(
                        gate_second[d, rows, lanes(b)], result[b * ROWS : (b + 1) * ROWS]
                    )
            if k:
                there(k, q).start()

    def start(q, _):
        early(q)
        return 0

    def follow(q, _):
        late(q)
        return 0

    lax.fori_loop(0, chunks, start, 0)
    lax.fori_loop(0, chunks, follow, 0)

    def spread(values, at):
        bins = padded_bins(values)
        for r in range(bin_count):
            re, im = bins[r]
            im = jnp.zeros_like(re) if im is None else im
            bins_in[r, at, :] = jnp.concatenate([re, im], axis=1).astype(jnp.bfloat16)

    loads[0].wait()
    loads[1].wait()

    def filter_rows(j, _):
        at = pl.ds(pl.multiple_of(j * ROWS, ROWS), ROWS)
        spread([long_filter[at, lanes(a)].astype(jnp.float32) for a in range(total_blocks)], at)
        return 0

    lax.fori_loop(0, per // ROWS, filter_rows, 0)

    for r in range(bin_count):
        spectrum[r] = jnp.dot(bins_in[r], forward[r], preferred_element_type=jnp.float32)
    loads[2].wait()

    span = bins_out.shape[1]
    pieces = span // chunk

    def convolve(w, _):
        for c in range(pieces):
            for k in range(1, n):
                there(k, w * pieces + c, True).wait_recv()

        def signal(rows):
            return [
                gathered[a // blocks, rows, lanes(a % blocks)].astype(jnp.float32)
                for a in range(total_blocks)
            ]

        def rows_in(j, _):
            at = pl.ds(pl.multiple_of(j * ROWS, ROWS), ROWS)
            spread(signal(rows_at(w * pieces, j)), at)
            return 0

        lax.fori_loop(0, span // ROWS, rows_in, 0)
        here = pl.ds(pl.multiple_of(w * span, span), span)

        for r in range(bin_count):
            sig = jnp.dot(bins_in[r, 0:span, :], forward[r], preferred_element_type=jnp.float32)
            filt = spectrum[r, here, :]
            sig_re, sig_im = sig[:, :LANES], sig[:, LANES:]
            filt_re, filt_im = filt[:, :LANES], filt[:, LANES:]
            products[r] = jnp.concatenate(
                [sig_re * filt_re - sig_im * filt_im, sig_re * filt_im + sig_im * filt_re], axis=1
            ).astype(jnp.bfloat16)

        for r in range(bin_count):
            bins_out[r] = jnp.dot(products[r], backward[r], preferred_element_type=jnp.float32)

        for c in range(pieces):
            q = w * pieces + c

            def rows_out(j, _):
                at = pl.ds(pl.multiple_of(c * chunk + j * ROWS, ROWS), ROWS)
                rows = rows_at(q, j)
                bins = {
                    r: (bins_out[r, at, :LANES], bins_out[r, at, LANES:]) for r in range(bin_count)
                }
                result = padded_back(bins, total_blocks)
                skip = skip_wide[rows, :]
                for a, value in enumerate(signal(rows)):
                    long_out[a // blocks, rows, lanes(a % blocks)] = (
                        skip * value + result[a]
                    ).astype(jnp.bfloat16)
                return 0

            lax.fori_loop(0, groups, rows_out, 0)
            for k in [*range(2, n), 1]:
                home(k, q).start()
            own(q).start()
        return 0

    lax.fori_loop(0, per // span, convolve, 0)

    def drain(q, _):
        @pl.when(me < n - 1)
        def _():
            rim(0, q).wait_send()
            rim(1, q).wait_send()

        own(q).wait()
        for k in range(1, n):
            there(k, q).wait_send()
            home(k, q).wait_send()
            home(k, q, True).wait_recv()
        return 0

    lax.fori_loop(0, chunks, drain, 0)


def fits_kernel(channels, length, n, tap_count):
    per = channels // n
    total = n * length
    return (
        tap_count == LANES
        and length % LANES == 0
        and length >= 2 * LANES
        and per % LANES == 0
        and n > 1
        and total & (total - 1) == 0
        and total <= 2048
        and channels * total <= 1024 * 2048
    )


def shards(
    value_in,
    key_in,
    gate_first,
    gate_second,
    gate_long,
    filter_first,
    filter_second,
    long_filter,
    skip_gain,
):
    channels, length = value_in.shape
    n = lax.axis_size("ctx")
    if not fits_kernel(channels, length, n, filter_first.shape[1]):
        return shards_general(
            value_in,
            key_in,
            gate_first,
            gate_second,
            gate_long,
            filter_first,
            filter_second,
            long_filter,
            skip_gain,
        )
    per = channels // n
    total = n * length
    chunk = 64
    span = 2 * chunk
    chunks = per // chunk
    group_count = filter_first.shape[0]
    bin_count = total // LANES + 1
    cut = lambda a: a.reshape(n, per, length)
    forward, back = inner_tables(total)
    bf16, f32 = jnp.bfloat16, jnp.float32
    vmem = pl.BlockSpec(memory_space=pltpu.VMEM)
    anywhere = pl.BlockSpec(memory_space=pl.ANY)
    in_hbm = pl.BlockSpec(memory_space=pltpu.HBM)
    dma = pltpu.SemaphoreType.DMA
    out = pl.pallas_call(
        functools.partial(whole_kernel, n, chunk),
        out_shape=jax.ShapeDtypeStruct((n, per, length), bf16),
        in_specs=[vmem] * 3 + [in_hbm] * 7,
        out_specs=anywhere,
        scratch_shapes=[
            pltpu.VMEM((n, per, length), bf16),
            pltpu.VMEM((n, per, length), bf16),
            pltpu.VMEM((n, per, length), bf16),
            pltpu.VMEM((n, per, length), bf16),
            pltpu.VMEM((per, total), bf16),
            pltpu.VMEM(forward.shape, bf16),
            pltpu.VMEM(back.shape, bf16),
            pltpu.VMEM(filter_first.shape, f32),
            pltpu.VMEM(filter_second.shape, f32),
            pltpu.VMEM((group_count, 2 * LANES, LANES), bf16),
            pltpu.VMEM((group_count, 2 * LANES, LANES), bf16),
            pltpu.VMEM((n, per, length), bf16),
            pltpu.VMEM((n, per, length), bf16),
            pltpu.VMEM((n, per, LANES), bf16),
            pltpu.VMEM((n, per, LANES), bf16),
            pltpu.VMEM((n, per, length), bf16),
            pltpu.VMEM((n, per, length), bf16),
            pltpu.VMEM((n, per, length), bf16),
            pltpu.VMEM((per, LANES), f32),
            pltpu.VMEM((bin_count, per, 2 * LANES), bf16),
            pltpu.VMEM((bin_count, per, 2 * LANES), f32),
            pltpu.VMEM((bin_count, span, 2 * LANES), bf16),
            pltpu.VMEM((bin_count, span, 2 * LANES), f32),
            dma((3,)),
            dma((4, chunks)),
            dma((chunks,)),
            dma((2, chunks)),
            dma((2, chunks)),
            dma((n, chunks)),
            dma((n, chunks)),
            dma((n, chunks)),
            dma((n, chunks)),
        ],
        compiler_params=pltpu.CompilerParams(
            collective_id=0, has_side_effects=True, vmem_limit_bytes=52 * 1024 * 1024
        ),
        cost_estimate=pl.CostEstimate(
            flops=8 * channels * length * 2 * LANES + 6 * 2 * per * total * 2 * LANES * 2,
            bytes_accessed=8 * channels * length * 2,
            transcendentals=0,
        ),
    )(
        filter_first,
        filter_second,
        skip_gain.reshape(channels // LANES, LANES),
        cut(value_in),
        cut(key_in),
        cut(gate_first),
        cut(gate_second),
        long_filter,
        jnp.asarray(forward),
        jnp.asarray(back),
    )
    return gated(gate_long, out.reshape(channels, length).astype(f32))


def solution(mesh):
    placed = (
        P("ch", "ctx"),
        P("ch", "ctx"),
        P("ch", "ctx"),
        P("ch", "ctx"),
        P("ch", "ctx"),
        P("ch", None),
        P("ch", None),
        P(("ch", "ctx"), None),
        P("ch"),
    )
    return jax.shard_map(
        shards, mesh=mesh, in_specs=placed, out_specs=P("ch", "ctx"), check_vma=False
    )
```

```python
import cmath
import functools
import math

import jax
import jax.numpy as jnp
import ml_dtypes
import numpy as np
from jax import lax
from jax.experimental import pallas as pl
from jax.experimental.pallas import tpu as pltpu
from jax.sharding import PartitionSpec as P

HIGH = lax.Precision.HIGH
LANES = 128
ROWS = 16
MESH = pl.DeviceIdType.MESH


def from_behind(shard, axis, by):
    devices = lax.axis_size(axis)
    pairs = [(i, i + by) for i in range(devices) if 0 <= i + by < devices]
    return lax.ppermute(shard, axis, pairs)


def band_matrix(filters, tap_count):
    group_count = filters.shape[0]
    zero_one = jnp.zeros((group_count, 1), filters.dtype)
    zero_rest = jnp.zeros((group_count, tap_count), filters.dtype)
    pattern = jnp.concatenate([zero_one, jnp.flip(filters, axis=1), zero_rest], axis=1)
    tiled = jnp.tile(pattern, (1, tap_count))
    return tiled[:, : tap_count * 2 * tap_count].reshape(group_count, tap_count, 2 * tap_count)


def toeplitz_conv(extended, filters, tap_count):
    channels, total_len = extended.shape
    length = total_len - tap_count
    block_count = length // tap_count
    front_half = extended[:, :length].reshape(channels, block_count, tap_count)
    back_half = extended[:, tap_count:].reshape(channels, block_count, tap_count)
    windows = jnp.concatenate([front_half, back_half], axis=2)
    group_count = filters.shape[0]
    windows = windows.reshape(group_count, channels // group_count, block_count, 2 * tap_count)
    toeplitz = band_matrix(filters, tap_count)
    result = jnp.einsum("gts,gcbs->gcbt", toeplitz, windows, preferred_element_type=jnp.float32)
    return result.reshape(channels, length)


def previous_rim(tail):
    return from_behind(tail, "ctx", 1)


def to_channels(data):
    return lax.all_to_all(data, "ctx", split_axis=0, concat_axis=1, tiled=True)


def first_section(mixed_in, gate_first, filter_first, tap_count):
    length = mixed_in.shape[1]
    extended = jnp.concatenate([previous_rim(mixed_in[:, length - tap_count :]), mixed_in], axis=1)
    return (
        gate_first.astype(jnp.float32) * toeplitz_conv(extended, filter_first, tap_count)
    ).astype(jnp.bfloat16)


def dft_tables(size):
    index = jnp.arange(size, dtype=jnp.int32)
    angle = (index[:, None] * index[None, :] % size).astype(jnp.float32) * (-2.0 * math.pi / size)
    return (jnp.cos(angle), jnp.sin(angle))


def split_factor(padded_len):
    outer = 2
    cand = 2
    while cand * cand <= padded_len:
        if padded_len % cand == 0:
            outer = cand
        cand = cand + 2
    return outer


def long_convolution(signal, filt_vals, skip_part):
    channels, length = signal.shape
    padded_len = 2 * length
    rows_outer = split_factor(padded_len)
    rows_inner = padded_len // rows_outer
    half_rows = rows_outer // 2
    outer_cos, outer_sin = dft_tables(rows_outer)
    inner_cos, inner_sin = dft_tables(rows_inner)
    k_index = jnp.arange(rows_outer, dtype=jnp.int32)[:, None]
    n_index = jnp.arange(rows_inner, dtype=jnp.int32)[None, :]
    twid_angle = (k_index * n_index % padded_len).astype(jnp.float32) * (
        -2.0 * math.pi / padded_len
    )
    twid_cos = jnp.cos(twid_angle)
    twid_sin = jnp.sin(twid_angle)
    outer_table = jnp.concatenate([outer_cos[:, :half_rows], outer_sin[:, :half_rows]], axis=0)
    inner_fwd = jnp.concatenate(
        [
            jnp.concatenate([inner_cos, inner_sin], axis=1),
            jnp.concatenate([-inner_sin, inner_cos], axis=1),
        ],
        axis=0,
    )
    inner_back = jnp.concatenate(
        [
            jnp.concatenate([inner_cos, -inner_sin], axis=1),
            jnp.concatenate([inner_sin, inner_cos], axis=1),
        ],
        axis=0,
    )

    def forward(values):
        grid = values.reshape(channels, half_rows, rows_inner)
        parts = jnp.einsum("kn,cnm->ckm", outer_table, grid, precision=HIGH)
        part_re = parts[:, :rows_outer]
        part_im = parts[:, rows_outer:]
        turned_re = part_re * twid_cos - part_im * twid_sin
        turned_im = part_re * twid_sin + part_im * twid_cos
        turned = jnp.concatenate([turned_re, turned_im], axis=2)
        spectrum = jnp.einsum("ckn,nm->ckm", turned, inner_fwd, precision=HIGH)
        return (spectrum[:, :, :rows_inner], spectrum[:, :, rows_inner:])

    sig_re, sig_im = forward(signal)
    filt_re, filt_im = forward(filt_vals)
    prod_re = sig_re * filt_re - sig_im * filt_im
    prod_im = sig_re * filt_im + sig_im * filt_re
    stacked = jnp.concatenate([prod_re, prod_im], axis=2)
    back = jnp.einsum("ckm,mn->ckn", stacked, inner_back, precision=HIGH)
    back_re = back[:, :, :rows_inner]
    back_im = back[:, :, rows_inner:]
    reverted_re = back_re * twid_cos + back_im * twid_sin
    reverted_im = back_im * twid_cos - back_re * twid_sin
    reverted = jnp.concatenate([reverted_re, reverted_im], axis=1)
    result = jnp.einsum("kn,ckm->cnm", outer_table, reverted, precision=HIGH)
    result = result.reshape(channels, length) / padded_len
    return skip_part[:, None] * signal + result


def shards_general(
    value_in,
    key_in,
    gate_first,
    gate_second,
    gate_long,
    filter_first,
    filter_second,
    long_filter,
    skip_gain,
):
    tap_count = filter_first.shape[1]
    channels, length = value_in.shape
    per_device = channels // lax.axis_size("ctx")
    channel_base = lax.axis_index("ctx") * per_device
    mixed_in = (key_in.astype(jnp.float32) * value_in.astype(jnp.float32)).astype(jnp.bfloat16)
    first_out = first_section(mixed_in, gate_first, filter_first, tap_count)
    prior_first = from_behind(first_out[:, length - tap_count :], "ctx", 1)
    first_wide = jnp.concatenate([prior_first, first_out], axis=1)
    second_out = (
        gate_second.astype(jnp.float32) * toeplitz_conv(first_wide, filter_second, tap_count)
    ).astype(jnp.bfloat16)
    moved = to_channels(second_out)
    skip_here = lax.dynamic_slice_in_dim(skip_gain, channel_base, per_device, 0)
    filt_vals = long_filter.astype(jnp.float32)
    long_out = long_convolution(moved.astype(jnp.float32), filt_vals, skip_here).astype(
        jnp.bfloat16
    )
    back_home = lax.all_to_all(long_out, "ctx", split_axis=1, concat_axis=0, tiled=True)
    return (gate_long.astype(jnp.float32) * back_home.astype(jnp.float32)).astype(jnp.bfloat16)


def unit(numerator, denominator):
    return cmath.exp(-2j * math.pi * numerator / denominator)


def turn(value, factor):
    re, im = value
    if abs(factor - 1) < 1e-12:
        return value
    if abs(factor + 1j) < 1e-12:
        return (im, -re)
    if abs(factor - 1j) < 1e-12:
        return (-im, re)
    if abs(abs(factor.real) - abs(factor.imag)) < 1e-12:
        size = abs(factor.real)
        re, im = re * size, im * size
        if factor.real > 0 and factor.imag < 0:
            return (re + im, im - re)
        if factor.real < 0 and factor.imag < 0:
            return (im - re, -re - im)
        if factor.real > 0:
            return (re - im, re + im)
        return (-re - im, re - im)
    return (re * factor.real - im * factor.imag, re * factor.imag + im * factor.real)


def complex_dft(values, sign):
    count = len(values)
    if count == 1:
        return values
    half = count // 2
    low, high = [], []
    for a in range(half):
        (p_re, p_im), (q_re, q_im) = values[a], values[a + half]
        low.append((p_re + q_re, p_im + q_im))
        factor = unit(a, count)
        high.append(turn((p_re - q_re, p_im - q_im), factor if sign > 0 else factor.conjugate()))
    result = [None] * count
    result[0::2] = complex_dft(low, sign)
    result[1::2] = complex_dft(high, sign)
    return result


def odd_bins(values):
    count = len(values)
    if count == 1:
        return {1: (values[0], None)}
    half = count // 2
    folded = [turn((values[a], -values[a + half]), unit(a, 2 * count)) for a in range(half)]
    bins = {}
    for place, (re, im) in enumerate(complex_dft(folded, 1)):
        r = 4 * place + 1
        if r < count:
            bins[r] = (re, im)
        else:
            bins[2 * count - r] = (re, -im)
    return bins


def real_bins(values):
    count = len(values)
    if count == 1:
        return {0: (values[0], None)}
    half = count // 2
    even = real_bins([values[a] + values[a + half] for a in range(half)])
    odd = odd_bins([values[a] - values[a + half] for a in range(half)])
    bins = {2 * r: v for r, v in even.items()}
    bins.update(odd)
    return bins


def padded_bins(values):
    bins = {2 * r: v for r, v in real_bins(values).items()}
    bins.update(odd_bins(values))
    return bins


def odd_back(bins, count):
    if count == 1:
        return [bins[1][0]]
    half = count // 2
    folded = []
    for place in range(half):
        r = 4 * place + 1
        if r < count:
            folded.append(bins[r])
        else:
            re, im = bins[2 * count - r]
            folded.append((re, -im))
    spread = complex_dft(folded, -1)
    spread = [turn(spread[a], unit(a, 2 * count).conjugate()) for a in range(half)]
    return [v[0] for v in spread] + [-v[1] for v in spread]


def real_back(bins, count):
    if count == 1:
        return [bins[0][0]]
    half = count // 2
    even = real_back({r // 2: v for r, v in bins.items() if r % 2 == 0}, half)
    odd = odd_back({r: v for r, v in bins.items() if r % 2 == 1}, half)
    return [even[a] + odd[a] for a in range(half)] + [even[a] - odd[a] for a in range(half)]


def padded_back(bins, count):
    even = real_back({r // 2: v for r, v in bins.items() if r % 2 == 0}, count)
    odd = odd_back({r: v for r, v in bins.items() if r % 2 == 1}, count)
    return [even[a] + odd[a] for a in range(count)]


def inner_tables(length):
    padded_len = 2 * length
    outer = padded_len // LANES
    b = np.arange(LANES)[:, None]
    q = np.arange(LANES)[None, :]
    forward, back = [], []
    for r in range(outer // 2 + 1):
        angle = (b * (r + outer * q) % padded_len) * (-2.0 * math.pi / padded_len)
        c, s = np.cos(angle), np.sin(angle)
        table = np.block([[c, s], [-s, c]])
        weight = (1.0 if r in (0, outer // 2) else 2.0) / padded_len
        forward.append(table)
        back.append(table.T * weight)
    return (
        np.stack(forward).astype(ml_dtypes.bfloat16),
        np.stack(back).astype(ml_dtypes.bfloat16),
    )


def band(row):
    rolled = pltpu.roll(jnp.broadcast_to(row, (LANES, LANES)), 0, 1, stride=1, stride_axis=0)
    s = lax.broadcasted_iota(jnp.int32, (LANES, LANES), 0)
    t = lax.broadcasted_iota(jnp.int32, (LANES, LANES), 1)
    zero = jnp.zeros((LANES, LANES), jnp.float32)
    return jnp.concatenate(
        [jnp.where(t < s, rolled, zero), jnp.where(t >= s, rolled, zero)], axis=0
    ).astype(jnp.bfloat16)


def gated(gate, value):
    return (gate.astype(jnp.float32) * value).astype(jnp.bfloat16)


def whole_kernel(
    n,
    chunk,
    filter_first_ref,
    filter_second_ref,
    skip_ref,
    value_hbm,
    key_hbm,
    gate_first_hbm,
    gate_second_hbm,
    long_filter_hbm,
    forward_hbm,
    back_hbm,
    returned,
    value_ref,
    key_ref,
    gate_first_ref,
    gate_second,
    long_filter,
    forward,
    backward,
    taps_first,
    taps_second,
    band_first,
    band_second,
    mixed,
    first,
    halo_mixed,
    halo_first,
    second,
    gathered,
    long_out,
    skip_wide,
    bins_in,
    spectrum,
    products,
    bins_out,
    load_sem,
    part_sem,
    own_sem,
    rim_send,
    rim_recv,
    there_send,
    there_recv,
    home_send,
    home_recv,
):
    _, per, length = value_hbm.shape
    me = lax.axis_index("ctx")
    blocks = length // LANES
    chunks = per // chunk
    groups = chunk // ROWS
    total_blocks = n * blocks
    bin_count = total_blocks + 1
    last = slice(length - LANES, length)

    barrier = pltpu.get_barrier_semaphore()
    for k in range(1, n):
        pl.semaphore_signal(
            barrier, inc=1, device_id={"ctx": lax.rem(me + k, n)}, device_id_type=MESH
        )

    def part(q):
        return pl.ds(pl.multiple_of(q * chunk, chunk), chunk)

    def loaded(i, q):
        src, dst = (
            (key_hbm, key_ref),
            (value_hbm, value_ref),
            (gate_first_hbm, gate_first_ref),
            (gate_second_hbm, gate_second),
        )[i]
        return pltpu.make_async_copy(
            src.at[:, part(q), :], dst.at[:, part(q), :], part_sem.at[i, q]
        )

    for q in range(chunks):
        for i in range(4):
            loaded(i, q).start()
    loads = [
        pltpu.make_async_copy(src, dst, load_sem.at[i])
        for i, (src, dst) in enumerate(
            [(long_filter_hbm, long_filter), (forward_hbm, forward), (back_hbm, backward)]
        )
    ]
    for load in loads:
        load.start()

    def own(q):
        return pltpu.make_async_copy(
            long_out.at[me, part(q), :], returned.at[me, part(q), :], own_sem.at[q]
        )

    def rim(which, q):
        src, dst = ((mixed, halo_mixed), (first, halo_first))[which]
        return pltpu.make_async_remote_copy(
            src_ref=src.at[:, part(q), last],
            dst_ref=dst.at[:, part(q), :],
            send_sem=rim_send.at[which, q],
            recv_sem=rim_recv.at[which, q],
            device_id={"ctx": lax.rem(me + 1, n)},
            device_id_type=MESH,
        )

    def there(k, q, arriving=False):
        peer = lax.rem(me + (n - k if arriving else k), n)
        slot = peer if arriving else me
        return pltpu.make_async_remote_copy(
            src_ref=second.at[peer, part(q), :],
            dst_ref=gathered.at[slot, part(q), :],
            send_sem=there_send.at[k, q],
            recv_sem=there_recv.at[k, q],
            device_id={"ctx": peer},
            device_id_type=MESH,
        )

    def home(k, q, arriving=False):
        peer = lax.rem(me + (n - k if arriving else k), n)
        slot = peer if arriving else me
        return pltpu.make_async_remote_copy(
            src_ref=long_out.at[peer, part(q), :],
            dst_ref=returned.at[slot, part(q), :],
            send_sem=home_send.at[k, q],
            recv_sem=home_recv.at[k, q],
            device_id={"ctx": peer},
            device_id_type=MESH,
        )

    def rows_at(q, j):
        return pl.ds(pl.multiple_of(q * chunk + j * ROWS, ROWS), ROWS)

    def lanes(b):
        return slice(b * LANES, (b + 1) * LANES)

    taps_first[...] = filter_first_ref[...].astype(jnp.float32)
    taps_second[...] = filter_second_ref[...].astype(jnp.float32)
    eye = lax.broadcasted_iota(jnp.int32, (LANES, LANES), 0) == lax.broadcasted_iota(
        jnp.int32, (LANES, LANES), 1
    )
    for i in range(per // LANES):
        line = skip_ref[pl.ds(me * (per // LANES) + i, 1), :]
        column = jnp.sum(jnp.where(eye, line, 0.0), axis=1, keepdims=True)
        skip_wide[i * LANES : (i + 1) * LANES, :] = jnp.broadcast_to(column, (LANES, LANES))

    pl.semaphore_wait(barrier, n - 1)

    @pl.when(me == 0)
    def _():
        halo_mixed[...] = jnp.zeros_like(halo_mixed)
        halo_first[...] = jnp.zeros_like(halo_first)

    def early(q):
        loaded(0, q).wait()
        loaded(1, q).wait()

        for d in range(n):
            mixed[d, part(q), :] = (
                key_ref[d, part(q), :].astype(jnp.float32)
                * value_ref[d, part(q), :].astype(jnp.float32)
            ).astype(jnp.bfloat16)

        @pl.when(me < n - 1)
        def _():
            rim(0, q).start()

        loaded(2, q).wait()

        for d in range(n):
            for j in range(groups):
                g = d * (per // ROWS) + q * groups + j
                w = band(taps_first[pl.ds(g, 1), :])
                band_first[g] = w
                band_second[g] = band(taps_second[pl.ds(g, 1), :])
                rows = rows_at(q, j)
                windows = jnp.concatenate(
                    [mixed[d, rows, b * LANES - LANES : (b + 1) * LANES] for b in range(1, blocks)],
                    axis=0,
                )
                result = jnp.dot(windows, w, preferred_element_type=jnp.float32)
                for b in range(1, blocks):
                    first[d, rows, lanes(b)] = gated(
                        gate_first_ref[d, rows, lanes(b)], result[(b - 1) * ROWS : b * ROWS]
                    )

        @pl.when(me < n - 1)
        def _():
            rim(1, q).start()

    def late(q):
        loaded(3, q).wait()

        @pl.when(me > 0)
        def _():
            rim(0, q).wait_recv()
            rim(1, q).wait_recv()

        for d in range(n):
            for j in range(groups):
                g = d * (per // ROWS) + q * groups + j
                rows = rows_at(q, j)
                head = jnp.concatenate([halo_mixed[d, rows, :], mixed[d, rows, lanes(0)]], axis=1)
                head = jnp.dot(head, band_first[g], preferred_element_type=jnp.float32)
                first[d, rows, lanes(0)] = gated(gate_first_ref[d, rows, lanes(0)], head)

        for k in [*range(2, n), 1, 0]:
            d = lax.rem(me + k, n)
            target = second if k else gathered
            for j in range(groups):
                g = d * (per // ROWS) + q * groups + j
                rows = rows_at(q, j)
                ahead = jnp.concatenate([halo_first[d, rows, :], first[d, rows, lanes(0)]], axis=1)
                windows = [ahead] + [
                    first[d, rows, b * LANES - LANES : (b + 1) * LANES] for b in range(1, blocks)
                ]
                result = jnp.dot(
                    jnp.concatenate(windows, axis=0),
                    band_second[g],
                    preferred_element_type=jnp.float32,
                )
                for b in range(blocks):
                    target[d, rows, lanes(b)] = gated(
                        gate_second[d, rows, lanes(b)], result[b * ROWS : (b + 1) * ROWS]
                    )
            if k:
                there(k, q).start()

    def start(q, _):
        early(q)
        return 0

    def follow(q, _):
        late(q)
        return 0

    lax.fori_loop(0, chunks, start, 0)
    lax.fori_loop(0, chunks, follow, 0)

    def spread(values, at):
        bins = padded_bins(values)
        for r in range(bin_count):
            re, im = bins[r]
            im = jnp.zeros_like(re) if im is None else im
            bins_in[r, at, :] = jnp.concatenate([re, im], axis=1).astype(jnp.bfloat16)

    loads[0].wait()
    loads[1].wait()

    def filter_rows(j, _):
        at = pl.ds(pl.multiple_of(j * ROWS, ROWS), ROWS)
        spread([long_filter[at, lanes(a)].astype(jnp.float32) for a in range(total_blocks)], at)
        return 0

    lax.fori_loop(0, per // ROWS, filter_rows, 0)

    for r in range(bin_count):
        spectrum[r] = jnp.dot(bins_in[r], forward[r], preferred_element_type=jnp.float32)
    loads[2].wait()

    span = bins_out.shape[1]
    pieces = span // chunk

    def convolve(w, _):
        for c in range(pieces):
            for k in range(1, n):
                there(k, w * pieces + c, True).wait_recv()

        def signal(rows):
            return [
                gathered[a // blocks, rows, lanes(a % blocks)].astype(jnp.float32)
                for a in range(total_blocks)
            ]

        def rows_in(j, _):
            at = pl.ds(pl.multiple_of(j * ROWS, ROWS), ROWS)
            spread(signal(rows_at(w * pieces, j)), at)
            return 0

        lax.fori_loop(0, span // ROWS, rows_in, 0)
        here = pl.ds(pl.multiple_of(w * span, span), span)

        for r in range(bin_count):
            sig = jnp.dot(bins_in[r, 0:span, :], forward[r], preferred_element_type=jnp.float32)
            filt = spectrum[r, here, :]
            sig_re, sig_im = sig[:, :LANES], sig[:, LANES:]
            filt_re, filt_im = filt[:, :LANES], filt[:, LANES:]
            products[r] = jnp.concatenate(
                [sig_re * filt_re - sig_im * filt_im, sig_re * filt_im + sig_im * filt_re], axis=1
            ).astype(jnp.bfloat16)

        for r in range(bin_count):
            bins_out[r] = jnp.dot(products[r], backward[r], preferred_element_type=jnp.float32)

        for c in range(pieces):
            q = w * pieces + c

            def rows_out(j, _):
                at = pl.ds(pl.multiple_of(c * chunk + j * ROWS, ROWS), ROWS)
                rows = rows_at(q, j)
                bins = {
                    r: (bins_out[r, at, :LANES], bins_out[r, at, LANES:]) for r in range(bin_count)
                }
                result = padded_back(bins, total_blocks)
                skip = skip_wide[rows, :]
                for a, value in enumerate(signal(rows)):
                    long_out[a // blocks, rows, lanes(a % blocks)] = (
                        skip * value + result[a]
                    ).astype(jnp.bfloat16)
                return 0

            lax.fori_loop(0, groups, rows_out, 0)
            for k in [*range(2, n), 1]:
                home(k, q).start()
            own(q).start()
        return 0

    lax.fori_loop(0, per // span, convolve, 0)

    def drain(q, _):
        @pl.when(me < n - 1)
        def _():
            rim(0, q).wait_send()
            rim(1, q).wait_send()

        own(q).wait()
        for k in range(1, n):
            there(k, q).wait_send()
            home(k, q).wait_send()
            home(k, q, True).wait_recv()
        return 0

    lax.fori_loop(0, chunks, drain, 0)


def fits_kernel(channels, length, n, tap_count):
    per = channels // n
    total = n * length
    return (
        tap_count == LANES
        and length % LANES == 0
        and length >= 2 * LANES
        and per % LANES == 0
        and n > 1
        and total & (total - 1) == 0
        and total <= 2048
        and channels * total <= 1024 * 2048
    )


def shards(
    value_in,
    key_in,
    gate_first,
    gate_second,
    gate_long,
    filter_first,
    filter_second,
    long_filter,
    skip_gain,
):
    channels, length = value_in.shape
    n = lax.axis_size("ctx")
    if not fits_kernel(channels, length, n, filter_first.shape[1]):
        return shards_general(
            value_in,
            key_in,
            gate_first,
            gate_second,
            gate_long,
            filter_first,
            filter_second,
            long_filter,
            skip_gain,
        )
    per = channels // n
    total = n * length
    chunk = 64
    span = 2 * chunk
    chunks = per // chunk
    group_count = filter_first.shape[0]
    bin_count = total // LANES + 1
    cut = lambda a: a.reshape(n, per, length)
    forward, back = inner_tables(total)
    bf16, f32 = jnp.bfloat16, jnp.float32
    vmem = pl.BlockSpec(memory_space=pltpu.VMEM)
    anywhere = pl.BlockSpec(memory_space=pl.ANY)
    in_hbm = pl.BlockSpec(memory_space=pltpu.HBM)
    dma = pltpu.SemaphoreType.DMA
    out = pl.pallas_call(
        functools.partial(whole_kernel, n, chunk),
        out_shape=jax.ShapeDtypeStruct((n, per, length), bf16),
        in_specs=[vmem] * 3 + [in_hbm] * 7,
        out_specs=anywhere,
        scratch_shapes=[
            pltpu.VMEM((n, per, length), bf16),
            pltpu.VMEM((n, per, length), bf16),
            pltpu.VMEM((n, per, length), bf16),
            pltpu.VMEM((n, per, length), bf16),
            pltpu.VMEM((per, total), bf16),
            pltpu.VMEM(forward.shape, bf16),
            pltpu.VMEM(back.shape, bf16),
            pltpu.VMEM(filter_first.shape, f32),
            pltpu.VMEM(filter_second.shape, f32),
            pltpu.VMEM((group_count, 2 * LANES, LANES), bf16),
            pltpu.VMEM((group_count, 2 * LANES, LANES), bf16),
            pltpu.VMEM((n, per, length), bf16),
            pltpu.VMEM((n, per, length), bf16),
            pltpu.VMEM((n, per, LANES), bf16),
            pltpu.VMEM((n, per, LANES), bf16),
            pltpu.VMEM((n, per, length), bf16),
            pltpu.VMEM((n, per, length), bf16),
            pltpu.VMEM((n, per, length), bf16),
            pltpu.VMEM((per, LANES), f32),
            pltpu.VMEM((bin_count, per, 2 * LANES), bf16),
            pltpu.VMEM((bin_count, per, 2 * LANES), f32),
            pltpu.VMEM((bin_count, span, 2 * LANES), bf16),
            pltpu.VMEM((bin_count, span, 2 * LANES), f32),
            dma((3,)),
            dma((4, chunks)),
            dma((chunks,)),
            dma((2, chunks)),
            dma((2, chunks)),
            dma((n, chunks)),
            dma((n, chunks)),
            dma((n, chunks)),
            dma((n, chunks)),
        ],
        compiler_params=pltpu.CompilerParams(
            collective_id=0, has_side_effects=True, vmem_limit_bytes=52 * 1024 * 1024
        ),
        cost_estimate=pl.CostEstimate(
            flops=8 * channels * length * 2 * LANES + 6 * 2 * per * total * 2 * LANES * 2,
            bytes_accessed=8 * channels * length * 2,
            transcendentals=0,
        ),
    )(
        *[
            pltpu.with_memory_space_constraint(a, pltpu.HBM)
            for a in (
                filter_first,
                filter_second,
                skip_gain.reshape(channels // LANES, LANES),
                cut(value_in),
                cut(key_in),
                cut(gate_first),
                cut(gate_second),
                long_filter,
                jnp.asarray(forward),
                jnp.asarray(back),
            )
        ]
    )
    return gated(gate_long, out.reshape(channels, length).astype(f32))


def solution(mesh):
    placed = (
        P("ch", "ctx"),
        P("ch", "ctx"),
        P("ch", "ctx"),
        P("ch", "ctx"),
        P("ch", "ctx"),
        P("ch", None),
        P("ch", None),
        P(("ch", "ctx"), None),
        P("ch"),
    )
    return jax.shard_map(
        shards, mesh=mesh, in_specs=placed, out_specs=P("ch", "ctx"), check_vma=False
    )
```

```python
import cmath
import functools
import math

import jax
import jax.numpy as jnp
import ml_dtypes
import numpy as np
from jax import lax
from jax.experimental import pallas as pl
from jax.experimental.pallas import tpu as pltpu
from jax.sharding import PartitionSpec as P

HIGH = lax.Precision.HIGH
LANES = 128
ROWS = 16
MESH = pl.DeviceIdType.MESH


def from_behind(shard, axis, by):
    devices = lax.axis_size(axis)
    pairs = [(i, i + by) for i in range(devices) if 0 <= i + by < devices]
    return lax.ppermute(shard, axis, pairs)


def band_matrix(filters, tap_count):
    group_count = filters.shape[0]
    zero_one = jnp.zeros((group_count, 1), filters.dtype)
    zero_rest = jnp.zeros((group_count, tap_count), filters.dtype)
    pattern = jnp.concatenate([zero_one, jnp.flip(filters, axis=1), zero_rest], axis=1)
    tiled = jnp.tile(pattern, (1, tap_count))
    return tiled[:, : tap_count * 2 * tap_count].reshape(group_count, tap_count, 2 * tap_count)


def toeplitz_conv(extended, filters, tap_count):
    channels, total_len = extended.shape
    length = total_len - tap_count
    block_count = length // tap_count
    front_half = extended[:, :length].reshape(channels, block_count, tap_count)
    back_half = extended[:, tap_count:].reshape(channels, block_count, tap_count)
    windows = jnp.concatenate([front_half, back_half], axis=2)
    group_count = filters.shape[0]
    windows = windows.reshape(group_count, channels // group_count, block_count, 2 * tap_count)
    toeplitz = band_matrix(filters, tap_count)
    result = jnp.einsum("gts,gcbs->gcbt", toeplitz, windows, preferred_element_type=jnp.float32)
    return result.reshape(channels, length)


def previous_rim(tail):
    return from_behind(tail, "ctx", 1)


def to_channels(data):
    return lax.all_to_all(data, "ctx", split_axis=0, concat_axis=1, tiled=True)


def first_section(mixed_in, gate_first, filter_first, tap_count):
    length = mixed_in.shape[1]
    extended = jnp.concatenate([previous_rim(mixed_in[:, length - tap_count :]), mixed_in], axis=1)
    return (
        gate_first.astype(jnp.float32) * toeplitz_conv(extended, filter_first, tap_count)
    ).astype(jnp.bfloat16)


def dft_tables(size):
    index = jnp.arange(size, dtype=jnp.int32)
    angle = (index[:, None] * index[None, :] % size).astype(jnp.float32) * (-2.0 * math.pi / size)
    return (jnp.cos(angle), jnp.sin(angle))


def split_factor(padded_len):
    outer = 2
    cand = 2
    while cand * cand <= padded_len:
        if padded_len % cand == 0:
            outer = cand
        cand = cand + 2
    return outer


def long_convolution(signal, filt_vals, skip_part):
    channels, length = signal.shape
    padded_len = 2 * length
    rows_outer = split_factor(padded_len)
    rows_inner = padded_len // rows_outer
    half_rows = rows_outer // 2
    outer_cos, outer_sin = dft_tables(rows_outer)
    inner_cos, inner_sin = dft_tables(rows_inner)
    k_index = jnp.arange(rows_outer, dtype=jnp.int32)[:, None]
    n_index = jnp.arange(rows_inner, dtype=jnp.int32)[None, :]
    twid_angle = (k_index * n_index % padded_len).astype(jnp.float32) * (
        -2.0 * math.pi / padded_len
    )
    twid_cos = jnp.cos(twid_angle)
    twid_sin = jnp.sin(twid_angle)
    outer_table = jnp.concatenate([outer_cos[:, :half_rows], outer_sin[:, :half_rows]], axis=0)
    inner_fwd = jnp.concatenate(
        [
            jnp.concatenate([inner_cos, inner_sin], axis=1),
            jnp.concatenate([-inner_sin, inner_cos], axis=1),
        ],
        axis=0,
    )
    inner_back = jnp.concatenate(
        [
            jnp.concatenate([inner_cos, -inner_sin], axis=1),
            jnp.concatenate([inner_sin, inner_cos], axis=1),
        ],
        axis=0,
    )

    def forward(values):
        grid = values.reshape(channels, half_rows, rows_inner)
        parts = jnp.einsum("kn,cnm->ckm", outer_table, grid, precision=HIGH)
        part_re = parts[:, :rows_outer]
        part_im = parts[:, rows_outer:]
        turned_re = part_re * twid_cos - part_im * twid_sin
        turned_im = part_re * twid_sin + part_im * twid_cos
        turned = jnp.concatenate([turned_re, turned_im], axis=2)
        spectrum = jnp.einsum("ckn,nm->ckm", turned, inner_fwd, precision=HIGH)
        return (spectrum[:, :, :rows_inner], spectrum[:, :, rows_inner:])

    sig_re, sig_im = forward(signal)
    filt_re, filt_im = forward(filt_vals)
    prod_re = sig_re * filt_re - sig_im * filt_im
    prod_im = sig_re * filt_im + sig_im * filt_re
    stacked = jnp.concatenate([prod_re, prod_im], axis=2)
    back = jnp.einsum("ckm,mn->ckn", stacked, inner_back, precision=HIGH)
    back_re = back[:, :, :rows_inner]
    back_im = back[:, :, rows_inner:]
    reverted_re = back_re * twid_cos + back_im * twid_sin
    reverted_im = back_im * twid_cos - back_re * twid_sin
    reverted = jnp.concatenate([reverted_re, reverted_im], axis=1)
    result = jnp.einsum("kn,ckm->cnm", outer_table, reverted, precision=HIGH)
    result = result.reshape(channels, length) / padded_len
    return skip_part[:, None] * signal + result


def shards_general(
    value_in,
    key_in,
    gate_first,
    gate_second,
    gate_long,
    filter_first,
    filter_second,
    long_filter,
    skip_gain,
):
    tap_count = filter_first.shape[1]
    channels, length = value_in.shape
    per_device = channels // lax.axis_size("ctx")
    channel_base = lax.axis_index("ctx") * per_device
    mixed_in = (key_in.astype(jnp.float32) * value_in.astype(jnp.float32)).astype(jnp.bfloat16)
    first_out = first_section(mixed_in, gate_first, filter_first, tap_count)
    prior_first = from_behind(first_out[:, length - tap_count :], "ctx", 1)
    first_wide = jnp.concatenate([prior_first, first_out], axis=1)
    second_out = (
        gate_second.astype(jnp.float32) * toeplitz_conv(first_wide, filter_second, tap_count)
    ).astype(jnp.bfloat16)
    moved = to_channels(second_out)
    skip_here = lax.dynamic_slice_in_dim(skip_gain, channel_base, per_device, 0)
    filt_vals = long_filter.astype(jnp.float32)
    long_out = long_convolution(moved.astype(jnp.float32), filt_vals, skip_here).astype(
        jnp.bfloat16
    )
    back_home = lax.all_to_all(long_out, "ctx", split_axis=1, concat_axis=0, tiled=True)
    return (gate_long.astype(jnp.float32) * back_home.astype(jnp.float32)).astype(jnp.bfloat16)


def unit(numerator, denominator):
    return cmath.exp(-2j * math.pi * numerator / denominator)


def turn(value, factor):
    re, im = value
    if abs(factor - 1) < 1e-12:
        return value
    if abs(factor + 1j) < 1e-12:
        return (im, -re)
    if abs(factor - 1j) < 1e-12:
        return (-im, re)
    if abs(abs(factor.real) - abs(factor.imag)) < 1e-12:
        size = abs(factor.real)
        re, im = re * size, im * size
        if factor.real > 0 and factor.imag < 0:
            return (re + im, im - re)
        if factor.real < 0 and factor.imag < 0:
            return (im - re, -re - im)
        if factor.real > 0:
            return (re - im, re + im)
        return (-re - im, re - im)
    return (re * factor.real - im * factor.imag, re * factor.imag + im * factor.real)


def complex_dft(values, sign):
    count = len(values)
    if count == 1:
        return values
    half = count // 2
    low, high = [], []
    for a in range(half):
        (p_re, p_im), (q_re, q_im) = values[a], values[a + half]
        low.append((p_re + q_re, p_im + q_im))
        factor = unit(a, count)
        high.append(turn((p_re - q_re, p_im - q_im), factor if sign > 0 else factor.conjugate()))
    result = [None] * count
    result[0::2] = complex_dft(low, sign)
    result[1::2] = complex_dft(high, sign)
    return result


def odd_bins(values):
    count = len(values)
    if count == 1:
        return {1: (values[0], None)}
    half = count // 2
    folded = [turn((values[a], -values[a + half]), unit(a, 2 * count)) for a in range(half)]
    bins = {}
    for place, (re, im) in enumerate(complex_dft(folded, 1)):
        r = 4 * place + 1
        if r < count:
            bins[r] = (re, im)
        else:
            bins[2 * count - r] = (re, -im)
    return bins


def real_bins(values):
    count = len(values)
    if count == 1:
        return {0: (values[0], None)}
    half = count // 2
    even = real_bins([values[a] + values[a + half] for a in range(half)])
    odd = odd_bins([values[a] - values[a + half] for a in range(half)])
    bins = {2 * r: v for r, v in even.items()}
    bins.update(odd)
    return bins


def padded_bins(values):
    bins = {2 * r: v for r, v in real_bins(values).items()}
    bins.update(odd_bins(values))
    return bins


def odd_back(bins, count):
    if count == 1:
        return [bins[1][0]]
    half = count // 2
    folded = []
    for place in range(half):
        r = 4 * place + 1
        if r < count:
            folded.append(bins[r])
        else:
            re, im = bins[2 * count - r]
            folded.append((re, -im))
    spread = complex_dft(folded, -1)
    spread = [turn(spread[a], unit(a, 2 * count).conjugate()) for a in range(half)]
    return [v[0] for v in spread] + [-v[1] for v in spread]


def real_back(bins, count):
    if count == 1:
        return [bins[0][0]]
    half = count // 2
    even = real_back({r // 2: v for r, v in bins.items() if r % 2 == 0}, half)
    odd = odd_back({r: v for r, v in bins.items() if r % 2 == 1}, half)
    return [even[a] + odd[a] for a in range(half)] + [even[a] - odd[a] for a in range(half)]


def padded_back(bins, count):
    even = real_back({r // 2: v for r, v in bins.items() if r % 2 == 0}, count)
    odd = odd_back({r: v for r, v in bins.items() if r % 2 == 1}, count)
    return [even[a] + odd[a] for a in range(count)]


def inner_tables(length):
    padded_len = 2 * length
    outer = padded_len // LANES
    b = np.arange(LANES)[:, None]
    q = np.arange(LANES)[None, :]
    forward, back = [], []
    for r in range(outer // 2 + 1):
        angle = (b * (r + outer * q) % padded_len) * (-2.0 * math.pi / padded_len)
        c, s = np.cos(angle), np.sin(angle)
        table = np.block([[c, s], [-s, c]])
        weight = (1.0 if r in (0, outer // 2) else 2.0) / padded_len
        forward.append(table)
        back.append(table.T * weight)
    return (
        np.stack(forward).astype(ml_dtypes.bfloat16),
        np.stack(back).astype(ml_dtypes.bfloat16),
    )


def band(row):
    rolled = pltpu.roll(jnp.broadcast_to(row, (LANES, LANES)), 0, 1, stride=1, stride_axis=0)
    s = lax.broadcasted_iota(jnp.int32, (LANES, LANES), 0)
    t = lax.broadcasted_iota(jnp.int32, (LANES, LANES), 1)
    zero = jnp.zeros((LANES, LANES), jnp.float32)
    return jnp.concatenate(
        [jnp.where(t < s, rolled, zero), jnp.where(t >= s, rolled, zero)], axis=0
    ).astype(jnp.bfloat16)


def gated(gate, value):
    return (gate.astype(jnp.float32) * value).astype(jnp.bfloat16)


def whole_kernel(
    n,
    chunk,
    filter_first_ref,
    filter_second_ref,
    skip_ref,
    value_hbm,
    key_hbm,
    gate_first_hbm,
    gate_second_hbm,
    long_filter_hbm,
    forward_hbm,
    back_hbm,
    returned,
    value_ref,
    key_ref,
    gate_first_ref,
    gate_second,
    long_filter,
    forward,
    backward,
    taps_first,
    taps_second,
    band_first,
    band_second,
    mixed,
    first,
    halo_mixed,
    halo_first,
    second,
    gathered,
    long_out,
    skip_wide,
    bins_in,
    spectrum,
    products,
    bins_out,
    load_sem,
    part_sem,
    own_sem,
    rim_send,
    rim_recv,
    there_send,
    there_recv,
    home_send,
    home_recv,
):
    _, per, length = value_hbm.shape
    me = lax.axis_index("ctx")
    blocks = length // LANES
    chunks = per // chunk
    groups = chunk // ROWS
    total_blocks = n * blocks
    bin_count = total_blocks + 1
    last = slice(length - LANES, length)

    barrier = pltpu.get_barrier_semaphore()
    for k in range(1, n):
        pl.semaphore_signal(
            barrier, inc=1, device_id={"ctx": lax.rem(me + k, n)}, device_id_type=MESH
        )

    def part(q):
        return pl.ds(pl.multiple_of(q * chunk, chunk), chunk)

    def loaded(i, q):
        src, dst = (
            (key_hbm, key_ref),
            (value_hbm, value_ref),
            (gate_first_hbm, gate_first_ref),
            (gate_second_hbm, gate_second),
        )[i]
        return pltpu.make_async_copy(
            src.at[:, part(q), :], dst.at[:, part(q), :], part_sem.at[i, q]
        )

    for q in range(chunks):
        for i in range(4):
            loaded(i, q).start()
    loads = [
        pltpu.make_async_copy(src, dst, load_sem.at[i])
        for i, (src, dst) in enumerate(
            [(long_filter_hbm, long_filter), (forward_hbm, forward), (back_hbm, backward)]
        )
    ]
    for load in loads:
        load.start()

    def own(q):
        return pltpu.make_async_copy(
            long_out.at[me, part(q), :], returned.at[me, part(q), :], own_sem.at[q]
        )

    def rim(which, q):
        src, dst = ((mixed, halo_mixed), (first, halo_first))[which]
        return pltpu.make_async_remote_copy(
            src_ref=src.at[:, part(q), last],
            dst_ref=dst.at[:, part(q), :],
            send_sem=rim_send.at[which, q],
            recv_sem=rim_recv.at[which, q],
            device_id={"ctx": lax.rem(me + 1, n)},
            device_id_type=MESH,
        )

    def there(k, q, arriving=False):
        peer = lax.rem(me + (n - k if arriving else k), n)
        slot = peer if arriving else me
        return pltpu.make_async_remote_copy(
            src_ref=second.at[peer, part(q), :],
            dst_ref=gathered.at[slot, part(q), :],
            send_sem=there_send.at[k, q],
            recv_sem=there_recv.at[k, q],
            device_id={"ctx": peer},
            device_id_type=MESH,
        )

    def home(k, q, arriving=False):
        peer = lax.rem(me + (n - k if arriving else k), n)
        slot = peer if arriving else me
        return pltpu.make_async_remote_copy(
            src_ref=long_out.at[peer, part(q), :],
            dst_ref=returned.at[slot, part(q), :],
            send_sem=home_send.at[k, q],
            recv_sem=home_recv.at[k, q],
            device_id={"ctx": peer},
            device_id_type=MESH,
        )

    def rows_at(q, j):
        return pl.ds(pl.multiple_of(q * chunk + j * ROWS, ROWS), ROWS)

    def lanes(b):
        return slice(b * LANES, (b + 1) * LANES)

    taps_first[...] = filter_first_ref[...].astype(jnp.float32)
    taps_second[...] = filter_second_ref[...].astype(jnp.float32)
    eye = lax.broadcasted_iota(jnp.int32, (LANES, LANES), 0) == lax.broadcasted_iota(
        jnp.int32, (LANES, LANES), 1
    )
    for i in range(per // LANES):
        line = skip_ref[pl.ds(me * (per // LANES) + i, 1), :]
        column = jnp.sum(jnp.where(eye, line, 0.0), axis=1, keepdims=True)
        skip_wide[i * LANES : (i + 1) * LANES, :] = jnp.broadcast_to(column, (LANES, LANES))

    pl.semaphore_wait(barrier, n - 1)

    @pl.when(me == 0)
    def _():
        halo_mixed[...] = jnp.zeros_like(halo_mixed)
        halo_first[...] = jnp.zeros_like(halo_first)

    def early(q):
        loaded(0, q).wait()
        loaded(1, q).wait()

        for d in range(n):
            mixed[d, part(q), :] = (
                key_ref[d, part(q), :].astype(jnp.float32)
                * value_ref[d, part(q), :].astype(jnp.float32)
            ).astype(jnp.bfloat16)

        @pl.when(me < n - 1)
        def _():
            rim(0, q).start()

        loaded(2, q).wait()

        for d in range(n):
            for j in range(groups):
                g = d * (per // ROWS) + q * groups + j
                w = band(taps_first[pl.ds(g, 1), :])
                band_first[g] = w
                band_second[g] = band(taps_second[pl.ds(g, 1), :])
                rows = rows_at(q, j)
                windows = jnp.concatenate(
                    [mixed[d, rows, b * LANES - LANES : (b + 1) * LANES] for b in range(1, blocks)],
                    axis=0,
                )
                result = jnp.dot(windows, w, preferred_element_type=jnp.float32)
                for b in range(1, blocks):
                    first[d, rows, lanes(b)] = gated(
                        gate_first_ref[d, rows, lanes(b)], result[(b - 1) * ROWS : b * ROWS]
                    )

        @pl.when(me < n - 1)
        def _():
            rim(1, q).start()

    def late(q):
        loaded(3, q).wait()

        @pl.when(me > 0)
        def _():
            rim(0, q).wait_recv()
            rim(1, q).wait_recv()

        for d in range(n):
            for j in range(groups):
                g = d * (per // ROWS) + q * groups + j
                rows = rows_at(q, j)
                head = jnp.concatenate([halo_mixed[d, rows, :], mixed[d, rows, lanes(0)]], axis=1)
                head = jnp.dot(head, band_first[g], preferred_element_type=jnp.float32)
                first[d, rows, lanes(0)] = gated(gate_first_ref[d, rows, lanes(0)], head)

        for k in [*range(2, n), 1, 0]:
            d = lax.rem(me + k, n)
            target = second if k else gathered
            for j in range(groups):
                g = d * (per // ROWS) + q * groups + j
                rows = rows_at(q, j)
                ahead = jnp.concatenate([halo_first[d, rows, :], first[d, rows, lanes(0)]], axis=1)
                windows = [ahead] + [
                    first[d, rows, b * LANES - LANES : (b + 1) * LANES] for b in range(1, blocks)
                ]
                result = jnp.dot(
                    jnp.concatenate(windows, axis=0),
                    band_second[g],
                    preferred_element_type=jnp.float32,
                )
                for b in range(blocks):
                    target[d, rows, lanes(b)] = gated(
                        gate_second[d, rows, lanes(b)], result[b * ROWS : (b + 1) * ROWS]
                    )
            if k:
                there(k, q).start()

    def start(q, _):
        early(q)
        return 0

    def follow(q, _):
        late(q)
        return 0

    lax.fori_loop(0, chunks, start, 0)
    lax.fori_loop(0, chunks, follow, 0)

    def spread(values, at):
        bins = padded_bins(values)
        for r in range(bin_count):
            re, im = bins[r]
            im = jnp.zeros_like(re) if im is None else im
            bins_in[r, at, :] = jnp.concatenate([re, im], axis=1).astype(jnp.bfloat16)

    loads[0].wait()
    loads[1].wait()

    def filter_rows(j, _):
        at = pl.ds(pl.multiple_of(j * ROWS, ROWS), ROWS)
        spread([long_filter[at, lanes(a)].astype(jnp.float32) for a in range(total_blocks)], at)
        return 0

    lax.fori_loop(0, per // ROWS, filter_rows, 0)

    for r in range(bin_count):
        spectrum[r] = jnp.dot(bins_in[r], forward[r], preferred_element_type=jnp.float32)
    loads[2].wait()

    span = bins_out.shape[1]
    pieces = span // chunk

    def convolve(w, _):
        for c in range(pieces):
            for k in range(1, n):
                there(k, w * pieces + c, True).wait_recv()

        def signal(rows):
            return [
                gathered[a // blocks, rows, lanes(a % blocks)].astype(jnp.float32)
                for a in range(total_blocks)
            ]

        def rows_in(j, _):
            at = pl.ds(pl.multiple_of(j * ROWS, ROWS), ROWS)
            spread(signal(rows_at(w * pieces, j)), at)
            return 0

        lax.fori_loop(0, span // ROWS, rows_in, 0)
        here = pl.ds(pl.multiple_of(w * span, span), span)

        for r in range(bin_count):
            sig = jnp.dot(bins_in[r, 0:span, :], forward[r], preferred_element_type=jnp.float32)
            filt = spectrum[r, here, :]
            sig_re, sig_im = sig[:, :LANES], sig[:, LANES:]
            filt_re, filt_im = filt[:, :LANES], filt[:, LANES:]
            products[r] = jnp.concatenate(
                [sig_re * filt_re - sig_im * filt_im, sig_re * filt_im + sig_im * filt_re], axis=1
            ).astype(jnp.bfloat16)

        for r in range(bin_count):
            bins_out[r] = jnp.dot(products[r], backward[r], preferred_element_type=jnp.float32)

        for c in range(pieces):
            q = w * pieces + c

            def rows_out(j, _):
                at = pl.ds(pl.multiple_of(c * chunk + j * ROWS, ROWS), ROWS)
                rows = rows_at(q, j)
                bins = {
                    r: (bins_out[r, at, :LANES], bins_out[r, at, LANES:]) for r in range(bin_count)
                }
                result = padded_back(bins, total_blocks)
                skip = skip_wide[rows, :]
                for a, value in enumerate(signal(rows)):
                    long_out[a // blocks, rows, lanes(a % blocks)] = (
                        skip * value + result[a]
                    ).astype(jnp.bfloat16)
                return 0

            lax.fori_loop(0, groups, rows_out, 0)
            for k in [*range(2, n), 1]:
                home(k, q).start()
            own(q).start()
        return 0

    lax.fori_loop(0, per // span, convolve, 0)

    def drain(q, _):
        @pl.when(me < n - 1)
        def _():
            rim(0, q).wait_send()
            rim(1, q).wait_send()

        own(q).wait()
        for k in range(1, n):
            there(k, q).wait_send()
            home(k, q).wait_send()
            home(k, q, True).wait_recv()
        return 0

    lax.fori_loop(0, chunks, drain, 0)


def fits_kernel(channels, length, n, tap_count):
    per = channels // n
    total = n * length
    return (
        tap_count == LANES
        and length % LANES == 0
        and length >= 2 * LANES
        and per % LANES == 0
        and n > 1
        and total & (total - 1) == 0
        and total <= 2048
        and channels * total <= 1024 * 2048
    )


def shards(
    value_in,
    key_in,
    gate_first,
    gate_second,
    gate_long,
    filter_first,
    filter_second,
    long_filter,
    skip_gain,
):
    channels, length = value_in.shape
    n = lax.axis_size("ctx")
    if not fits_kernel(channels, length, n, filter_first.shape[1]):
        return shards_general(
            value_in,
            key_in,
            gate_first,
            gate_second,
            gate_long,
            filter_first,
            filter_second,
            long_filter,
            skip_gain,
        )
    per = channels // n
    total = n * length
    chunk = 64
    span = chunk
    chunks = per // chunk
    group_count = filter_first.shape[0]
    bin_count = total // LANES + 1
    cut = lambda a: a.reshape(n, per, length)
    forward, back = inner_tables(total)
    bf16, f32 = jnp.bfloat16, jnp.float32
    vmem = pl.BlockSpec(memory_space=pltpu.VMEM)
    anywhere = pl.BlockSpec(memory_space=pl.ANY)
    in_hbm = pl.BlockSpec(memory_space=pltpu.HBM)
    dma = pltpu.SemaphoreType.DMA
    out = pl.pallas_call(
        functools.partial(whole_kernel, n, chunk),
        out_shape=jax.ShapeDtypeStruct((n, per, length), bf16),
        in_specs=[vmem] * 3 + [in_hbm] * 7,
        out_specs=anywhere,
        scratch_shapes=[
            pltpu.VMEM((n, per, length), bf16),
            pltpu.VMEM((n, per, length), bf16),
            pltpu.VMEM((n, per, length), bf16),
            pltpu.VMEM((n, per, length), bf16),
            pltpu.VMEM((per, total), bf16),
            pltpu.VMEM(forward.shape, bf16),
            pltpu.VMEM(back.shape, bf16),
            pltpu.VMEM(filter_first.shape, f32),
            pltpu.VMEM(filter_second.shape, f32),
            pltpu.VMEM((group_count, 2 * LANES, LANES), bf16),
            pltpu.VMEM((group_count, 2 * LANES, LANES), bf16),
            pltpu.VMEM((n, per, length), bf16),
            pltpu.VMEM((n, per, length), bf16),
            pltpu.VMEM((n, per, LANES), bf16),
            pltpu.VMEM((n, per, LANES), bf16),
            pltpu.VMEM((n, per, length), bf16),
            pltpu.VMEM((n, per, length), bf16),
            pltpu.VMEM((n, per, length), bf16),
            pltpu.VMEM((per, LANES), f32),
            pltpu.VMEM((bin_count, per, 2 * LANES), bf16),
            pltpu.VMEM((bin_count, per, 2 * LANES), f32),
            pltpu.VMEM((bin_count, span, 2 * LANES), bf16),
            pltpu.VMEM((bin_count, span, 2 * LANES), f32),
            dma((3,)),
            dma((4, chunks)),
            dma((chunks,)),
            dma((2, chunks)),
            dma((2, chunks)),
            dma((n, chunks)),
            dma((n, chunks)),
            dma((n, chunks)),
            dma((n, chunks)),
        ],
        compiler_params=pltpu.CompilerParams(
            collective_id=0, has_side_effects=True, vmem_limit_bytes=52 * 1024 * 1024
        ),
        cost_estimate=pl.CostEstimate(
            flops=8 * channels * length * 2 * LANES + 6 * 2 * per * total * 2 * LANES * 2,
            bytes_accessed=8 * channels * length * 2,
            transcendentals=0,
        ),
    )(
        *[
            pltpu.with_memory_space_constraint(a, pltpu.HBM)
            for a in (
                filter_first,
                filter_second,
                skip_gain.reshape(channels // LANES, LANES),
                cut(value_in),
                cut(key_in),
                cut(gate_first),
                cut(gate_second),
                long_filter,
                jnp.asarray(forward),
                jnp.asarray(back),
            )
        ]
    )
    return gated(gate_long, out.reshape(channels, length).astype(f32))


def solution(mesh):
    placed = (
        P("ch", "ctx"),
        P("ch", "ctx"),
        P("ch", "ctx"),
        P("ch", "ctx"),
        P("ch", "ctx"),
        P("ch", None),
        P("ch", None),
        P(("ch", "ctx"), None),
        P("ch"),
    )
    return jax.shard_map(
        shards, mesh=mesh, in_specs=placed, out_specs=P("ch", "ctx"), check_vma=False
    )
```

```python
import cmath
import functools
import math

import jax
import jax.numpy as jnp
import ml_dtypes
import numpy as np
from jax import lax
from jax.experimental import pallas as pl
from jax.experimental.pallas import tpu as pltpu
from jax.sharding import PartitionSpec as P

HIGH = lax.Precision.HIGH
LANES = 128
ROWS = 16
MESH = pl.DeviceIdType.MESH


def from_behind(shard, axis, by):
    devices = lax.axis_size(axis)
    pairs = [(i, i + by) for i in range(devices) if 0 <= i + by < devices]
    return lax.ppermute(shard, axis, pairs)


def band_matrix(filters, tap_count):
    group_count = filters.shape[0]
    zero_one = jnp.zeros((group_count, 1), filters.dtype)
    zero_rest = jnp.zeros((group_count, tap_count), filters.dtype)
    pattern = jnp.concatenate([zero_one, jnp.flip(filters, axis=1), zero_rest], axis=1)
    tiled = jnp.tile(pattern, (1, tap_count))
    return tiled[:, : tap_count * 2 * tap_count].reshape(group_count, tap_count, 2 * tap_count)


def toeplitz_conv(extended, filters, tap_count):
    channels, total_len = extended.shape
    length = total_len - tap_count
    block_count = length // tap_count
    front_half = extended[:, :length].reshape(channels, block_count, tap_count)
    back_half = extended[:, tap_count:].reshape(channels, block_count, tap_count)
    windows = jnp.concatenate([front_half, back_half], axis=2)
    group_count = filters.shape[0]
    windows = windows.reshape(group_count, channels // group_count, block_count, 2 * tap_count)
    toeplitz = band_matrix(filters, tap_count)
    result = jnp.einsum("gts,gcbs->gcbt", toeplitz, windows, preferred_element_type=jnp.float32)
    return result.reshape(channels, length)


def previous_rim(tail):
    return from_behind(tail, "ctx", 1)


def to_channels(data):
    return lax.all_to_all(data, "ctx", split_axis=0, concat_axis=1, tiled=True)


def first_section(mixed_in, gate_first, filter_first, tap_count):
    length = mixed_in.shape[1]
    extended = jnp.concatenate([previous_rim(mixed_in[:, length - tap_count :]), mixed_in], axis=1)
    return (
        gate_first.astype(jnp.float32) * toeplitz_conv(extended, filter_first, tap_count)
    ).astype(jnp.bfloat16)


def dft_tables(size):
    index = jnp.arange(size, dtype=jnp.int32)
    angle = (index[:, None] * index[None, :] % size).astype(jnp.float32) * (-2.0 * math.pi / size)
    return (jnp.cos(angle), jnp.sin(angle))


def split_factor(padded_len):
    outer = 2
    cand = 2
    while cand * cand <= padded_len:
        if padded_len % cand == 0:
            outer = cand
        cand = cand + 2
    return outer


def long_convolution(signal, filt_vals, skip_part):
    channels, length = signal.shape
    padded_len = 2 * length
    rows_outer = split_factor(padded_len)
    rows_inner = padded_len // rows_outer
    half_rows = rows_outer // 2
    outer_cos, outer_sin = dft_tables(rows_outer)
    inner_cos, inner_sin = dft_tables(rows_inner)
    k_index = jnp.arange(rows_outer, dtype=jnp.int32)[:, None]
    n_index = jnp.arange(rows_inner, dtype=jnp.int32)[None, :]
    twid_angle = (k_index * n_index % padded_len).astype(jnp.float32) * (
        -2.0 * math.pi / padded_len
    )
    twid_cos = jnp.cos(twid_angle)
    twid_sin = jnp.sin(twid_angle)
    outer_table = jnp.concatenate([outer_cos[:, :half_rows], outer_sin[:, :half_rows]], axis=0)
    inner_fwd = jnp.concatenate(
        [
            jnp.concatenate([inner_cos, inner_sin], axis=1),
            jnp.concatenate([-inner_sin, inner_cos], axis=1),
        ],
        axis=0,
    )
    inner_back = jnp.concatenate(
        [
            jnp.concatenate([inner_cos, -inner_sin], axis=1),
            jnp.concatenate([inner_sin, inner_cos], axis=1),
        ],
        axis=0,
    )

    def forward(values):
        grid = values.reshape(channels, half_rows, rows_inner)
        parts = jnp.einsum("kn,cnm->ckm", outer_table, grid, precision=HIGH)
        part_re = parts[:, :rows_outer]
        part_im = parts[:, rows_outer:]
        turned_re = part_re * twid_cos - part_im * twid_sin
        turned_im = part_re * twid_sin + part_im * twid_cos
        turned = jnp.concatenate([turned_re, turned_im], axis=2)
        spectrum = jnp.einsum("ckn,nm->ckm", turned, inner_fwd, precision=HIGH)
        return (spectrum[:, :, :rows_inner], spectrum[:, :, rows_inner:])

    sig_re, sig_im = forward(signal)
    filt_re, filt_im = forward(filt_vals)
    prod_re = sig_re * filt_re - sig_im * filt_im
    prod_im = sig_re * filt_im + sig_im * filt_re
    stacked = jnp.concatenate([prod_re, prod_im], axis=2)
    back = jnp.einsum("ckm,mn->ckn", stacked, inner_back, precision=HIGH)
    back_re = back[:, :, :rows_inner]
    back_im = back[:, :, rows_inner:]
    reverted_re = back_re * twid_cos + back_im * twid_sin
    reverted_im = back_im * twid_cos - back_re * twid_sin
    reverted = jnp.concatenate([reverted_re, reverted_im], axis=1)
    result = jnp.einsum("kn,ckm->cnm", outer_table, reverted, precision=HIGH)
    result = result.reshape(channels, length) / padded_len
    return skip_part[:, None] * signal + result


def shards_general(
    value_in,
    key_in,
    gate_first,
    gate_second,
    gate_long,
    filter_first,
    filter_second,
    long_filter,
    skip_gain,
):
    tap_count = filter_first.shape[1]
    channels, length = value_in.shape
    per_device = channels // lax.axis_size("ctx")
    channel_base = lax.axis_index("ctx") * per_device
    mixed_in = (key_in.astype(jnp.float32) * value_in.astype(jnp.float32)).astype(jnp.bfloat16)
    first_out = first_section(mixed_in, gate_first, filter_first, tap_count)
    prior_first = from_behind(first_out[:, length - tap_count :], "ctx", 1)
    first_wide = jnp.concatenate([prior_first, first_out], axis=1)
    second_out = (
        gate_second.astype(jnp.float32) * toeplitz_conv(first_wide, filter_second, tap_count)
    ).astype(jnp.bfloat16)
    moved = to_channels(second_out)
    skip_here = lax.dynamic_slice_in_dim(skip_gain, channel_base, per_device, 0)
    filt_vals = long_filter.astype(jnp.float32)
    long_out = long_convolution(moved.astype(jnp.float32), filt_vals, skip_here).astype(
        jnp.bfloat16
    )
    back_home = lax.all_to_all(long_out, "ctx", split_axis=1, concat_axis=0, tiled=True)
    return (gate_long.astype(jnp.float32) * back_home.astype(jnp.float32)).astype(jnp.bfloat16)


def unit(numerator, denominator):
    return cmath.exp(-2j * math.pi * numerator / denominator)


def turn(value, factor):
    re, im = value
    if abs(factor - 1) < 1e-12:
        return value
    if abs(factor + 1j) < 1e-12:
        return (im, -re)
    if abs(factor - 1j) < 1e-12:
        return (-im, re)
    if abs(abs(factor.real) - abs(factor.imag)) < 1e-12:
        size = abs(factor.real)
        re, im = re * size, im * size
        if factor.real > 0 and factor.imag < 0:
            return (re + im, im - re)
        if factor.real < 0 and factor.imag < 0:
            return (im - re, -re - im)
        if factor.real > 0:
            return (re - im, re + im)
        return (-re - im, re - im)
    return (re * factor.real - im * factor.imag, re * factor.imag + im * factor.real)


def complex_dft(values, sign):
    count = len(values)
    if count == 1:
        return values
    half = count // 2
    low, high = [], []
    for a in range(half):
        (p_re, p_im), (q_re, q_im) = values[a], values[a + half]
        low.append((p_re + q_re, p_im + q_im))
        factor = unit(a, count)
        high.append(turn((p_re - q_re, p_im - q_im), factor if sign > 0 else factor.conjugate()))
    result = [None] * count
    result[0::2] = complex_dft(low, sign)
    result[1::2] = complex_dft(high, sign)
    return result


def odd_bins(values):
    count = len(values)
    if count == 1:
        return {1: (values[0], None)}
    half = count // 2
    folded = [turn((values[a], -values[a + half]), unit(a, 2 * count)) for a in range(half)]
    bins = {}
    for place, (re, im) in enumerate(complex_dft(folded, 1)):
        r = 4 * place + 1
        if r < count:
            bins[r] = (re, im)
        else:
            bins[2 * count - r] = (re, -im)
    return bins


def real_bins(values):
    count = len(values)
    if count == 1:
        return {0: (values[0], None)}
    half = count // 2
    even = real_bins([values[a] + values[a + half] for a in range(half)])
    odd = odd_bins([values[a] - values[a + half] for a in range(half)])
    bins = {2 * r: v for r, v in even.items()}
    bins.update(odd)
    return bins


def padded_bins(values):
    bins = {2 * r: v for r, v in real_bins(values).items()}
    bins.update(odd_bins(values))
    return bins


def odd_back(bins, count):
    if count == 1:
        return [bins[1][0]]
    half = count // 2
    folded = []
    for place in range(half):
        r = 4 * place + 1
        if r < count:
            folded.append(bins[r])
        else:
            re, im = bins[2 * count - r]
            folded.append((re, -im))
    spread = complex_dft(folded, -1)
    spread = [turn(spread[a], unit(a, 2 * count).conjugate()) for a in range(half)]
    return [v[0] for v in spread] + [-v[1] for v in spread]


def real_back(bins, count):
    if count == 1:
        return [bins[0][0]]
    half = count // 2
    even = real_back({r // 2: v for r, v in bins.items() if r % 2 == 0}, half)
    odd = odd_back({r: v for r, v in bins.items() if r % 2 == 1}, half)
    return [even[a] + odd[a] for a in range(half)] + [even[a] - odd[a] for a in range(half)]


def padded_back(bins, count):
    even = real_back({r // 2: v for r, v in bins.items() if r % 2 == 0}, count)
    odd = odd_back({r: v for r, v in bins.items() if r % 2 == 1}, count)
    return [even[a] + odd[a] for a in range(count)]


def inner_tables(length):
    padded_len = 2 * length
    outer = padded_len // LANES
    b = np.arange(LANES)[:, None]
    q = np.arange(LANES)[None, :]
    forward, back = [], []
    for r in range(outer // 2 + 1):
        angle = (b * (r + outer * q) % padded_len) * (-2.0 * math.pi / padded_len)
        c, s = np.cos(angle), np.sin(angle)
        table = np.block([[c, s], [-s, c]])
        weight = (1.0 if r in (0, outer // 2) else 2.0) / padded_len
        forward.append(table)
        back.append(table.T * weight)
    return (
        np.stack(forward).astype(ml_dtypes.bfloat16),
        np.stack(back).astype(ml_dtypes.bfloat16),
    )


def band(row):
    rolled = pltpu.roll(jnp.broadcast_to(row, (LANES, LANES)), 0, 1, stride=1, stride_axis=0)
    s = lax.broadcasted_iota(jnp.int32, (LANES, LANES), 0)
    t = lax.broadcasted_iota(jnp.int32, (LANES, LANES), 1)
    zero = jnp.zeros((LANES, LANES), jnp.float32)
    return jnp.concatenate(
        [jnp.where(t < s, rolled, zero), jnp.where(t >= s, rolled, zero)], axis=0
    ).astype(jnp.bfloat16)


def gated(gate, value):
    return (gate.astype(jnp.float32) * value).astype(jnp.bfloat16)


def whole_kernel(
    n,
    chunk,
    filter_first_ref,
    filter_second_ref,
    skip_ref,
    value_hbm,
    key_hbm,
    gate_first_hbm,
    gate_second_hbm,
    long_filter_hbm,
    forward_hbm,
    back_hbm,
    returned,
    value_ref,
    key_ref,
    gate_first_ref,
    gate_second,
    long_filter,
    forward,
    backward,
    taps_first,
    taps_second,
    band_first,
    band_second,
    mixed,
    first,
    halo_mixed,
    halo_first,
    second,
    gathered,
    long_out,
    skip_wide,
    bins_in,
    spectrum,
    products,
    bins_out,
    load_sem,
    part_sem,
    own_sem,
    rim_send,
    rim_recv,
    there_send,
    there_recv,
    home_send,
    home_recv,
):
    _, per, length = value_hbm.shape
    me = lax.axis_index("ctx")
    blocks = length // LANES
    chunks = per // chunk
    groups = chunk // ROWS
    total_blocks = n * blocks
    bin_count = total_blocks + 1
    last = slice(length - LANES, length)

    barrier = pltpu.get_barrier_semaphore()
    for k in range(1, n):
        pl.semaphore_signal(
            barrier, inc=1, device_id={"ctx": lax.rem(me + k, n)}, device_id_type=MESH
        )

    def part(q):
        return pl.ds(pl.multiple_of(q * chunk, chunk), chunk)

    def loaded(i, q):
        src, dst = (
            (key_hbm, key_ref),
            (value_hbm, value_ref),
            (gate_first_hbm, gate_first_ref),
            (gate_second_hbm, gate_second),
        )[i]
        return pltpu.make_async_copy(
            src.at[:, part(q), :], dst.at[:, part(q), :], part_sem.at[i, q]
        )

    for q in range(chunks):
        for i in range(4):
            loaded(i, q).start()
    loads = [
        pltpu.make_async_copy(src, dst, load_sem.at[i])
        for i, (src, dst) in enumerate(
            [(long_filter_hbm, long_filter), (forward_hbm, forward), (back_hbm, backward)]
        )
    ]
    for load in loads:
        load.start()

    def own(q):
        return pltpu.make_async_copy(
            long_out.at[me, part(q), :], returned.at[me, part(q), :], own_sem.at[q]
        )

    def rim(which, q):
        src, dst = ((mixed, halo_mixed), (first, halo_first))[which]
        return pltpu.make_async_remote_copy(
            src_ref=src.at[:, part(q), last],
            dst_ref=dst.at[:, part(q), :],
            send_sem=rim_send.at[which, q],
            recv_sem=rim_recv.at[which, q],
            device_id={"ctx": lax.rem(me + 1, n)},
            device_id_type=MESH,
        )

    def there(k, q, arriving=False):
        peer = lax.rem(me + (n - k if arriving else k), n)
        slot = peer if arriving else me
        return pltpu.make_async_remote_copy(
            src_ref=second.at[peer, part(q), :],
            dst_ref=gathered.at[slot, part(q), :],
            send_sem=there_send.at[k, q],
            recv_sem=there_recv.at[k, q],
            device_id={"ctx": peer},
            device_id_type=MESH,
        )

    def home(k, q, arriving=False):
        peer = lax.rem(me + (n - k if arriving else k), n)
        slot = peer if arriving else me
        return pltpu.make_async_remote_copy(
            src_ref=long_out.at[peer, part(q), :],
            dst_ref=returned.at[slot, part(q), :],
            send_sem=home_send.at[k, q],
            recv_sem=home_recv.at[k, q],
            device_id={"ctx": peer},
            device_id_type=MESH,
        )

    def rows_at(q, j):
        return pl.ds(pl.multiple_of(q * chunk + j * ROWS, ROWS), ROWS)

    def lanes(b):
        return slice(b * LANES, (b + 1) * LANES)

    taps_first[...] = filter_first_ref[...].astype(jnp.float32)
    taps_second[...] = filter_second_ref[...].astype(jnp.float32)
    eye = lax.broadcasted_iota(jnp.int32, (LANES, LANES), 0) == lax.broadcasted_iota(
        jnp.int32, (LANES, LANES), 1
    )
    for i in range(per // LANES):
        line = skip_ref[pl.ds(me * (per // LANES) + i, 1), :]
        column = jnp.sum(jnp.where(eye, line, 0.0), axis=1, keepdims=True)
        skip_wide[i * LANES : (i + 1) * LANES, :] = jnp.broadcast_to(column, (LANES, LANES))

    pl.semaphore_wait(barrier, n - 1)

    @pl.when(me == 0)
    def _():
        halo_mixed[...] = jnp.zeros_like(halo_mixed)
        halo_first[...] = jnp.zeros_like(halo_first)

    def early(q):
        loaded(0, q).wait()
        loaded(1, q).wait()

        for d in range(n):
            mixed[d, part(q), :] = (
                key_ref[d, part(q), :].astype(jnp.float32)
                * value_ref[d, part(q), :].astype(jnp.float32)
            ).astype(jnp.bfloat16)

        @pl.when(me < n - 1)
        def _():
            rim(0, q).start()

        loaded(2, q).wait()

        for d in range(n):
            for j in range(groups):
                g = d * (per // ROWS) + q * groups + j
                w = band(taps_first[pl.ds(g, 1), :])
                band_first[g] = w
                band_second[g] = band(taps_second[pl.ds(g, 1), :])
                rows = rows_at(q, j)
                windows = jnp.concatenate(
                    [mixed[d, rows, b * LANES - LANES : (b + 1) * LANES] for b in range(1, blocks)],
                    axis=0,
                )
                result = jnp.dot(windows, w, preferred_element_type=jnp.float32)
                for b in range(1, blocks):
                    first[d, rows, lanes(b)] = gated(
                        gate_first_ref[d, rows, lanes(b)], result[(b - 1) * ROWS : b * ROWS]
                    )

        @pl.when(me < n - 1)
        def _():
            rim(1, q).start()

    def late(q):
        loaded(3, q).wait()

        @pl.when(me > 0)
        def _():
            rim(0, q).wait_recv()
            rim(1, q).wait_recv()

        for d in range(n):
            for j in range(groups):
                g = d * (per // ROWS) + q * groups + j
                rows = rows_at(q, j)
                head = jnp.concatenate([halo_mixed[d, rows, :], mixed[d, rows, lanes(0)]], axis=1)
                head = jnp.dot(head, band_first[g], preferred_element_type=jnp.float32)
                first[d, rows, lanes(0)] = gated(gate_first_ref[d, rows, lanes(0)], head)

        for k in [*range(2, n), 1, 0]:
            d = lax.rem(me + k, n)
            target = second if k else gathered
            for j in range(groups):
                g = d * (per // ROWS) + q * groups + j
                rows = rows_at(q, j)
                ahead = jnp.concatenate([halo_first[d, rows, :], first[d, rows, lanes(0)]], axis=1)
                windows = [ahead] + [
                    first[d, rows, b * LANES - LANES : (b + 1) * LANES] for b in range(1, blocks)
                ]
                result = jnp.dot(
                    jnp.concatenate(windows, axis=0),
                    band_second[g],
                    preferred_element_type=jnp.float32,
                )
                for b in range(blocks):
                    target[d, rows, lanes(b)] = gated(
                        gate_second[d, rows, lanes(b)], result[b * ROWS : (b + 1) * ROWS]
                    )
            if k:
                there(k, q).start()

    def start(q, _):
        early(q)
        return 0

    def follow(q, _):
        late(q)
        return 0

    lax.fori_loop(0, chunks, start, 0)
    lax.fori_loop(0, chunks, follow, 0)

    def spread(values, at):
        bins = padded_bins(values)
        for r in range(bin_count):
            re, im = bins[r]
            im = jnp.zeros_like(re) if im is None else im
            bins_in[r, at, :] = jnp.concatenate([re, im], axis=1).astype(jnp.bfloat16)

    loads[0].wait()
    loads[1].wait()

    def filter_rows(j, _):
        at = pl.ds(pl.multiple_of(j * ROWS, ROWS), ROWS)
        spread([long_filter[at, lanes(a)].astype(jnp.float32) for a in range(total_blocks)], at)
        return 0

    lax.fori_loop(0, per // ROWS, filter_rows, 0)

    for r in range(bin_count):
        spectrum[r] = jnp.dot(bins_in[r], forward[r], preferred_element_type=jnp.float32)
    loads[2].wait()

    span = bins_out.shape[1]
    pieces = span // chunk

    def convolve(w, _):
        for c in range(pieces):
            for k in range(1, n):
                there(k, w * pieces + c, True).wait_recv()

        def signal(rows):
            return [
                gathered[a // blocks, rows, lanes(a % blocks)].astype(jnp.float32)
                for a in range(total_blocks)
            ]

        def rows_in(j, _):
            at = pl.ds(pl.multiple_of(j * ROWS, ROWS), ROWS)
            spread(signal(rows_at(w * pieces, j)), at)
            return 0

        lax.fori_loop(0, span // ROWS, rows_in, 0)
        here = pl.ds(pl.multiple_of(w * span, span), span)

        for r in range(bin_count):
            sig = jnp.dot(bins_in[r, 0:span, :], forward[r], preferred_element_type=jnp.float32)
            filt = spectrum[r, here, :]
            sig_re, sig_im = sig[:, :LANES], sig[:, LANES:]
            filt_re, filt_im = filt[:, :LANES], filt[:, LANES:]
            products[r] = jnp.concatenate(
                [sig_re * filt_re - sig_im * filt_im, sig_re * filt_im + sig_im * filt_re], axis=1
            ).astype(jnp.bfloat16)

        for r in range(bin_count):
            bins_out[r] = jnp.dot(products[r], backward[r], preferred_element_type=jnp.float32)

        for c in range(pieces):
            q = w * pieces + c

            def rows_out(j, _):
                at = pl.ds(pl.multiple_of(c * chunk + j * ROWS, ROWS), ROWS)
                rows = rows_at(q, j)
                bins = {
                    r: (bins_out[r, at, :LANES], bins_out[r, at, LANES:]) for r in range(bin_count)
                }
                result = padded_back(bins, total_blocks)
                skip = skip_wide[rows, :]
                for a, value in enumerate(signal(rows)):
                    long_out[a // blocks, rows, lanes(a % blocks)] = (
                        skip * value + result[a]
                    ).astype(jnp.bfloat16)
                return 0

            lax.fori_loop(0, groups, rows_out, 0)
            for k in [*range(2, n), 1]:
                home(k, q).start()
            own(q).start()
        return 0

    lax.fori_loop(0, per // span, convolve, 0)

    def drain(q, _):
        @pl.when(me < n - 1)
        def _():
            rim(0, q).wait_send()
            rim(1, q).wait_send()

        own(q).wait()
        for k in range(1, n):
            there(k, q).wait_send()
            home(k, q).wait_send()
            home(k, q, True).wait_recv()
        return 0

    lax.fori_loop(0, chunks, drain, 0)


def fits_kernel(channels, length, n, tap_count):
    per = channels // n
    total = n * length
    return (
        tap_count == LANES
        and length % LANES == 0
        and length >= 2 * LANES
        and per % LANES == 0
        and n > 1
        and total & (total - 1) == 0
        and total <= 2048
        and channels * total <= 1024 * 2048
    )


def shards(
    value_in,
    key_in,
    gate_first,
    gate_second,
    gate_long,
    filter_first,
    filter_second,
    long_filter,
    skip_gain,
):
    channels, length = value_in.shape
    n = lax.axis_size("ctx")
    if not fits_kernel(channels, length, n, filter_first.shape[1]):
        return shards_general(
            value_in,
            key_in,
            gate_first,
            gate_second,
            gate_long,
            filter_first,
            filter_second,
            long_filter,
            skip_gain,
        )
    per = channels // n
    total = n * length
    chunk = 32
    span = 2 * chunk
    chunks = per // chunk
    group_count = filter_first.shape[0]
    bin_count = total // LANES + 1
    cut = lambda a: a.reshape(n, per, length)
    forward, back = inner_tables(total)
    bf16, f32 = jnp.bfloat16, jnp.float32
    vmem = pl.BlockSpec(memory_space=pltpu.VMEM)
    anywhere = pl.BlockSpec(memory_space=pl.ANY)
    in_hbm = pl.BlockSpec(memory_space=pltpu.HBM)
    dma = pltpu.SemaphoreType.DMA
    out = pl.pallas_call(
        functools.partial(whole_kernel, n, chunk),
        out_shape=jax.ShapeDtypeStruct((n, per, length), bf16),
        in_specs=[vmem] * 3 + [in_hbm] * 7,
        out_specs=anywhere,
        scratch_shapes=[
            pltpu.VMEM((n, per, length), bf16),
            pltpu.VMEM((n, per, length), bf16),
            pltpu.VMEM((n, per, length), bf16),
            pltpu.VMEM((n, per, length), bf16),
            pltpu.VMEM((per, total), bf16),
            pltpu.VMEM(forward.shape, bf16),
            pltpu.VMEM(back.shape, bf16),
            pltpu.VMEM(filter_first.shape, f32),
            pltpu.VMEM(filter_second.shape, f32),
            pltpu.VMEM((group_count, 2 * LANES, LANES), bf16),
            pltpu.VMEM((group_count, 2 * LANES, LANES), bf16),
            pltpu.VMEM((n, per, length), bf16),
            pltpu.VMEM((n, per, length), bf16),
            pltpu.VMEM((n, per, LANES), bf16),
            pltpu.VMEM((n, per, LANES), bf16),
            pltpu.VMEM((n, per, length), bf16),
            pltpu.VMEM((n, per, length), bf16),
            pltpu.VMEM((n, per, length), bf16),
            pltpu.VMEM((per, LANES), f32),
            pltpu.VMEM((bin_count, per, 2 * LANES), bf16),
            pltpu.VMEM((bin_count, per, 2 * LANES), f32),
            pltpu.VMEM((bin_count, span, 2 * LANES), bf16),
            pltpu.VMEM((bin_count, span, 2 * LANES), f32),
            dma((3,)),
            dma((4, chunks)),
            dma((chunks,)),
            dma((2, chunks)),
            dma((2, chunks)),
            dma((n, chunks)),
            dma((n, chunks)),
            dma((n, chunks)),
            dma((n, chunks)),
        ],
        compiler_params=pltpu.CompilerParams(
            collective_id=0, has_side_effects=True, vmem_limit_bytes=52 * 1024 * 1024
        ),
        cost_estimate=pl.CostEstimate(
            flops=8 * channels * length * 2 * LANES + 6 * 2 * per * total * 2 * LANES * 2,
            bytes_accessed=8 * channels * length * 2,
            transcendentals=0,
        ),
    )(
        *[
            pltpu.with_memory_space_constraint(a, pltpu.HBM)
            for a in (
                filter_first,
                filter_second,
                skip_gain.reshape(channels // LANES, LANES),
                cut(value_in),
                cut(key_in),
                cut(gate_first),
                cut(gate_second),
                long_filter,
                jnp.asarray(forward),
                jnp.asarray(back),
            )
        ]
    )
    return gated(gate_long, out.reshape(channels, length).astype(f32))


def solution(mesh):
    placed = (
        P("ch", "ctx"),
        P("ch", "ctx"),
        P("ch", "ctx"),
        P("ch", "ctx"),
        P("ch", "ctx"),
        P("ch", None),
        P("ch", None),
        P(("ch", "ctx"), None),
        P("ch"),
    )
    return jax.shard_map(
        shards, mesh=mesh, in_specs=placed, out_specs=P("ch", "ctx"), check_vma=False
    )
```
